32 devices in a mesh: groups: 2 (over x), row: 4 (over y, core), col: 4 (over z).
Axes of the slice: x: 2, y: 2, z: 4, core: 2. Of those that a mesh axis runs over, the one named last changes fastest.
Arguments:
- state_blocks: bfloat16 [128, 64, 1024], P(('groups', 'row')), parts along dimension 0, may hold values from -6 to 6
- left_env: bfloat16 [64, 64, 1536], P(('groups', 'row'), None, 'col'), parts along dimension 0, may hold values from -0.75 to 0.75
- right_env: bfloat16 [64, 64, 1536], P(('groups', 'row')), parts along dimension 0, may hold values from -0.15625 to 0.15625
- mpo_tensor: bfloat16 [24, 24, 256], replicated, may hold values from -0.3125 to 0.3125
- block_left: int32 [128], P(('groups', 'row')), parts along dimension 0, may hold values from 0 to 7
- block_owner: int32 [128, 1], P(('groups', 'row')), parts along dimension 0, may hold values from 0 to 3; in each aligned block of 16 rows (0 to 15, 16 to 31, ...) at most 8 rows name the same one
- block_sub: int32 [128], P(('groups', 'row')), parts along dimension 0, may hold values from 0 to 7
Outputs:
- applied_blocks: bfloat16 [128, 64, 1024], P(('groups', 'row'), None, 'col'), parts along dimension 0
The draws below stay inside these ranges and needn't reach their ends.
There are 2 independent parts, one for each index of `groups`. The reference program is written for one: setup_inputs(seed, part) draws one part's arguments, and reference() takes and returns one part's arrays. A program takes and returns all parts, laid end to end along the dimension named above; an argument that names none is the same for every part. Nothing has to cross between parts.
Inputs may be any that keep to these rules, and one draw needn't show every extreme that they name: `block_owner`: among the 16 blocks of one row index, no owner is named by more than 8 blocks, a bound that some block reaches.
All inputs are finite; a program needn't handle non-finite values.
Results may differ from the reference program's by a relative error of at most 0.0057.
Values may be sent and summed in bfloat16 or wider, within the bound.
No kernel may reach another device: no remote copies, remote signals or barrier semaphores. Data moves between devices by JAX's collectives and lax.ppermute only.
A program may use at most 256 MiB of HBM per device.

```python
import math
import jax
import jax.numpy as jnp
import numpy as np
from jax import lax

B = 64
S = 16
W = 24
KD = 8
NBD = 16
CAP = 8
SECTORS = 32
BLOCKS = 64
N_ROW = 4


def with_ends(drawn, stream_key, low, largest):
    spot = [jax.random.randint(jax.random.fold_in(stream_key, axis), (), 0, length) for axis, length in enumerate(drawn.shape)]
    widest = drawn.shape.index(max(drawn.shape))
    next_to = spot[:widest] + [(spot[widest] + 1) % drawn.shape[widest]] + spot[widest + 1:]
    return drawn.at[tuple(spot)].set(low).at[tuple(next_to)].set(largest)


def steps_of(stream_key, extent, cuts, smallest, high):
    factor_of = 1.0
    for dim, shards_of in cuts:
        draws = jax.random.uniform(jax.random.fold_in(jax.random.fold_in(stream_key, 6), dim), (shards_of,), jnp.float32, smallest / len(cuts), high / len(cuts))
        factor_of = factor_of * jnp.repeat(jnp.exp(draws), extent[dim] // shards_of).reshape((-1,) + (1,) * (len(extent) - 1 - dim))
    return factor_of


def routed_block(rng, own, number, rows, count, top, most, slope):
    order = jax.random.permutation(rng, count)
    crowded, usual = load_shares(count, rows * top, most, slope, True), load_shares(count, rows * top, most, slope, False)
    places = jnp.arange(count)

    def named(lengths, rotation):
        used = int((lengths > 0).sum())
        fixed = max(1, used // 4)
        shifted = fixed + (places - fixed + rotation * (used - fixed)) % max(1, count - fixed)
        return jnp.zeros((count,), jnp.int32).at[order[jnp.where(places < fixed, places, shifted)]].set(jnp.asarray(lengths, jnp.int32))

    lengths = jnp.where(number % 4 == 0, named(crowded, number // 4), named(usual, number - number // 4 - 1))
    mixed = jax.random.permutation(jax.random.fold_in(own, 3), count)
    source_of, receiver = mixed[0:count // 2 * 2:2], mixed[1:count // 2 * 2:2]
    slack = jnp.minimum(lengths[source_of] - 1, most - lengths[receiver]) // 2
    slack = jnp.where((source_of == order[0]) | (receiver == order[0]) | (lengths[receiver] == 0), 0, jnp.maximum(slack, 0))
    shifted = jax.random.randint(jax.random.fold_in(own, 4), (count // 2,), 0, 1 << 20) % (slack + 1)
    lengths = lengths.at[source_of].add(-shifted).at[receiver].add(shifted)
    items = jnp.searchsorted(jnp.cumsum(lengths), jnp.arange(rows * top), side="right").astype(jnp.int32)
    table = items.reshape(top, rows).T
    table = table[jax.random.permutation(jax.random.fold_in(own, 1), rows)]
    rotation = jax.random.randint(jax.random.fold_in(own, 2), (rows, 1), 0, top)
    return jnp.take_along_axis(table, (jnp.arange(top)[None, :] + rotation) % top, axis=1)


def load_shares(number_of, total, bound, slope, full):
    portions = [(1 << 20) // math.isqrt(standing ** slope) + 1 for standing in range(1, number_of + 1)]
    largest = bound if full else min(bound, max(-(-total // number_of), total * portions[0] // sum(portions)))
    least = 1 if total - largest >= number_of - 1 else 0
    given, spare = [largest] + [least] * (number_of - 1), total - largest - least * (number_of - 1)
    while spare > 0:
        free = [i for i in range(1, number_of) if given[i] < largest] or [i for i in range(1, number_of) if given[i] < bound]
        whole, remaining = sum([portions[i] for i in free]), spare
        for i in free:
            addition = min(bound - given[i], max(1, remaining * portions[i] // whole), spare)
            given[i] = given[i] + addition
            spare = spare - addition
    return np.array(given)


def scatter_about(stream_key, extent, scale, reach, cuts=(), kind=jnp.bfloat16):
    values = jax.random.normal(stream_key, extent, jnp.float32) * scale
    if len(cuts) > 0:
        values = steps_of(stream_key, extent, cuts, -0.22, 0.18) * values
    return jnp.clip(values, min=-reach, max=reach).astype(kind)


def setup_inputs(seed: int = 0, part: int = 0) -> dict:
    streams_of = jax.random.split(jax.random.key(seed), 8)
    part_keys = jax.random.split(jax.random.fold_in(streams_of[7], part), 8)
    state_blocks = scatter_about(part_keys[0], (BLOCKS, B, S * B), 1.0, 6.0, ((0, 4),))
    left_env = scatter_about(part_keys[1], (SECTORS, B, W * B), B ** -0.5, 0.75, ((0, 4), (2, 4)))
    right_env = scatter_about(part_keys[2], (SECTORS, B, W * B), (W * B) ** -0.5, 0.15625, ((0, 4),))
    mpo_tensor = scatter_about(streams_of[3], (W, W, S * S), (W * S) ** -0.5, 0.3125)
    block_left = with_ends(jax.random.randint(part_keys[4], (BLOCKS,), 0, KD), jax.random.fold_in(part_keys[4], 1), 0, KD - 1).astype(jnp.int32)
    block_owner_keys = jax.random.split(jax.random.fold_in(part_keys[5], 1), BLOCKS // NBD)
    block_owner_turns = jax.random.permutation(jax.random.fold_in(part_keys[5], 3), BLOCKS // NBD)
    block_owner = jax.vmap(lambda own, number: routed_block(jax.random.fold_in(part_keys[5], 2), own, number, NBD, N_ROW, 1, CAP, 2))(block_owner_keys, block_owner_turns).reshape((BLOCKS, 1))
    block_sub = with_ends(jax.random.randint(part_keys[6], (BLOCKS,), 0, KD), jax.random.fold_in(part_keys[6], 1), 0, KD - 1).astype(jnp.int32)
    return dict(state_blocks=state_blocks, left_env=left_env, right_env=right_env, mpo_tensor=mpo_tensor, block_left=block_left, block_owner=block_owner, block_sub=block_sub)


def reference(state_blocks, left_env, right_env, mpo_tensor, block_left, block_owner, block_sub):
    mpo_table = mpo_tensor.astype(jnp.float32).reshape(W, W, S, S)

    def single(index):
        source = index // NBD
        left_sector = (source * KD + block_left[index]).astype(jnp.int32)
        right_sector = (block_owner[index, 0] * KD + block_sub[index]).astype(jnp.int32)
        left_mat = lax.dynamic_index_in_dim(left_env, left_sector, 0, keepdims=False).astype(jnp.float32).reshape(B, W, B)
        right_mat = lax.dynamic_index_in_dim(right_env, right_sector, 0, keepdims=False).astype(jnp.float32).reshape(B, W, B)
        block = lax.dynamic_index_in_dim(state_blocks, index, 0, keepdims=False).astype(jnp.float32)
        first = jnp.einsum('xwa,ac->wxc', left_mat, block).astype(jnp.bfloat16)
        first = lax.optimization_barrier(first)
        first = first.astype(jnp.float32).reshape(W, B, S, B)
        channels = jnp.einsum('wvts,wxsb->vxtb', mpo_table, first).astype(jnp.bfloat16)
        channels = lax.optimization_barrier(channels)
        result = jnp.einsum('vxtb,bvy->xty', channels.astype(jnp.float32), right_mat)
        return result.astype(jnp.bfloat16).reshape(B, S * B)

    return lax.map(single, jnp.arange(NBD * N_ROW, dtype=jnp.int32))
```

```python
import functools

import jax
import jax.numpy as jnp
from jax import lax
from jax.experimental import pallas as pl
from jax.experimental.pallas import tpu as pltpu
from jax.sharding import PartitionSpec as P


def route_kernel(cols, rows, near, left_ref, owner_ref, sub_ref, env_ref, send_ref, order_ref, want_ref, slot_ref, sem):
    count = left_ref.shape[0]
    for owner in range(rows):
        for slot in range(near):
            want_ref[owner, slot] = 0
    owners = [owner_ref[p] for p in range(count)]
    copies = []
    mine = lax.axis_index("col")
    for p in range(count):
        rank = jnp.int32(0)
        first = jnp.int32(0)
        for other in range(count):
            less = (owners[other] < owners[p]).astype(jnp.int32)
            first = first + less
            if other < p:
                rank = rank + (owners[other] == owners[p]).astype(jnp.int32)
        place = first + rank
        col = lax.rem(place, cols)
        step = lax.div(place, cols)
        order_ref[place] = p
        start_col = lax.rem(first, cols)
        offset = lax.rem(col - start_col + cols, cols)
        slot = lax.div(rank - offset, cols)
        slot_ref[place] = owners[p] * near + slot

        @pl.when(col == mine)
        def _():
            want_ref[owners[p], slot] = sub_ref[p]

        copy = pltpu.make_async_copy(env_ref.at[left_ref[p]], send_ref.at[col, step], sem.at[p])
        copy.start()
        copies.append(copy)
    for copy in copies:
        copy.wait()


def route(block_left, owners, block_sub, left_env, rows, cols, near):
    count = block_left.shape[0]
    size, width = left_env.shape[1:]
    smem = pl.BlockSpec(memory_space=pltpu.SMEM)
    hbm = pl.BlockSpec(memory_space=pl.ANY)
    return pl.pallas_call(
        functools.partial(route_kernel, cols, rows, near),
        out_shape=(
            jax.ShapeDtypeStruct((cols, count // cols, size, width), left_env.dtype),
            jax.ShapeDtypeStruct((count,), jnp.int32),
            jax.ShapeDtypeStruct((rows, near), jnp.int32),
            jax.ShapeDtypeStruct((count,), jnp.int32),
        ),
        in_specs=[smem, smem, smem, hbm],
        out_specs=(hbm, smem, smem, smem),
        scratch_shapes=[pltpu.SemaphoreType.DMA((count,))],
        name="route",
    )(block_left, owners, block_sub, left_env)


def pick_kernel(want_ref, env_ref, send_ref, sem):
    rows, near = want_ref.shape
    copies = []
    for row in range(rows):
        for slot in range(near):
            copy = pltpu.make_async_copy(
                env_ref.at[want_ref[row, slot]], send_ref.at[row, slot], sem.at[row * near + slot]
            )
            copy.start()
            copies.append(copy)
    for copy in copies:
        copy.wait()


def pick(wanted, right_env):
    rows, near = wanted.shape
    return pl.pallas_call(
        pick_kernel,
        out_shape=jax.ShapeDtypeStruct((rows, near) + right_env.shape[1:], right_env.dtype),
        in_specs=[pl.BlockSpec(memory_space=pltpu.SMEM), pl.BlockSpec(memory_space=pl.ANY)],
        out_specs=pl.BlockSpec(memory_space=pl.ANY),
        scratch_shapes=[pltpu.SemaphoreType.DMA((rows * near,))],
        name="pick",
    )(wanted, right_env)


def halves(tile, low):
    swapped = pltpu.roll(tile, tile.shape[1] // 2, 1)
    zero = jnp.zeros_like(tile)
    return (
        jnp.where(low, tile, zero),
        jnp.where(low, zero, swapped),
        jnp.where(low, swapped, zero),
        jnp.where(low, zero, tile),
    )


def apply_kernel(
    states, chunk, order_ref, slot_ref, block_ref, left_ref, right_ref, mpo_ref, out_ref,
    left_rows, state_diag, right_diag, mixed, result,
):
    size = block_ref.shape[1]
    half = size // 2
    lanes = 2 * size
    width = mpo_ref.shape[0] // states
    cols = left_ref.shape[0]
    share = width // cols
    low = lax.broadcasted_iota(jnp.int32, (size, lanes), 1) < size

    for v in range(0, width, 2):
        tile = right_ref[0, 0, :, v * size : (v + 2) * size].astype(jnp.float32)
        parts = halves(tile, low)
        for i in range(4):
            at = v * lanes + i * size
            right_diag[at : at + size, :] = parts[i].astype(jnp.bfloat16)
    for s in range(0, states, 2):
        tile = block_ref[0, :, s * size : (s + 2) * size].astype(jnp.float32)
        parts = halves(tile, low)
        for i in range(4):
            row, col = (i % 2) * size, (s + i // 2) * lanes
            state_diag[row : row + size, col : col + lanes] = parts[i].astype(jnp.bfloat16)
    for c in range(cols):
        for k in range(share):
            w = c * share + k
            piece = left_ref[c, 0, :, k * size : (k + 1) * size].astype(jnp.float32)
            both = jnp.concatenate([piece[:half], piece[half:]], axis=1)
            left_rows[pl.ds(w, half, stride=width), :] = both

    for start in range(0, half, chunk):
        rows = left_rows[start * width : (start + chunk) * width, :].astype(jnp.bfloat16)
        first = jnp.dot(rows, state_diag[...], preferred_element_type=jnp.float32)
        columns = []
        for x in range(chunk):
            one = first[x * width : (x + 1) * width, :]
            columns.append(
                jnp.concatenate(
                    [one[:, s * lanes : (s + 1) * lanes] for s in range(states)], axis=0
                ).astype(jnp.bfloat16)
            )
        gathered = jnp.concatenate(columns, axis=1)
        channels = jnp.dot(mpo_ref[...], gathered, preferred_element_type=jnp.float32).astype(jnp.bfloat16)
        for x in range(chunk):
            for v in range(width):
                mixed[(start + x) * states : (start + x + 1) * states, v * lanes : (v + 1) * lanes] = channels[
                    v * states : (v + 1) * states, x * lanes : (x + 1) * lanes
                ]
    result[...] = jnp.dot(mixed[...], right_diag[...], preferred_element_type=jnp.float32)
    low = low[:half]
    per = states // cols
    for t in range(0, states, 2):
        one = result[pl.ds(t, half, stride=states), :]
        two = result[pl.ds(t + 1, half, stride=states), :]
        upper = jnp.where(low, one, pltpu.roll(two, size, 1))
        lower = jnp.where(low, pltpu.roll(one, size, 1), two)
        at = (t % per) * size
        out_ref[t // per, 0, :half, at : at + lanes] = upper.astype(jnp.bfloat16)
        out_ref[t // per, 0, half:, at : at + lanes] = lower.astype(jnp.bfloat16)


def apply_blocks(order, slots, state_blocks, left, right, mpo_rows, states):
    cols, steps, size, share = left.shape
    near = right.shape[1]
    width = mpo_rows.shape[0] // states
    half, lanes = size // 2, 2 * size
    chunk = 8
    grid_spec = pltpu.PrefetchScalarGridSpec(
        num_scalar_prefetch=2,
        grid=(steps,),
        in_specs=[
            pl.BlockSpec((1, size, states * size), lambda k, o, s: (o[k], 0, 0)),
            pl.BlockSpec((cols, 1, size, share), lambda k, o, s: (0, k, 0, 0)),
            pl.BlockSpec((1, 1, size, width * size), lambda k, o, s: (s[k] // near, s[k] % near, 0, 0)),
            pl.BlockSpec(mpo_rows.shape, lambda k, o, s: (0, 0)),
        ],
        out_specs=pl.BlockSpec((cols, 1, size, states // cols * size), lambda k, o, s: (0, k, 0, 0)),
        scratch_shapes=[
            pltpu.VMEM((half * width, lanes), jnp.float32),
            pltpu.VMEM((lanes, states * lanes), jnp.bfloat16),
            pltpu.VMEM((width * lanes, lanes), jnp.bfloat16),
            pltpu.VMEM((half * states, width * lanes), jnp.bfloat16),
            pltpu.VMEM((half * states, lanes), jnp.float32),
        ],
    )
    return pl.pallas_call(
        functools.partial(apply_kernel, states, chunk),
        out_shape=jax.ShapeDtypeStruct((cols, steps, size, states // cols * size), jnp.bfloat16),
        grid_spec=grid_spec,
        compiler_params=pltpu.CompilerParams(vmem_limit_bytes=40 << 20),
        name="apply",
    )(order, slots, state_blocks, left, right, mpo_rows)


def place_kernel(order_ref, came_ref, out_ref, sem):
    cols, steps = came_ref.shape[:2]
    copies = []
    for col in range(cols):
        for step in range(steps):
            place = step * cols + col
            copy = pltpu.make_async_copy(came_ref.at[col, step], out_ref.at[order_ref[place]], sem.at[place])
            copy.start()
            copies.append(copy)
    for copy in copies:
        copy.wait()


def place_blocks(order, came):
    count = order.shape[0]
    return pl.pallas_call(
        place_kernel,
        out_shape=jax.ShapeDtypeStruct((count,) + came.shape[2:], came.dtype),
        in_specs=[pl.BlockSpec(memory_space=pltpu.SMEM), pl.BlockSpec(memory_space=pl.ANY)],
        out_specs=pl.BlockSpec(memory_space=pl.ANY),
        scratch_shapes=[pltpu.SemaphoreType.DMA((count,))],
        name="place",
    )(order, came)


def shards(state_blocks, left_env, right_env, mpo_tensor, block_left, block_owner, block_sub):
    rows = lax.axis_size("row")
    cols = lax.axis_size("col")
    count, size = state_blocks.shape[:2]
    states = state_blocks.shape[2] // size
    width = mpo_tensor.shape[0]
    most = max(2, (2 * count + rows - 1) // rows)
    near = -(-most // cols)

    mpo_rows = jnp.transpose(mpo_tensor.reshape(width, width, states, states), (1, 2, 3, 0)).reshape(
        width * states, states * width
    )
    left_out, order, wanted, slots = route(block_left, block_owner[:, 0], block_sub, left_env, rows, cols, near)
    asked = lax.all_to_all(wanted, "row", split_axis=0, concat_axis=0, tiled=True)
    left = lax.all_to_all(left_out, "col", split_axis=0, concat_axis=0, tiled=True)
    right = lax.all_to_all(pick(asked, right_env), "row", split_axis=0, concat_axis=0, tiled=True)
    mine = lax.axis_index("col")
    my_order = lax.dynamic_slice_in_dim(order.reshape(-1, cols), mine, 1, 1)[:, 0]
    my_slots = lax.dynamic_slice_in_dim(slots.reshape(-1, cols), mine, 1, 1)[:, 0]
    done = apply_blocks(my_order, my_slots, state_blocks, left, right, mpo_rows, states)
    came = lax.all_to_all(done, "col", split_axis=0, concat_axis=0, tiled=True)
    return place_blocks(order, came)


def solution(mesh):
    placed = (
        P(("groups", "row"), None, None),
        P(("groups", "row"), None, "col"),
        P(("groups", "row"), None, None),
        P(),
        P(("groups", "row")),
        P(("groups", "row"), None),
        P(("groups", "row")),
    )
    return jax.shard_map(
        shards,
        mesh=mesh,
        in_specs=placed,
        out_specs=P(("groups", "row"), None, "col"),
        check_vma=False,
    )
```

```python
import functools

import jax
import jax.numpy as jnp
from jax import lax
from jax.experimental import pallas as pl
from jax.experimental.pallas import tpu as pltpu
from jax.sharding import PartitionSpec as P

PARTS = 2
CHUNK = 8
SMEM = pl.BlockSpec(memory_space=pltpu.SMEM)
VMEM = pl.BlockSpec(memory_space=pltpu.VMEM)
ANY = pl.BlockSpec(memory_space=pl.ANY)


def swap(array, axis, step):
    size = lax.axis_size(axis)
    return lax.ppermute(array, axis, [(i, i ^ step) for i in range(size)])


def run_copies(copies):
    for copy in copies:
        copy.start()
    for copy in copies:
        copy.wait()


def route_kernel(rows, cols, near, parts, left_ref, key_ref, env_ref, *refs):
    sends = refs[: cols * parts]
    order_ref, slot_ref, by_place, place_slot, sem = refs[cols * parts :]
    count = left_ref.shape[0]
    steps = count // cols
    per_part = steps // parts
    mine = lax.axis_index("col")
    owners = [lax.div(key_ref[p], 1 << 16) for p in range(count)]
    for p in range(count):
        rank = jnp.int32(0)
        first = jnp.int32(0)
        for other in range(count):
            first = first + (owners[other] < owners[p]).astype(jnp.int32)
            if other < p:
                rank = rank + (owners[other] == owners[p]).astype(jnp.int32)
        place = first + rank
        offset = lax.rem(lax.rem(place, cols) - lax.rem(first, cols) + cols, cols)
        by_place[place] = p
        place_slot[place] = lax.div(rank - offset, cols)
    for col in range(cols):
        at = jnp.int32(col * steps)
        for slot in range(near):
            for step in range(steps):
                place = step * cols + col

                @pl.when(place_slot[place] == slot)
                def _():
                    p = by_place[place]
                    order_ref[at] = p
                    slot_ref[at] = lax.div(key_ref[p], 1 << 16) * near + slot

                at = at + (place_slot[place] == slot).astype(jnp.int32)
    copies = []
    for part in range(parts):
        for other in range(cols):
            col = jnp.bitwise_xor(mine, other)
            for step in range(per_part):
                p = order_ref[col * steps + part * per_part + step]
                copies.append(
                    pltpu.make_async_copy(
                        env_ref.at[left_ref[p]],
                        sends[part * cols + other].at[step],
                        sem.at[(part * cols + other) * per_part + step],
                    )
                )
    run_copies(copies)


def route(block_left, keys, left_env, rows, cols, near, parts):
    count = block_left.shape[0]
    size, width = left_env.shape[1:]
    piece = jax.ShapeDtypeStruct((count // cols // parts, size, width), left_env.dtype)
    listed = jax.ShapeDtypeStruct((count,), jnp.int32)
    *sends, order, slots = pl.pallas_call(
        functools.partial(route_kernel, rows, cols, near, parts),
        out_shape=(piece,) * (cols * parts) + (listed, listed),
        in_specs=[SMEM, SMEM, ANY],
        out_specs=(VMEM,) * (cols * parts) + (SMEM, SMEM),
        scratch_shapes=[
            pltpu.SMEM((count,), jnp.int32),
            pltpu.SMEM((count,), jnp.int32),
            pltpu.SemaphoreType.DMA((count,)),
        ],
        name="route",
    )(block_left, keys, left_env)
    return [sends[part * cols : (part + 1) * cols] for part in range(parts)], order, slots


def pick_kernel(rows, cols, near, *refs):
    key_refs = refs[: rows - 1]
    env_ref = refs[rows - 1]
    sends = refs[rows : rows + (rows - 1) * near]
    want, sem = refs[rows + (rows - 1) * near :]
    count = key_refs[0].shape[0]
    me = lax.axis_index("row")
    mine = lax.axis_index("col")
    copies = []
    for other in range(rows - 1):
        for slot in range(near):
            want[slot] = 0
        keys = [key_refs[other][p] for p in range(count)]
        owners = [lax.div(key, 1 << 16) for key in keys]
        place = jnp.int32(0)
        for p in range(count):
            place = place + (owners[p] < me).astype(jnp.int32)
        offset = lax.rem(mine - lax.rem(place, cols) + cols, cols)
        rank = jnp.int32(0)
        for p in range(count):
            here = owners[p] == me
            past = rank - offset

            @pl.when(here & (past >= 0) & (lax.rem(past + cols, cols) == 0))
            def _():
                want[lax.div(past, cols)] = lax.rem(keys[p], 1 << 16)

            rank = rank + here.astype(jnp.int32)
        for slot in range(near):
            at = slot * (rows - 1) + other
            copies.append(pltpu.make_async_copy(env_ref.at[want[slot]], sends[at], sem.at[at]))
            copies[-1].start()
    for copy in copies:
        copy.wait()


def pick(keys, right_env, cols, near):
    rows = len(keys) + 1
    sends = (rows - 1) * near
    piece = jax.ShapeDtypeStruct(right_env.shape[1:], right_env.dtype)
    return pl.pallas_call(
        functools.partial(pick_kernel, rows, cols, near),
        out_shape=(piece,) * sends,
        in_specs=[SMEM] * (rows - 1) + [ANY],
        out_specs=(VMEM,) * sends,
        scratch_shapes=[pltpu.SMEM((near,), jnp.int32), pltpu.SemaphoreType.DMA((sends,))],
        name="pick",
    )(*keys, right_env)


def halves(tile, low):
    swapped = pltpu.roll(tile, tile.shape[1] // 2, 1)
    zero = jnp.zeros_like(tile)
    return (
        jnp.where(low, tile, zero),
        jnp.where(low, zero, swapped),
        jnp.where(low, swapped, zero),
        jnp.where(low, zero, tile),
    )


def apply_kernel(states, rows, cols, near, waves, part, order_ref, slot_ref, key_ref, state_ref, mpo_ref, env_ref, *refs):
    lefts = refs[:cols]
    rights = refs[cols : cols + waves * (rows - 1)]
    outs = refs[cols + waves * (rows - 1) : 2 * cols + waves * (rows - 1)]
    block, right_now, left_rows, state_diag, right_diag, mixed, result, sem = refs[2 * cols + waves * (rows - 1) :]
    per_part, size = block.shape[:2]
    half = size // 2
    lanes = 2 * size
    width = mpo_ref.shape[0] // states
    share = width // cols
    steps = order_ref.shape[0] // cols
    low = lax.broadcasted_iota(jnp.int32, (size, lanes), 1) < size
    me = lax.axis_index("row")
    mine = lax.axis_index("col")
    step = pl.program_id(0)

    @pl.when(step == 0)
    def _():
        for k in range(per_part):
            at = mine * steps + part * per_part + k
            p = order_ref[at]
            owner = lax.div(slot_ref[at], near)
            slot = lax.rem(slot_ref[at], near)
            apart = jnp.bitwise_xor(owner, me)
            pltpu.make_async_copy(state_ref.at[p], block.at[k], sem.at[0, k]).start()

            @pl.when(apart == 0)
            def _():
                sector = lax.rem(key_ref[p], 1 << 16)
                pltpu.make_async_copy(env_ref.at[sector], right_now.at[k], sem.at[1, k]).start()

            for other in range(1, rows):
                for wave in range(waves):

                    @pl.when((apart == other) & (slot == wave))
                    def _():
                        pltpu.make_async_copy(
                            rights[wave * (rows - 1) + other - 1], right_now.at[k], sem.at[1, k]
                        ).start()

    pltpu.make_async_copy(state_ref.at[0], block.at[step], sem.at[0, step]).wait()
    for s in range(0, states, 2):
        tile = block[step, :, s * size : (s + 2) * size].astype(jnp.float32)
        pieces = halves(tile, low)
        for i in range(4):
            row, col = (i % 2) * size, (s + i // 2) * lanes
            state_diag[row : row + size, col : col + lanes] = pieces[i].astype(jnp.bfloat16)
    for other in range(cols):
        col = jnp.bitwise_xor(mine, other)
        for k in range(share):
            piece = lefts[other][0, :, k * size : (k + 1) * size].astype(jnp.float32)
            both = jnp.concatenate([piece[:half], piece[half:]], axis=1)
            left_rows[pl.ds(col * share + k, half, stride=width), :] = both

    for start in range(0, half, CHUNK):
        taken = left_rows[start * width : (start + CHUNK) * width, :].astype(jnp.bfloat16)
        first = jnp.dot(taken, state_diag[...], preferred_element_type=jnp.float32)
        columns = []
        for x in range(CHUNK):
            one = first[x * width : (x + 1) * width, :]
            columns.append(
                jnp.concatenate(
                    [one[:, s * lanes : (s + 1) * lanes] for s in range(states)], axis=0
                ).astype(jnp.bfloat16)
            )
        gathered = jnp.concatenate(columns, axis=1)
        channels = jnp.dot(mpo_ref[...], gathered, preferred_element_type=jnp.float32).astype(jnp.bfloat16)
        for x in range(CHUNK):
            for v in range(width):
                mixed[(start + x) * states : (start + x + 1) * states, v * lanes : (v + 1) * lanes] = channels[
                    v * states : (v + 1) * states, x * lanes : (x + 1) * lanes
                ]
    pltpu.make_async_copy(env_ref.at[0], right_now.at[step], sem.at[1, step]).wait()
    for v in range(0, width, 2):
        tile = right_now[step, :, v * size : (v + 2) * size].astype(jnp.float32)
        pieces = halves(tile, low)
        for i in range(4):
            at = v * lanes + i * size
            right_diag[at : at + size, :] = pieces[i].astype(jnp.bfloat16)
    result[...] = jnp.dot(mixed[...], right_diag[...], preferred_element_type=jnp.float32)
    low = low[:half]
    per = states // cols
    for other in range(cols):
        col = jnp.bitwise_xor(mine, other)
        for t in range(0, per, 2):
            one = result[pl.ds(col * per + t, half, stride=states), :]
            two = result[pl.ds(col * per + t + 1, half, stride=states), :]
            upper = jnp.where(low, one, pltpu.roll(two, size, 1))
            lower = jnp.where(low, pltpu.roll(one, size, 1), two)
            outs[other][0, :half, t * size : (t + 2) * size] = upper.astype(jnp.bfloat16)
            outs[other][0, half:, t * size : (t + 2) * size] = lower.astype(jnp.bfloat16)


def apply_blocks(order, slots, keys, state_blocks, mpo_rows, right_env, lefts, waves_of, states, rows, near, part):
    cols = len(lefts)
    per_part, size, share = lefts[0].shape
    waves = len(waves_of)
    width = mpo_rows.shape[0] // states
    half, lanes = size // 2, 2 * size
    out = (per_part, size, states // cols * size)
    flops = 2 * per_part * (width * size * size * states * size + (width * states) ** 2 * size * size)
    return pl.pallas_call(
        functools.partial(apply_kernel, states, rows, cols, near, waves, part),
        out_shape=[jax.ShapeDtypeStruct(out, jnp.bfloat16)] * cols,
        grid=(per_part,),
        in_specs=[SMEM, SMEM, SMEM, ANY, VMEM, ANY]
        + [pl.BlockSpec((1, size, share), lambda k: (k, 0, 0))] * cols
        + [ANY] * (waves * (rows - 1)),
        out_specs=[pl.BlockSpec((1,) + out[1:], lambda k: (k, 0, 0))] * cols,
        scratch_shapes=[
            pltpu.VMEM((per_part, size, states * size), jnp.bfloat16),
            pltpu.VMEM((per_part, size, width * size), jnp.bfloat16),
            pltpu.VMEM((half * width, lanes), jnp.float32),
            pltpu.VMEM((lanes, states * lanes), jnp.bfloat16),
            pltpu.VMEM((width * lanes, lanes), jnp.bfloat16),
            pltpu.VMEM((half * states, width * lanes), jnp.bfloat16),
            pltpu.VMEM((half * states, lanes), jnp.float32),
            pltpu.SemaphoreType.DMA((2, per_part)),
        ],
        compiler_params=pltpu.CompilerParams(vmem_limit_bytes=40 << 20),
        cost_estimate=pl.CostEstimate(flops=flops, bytes_accessed=4 << 20, transcendentals=0),
        name="apply",
    )(order, slots, keys, state_blocks, mpo_rows, right_env, *lefts, *[piece for wave in waves_of for piece in wave])


def place_kernel(cols, parts, order_ref, *refs):
    came = refs[: cols * parts]
    out_ref, sem = refs[cols * parts :]
    per_part = came[0].shape[0]
    steps = per_part * parts
    mine = lax.axis_index("col")
    copies = []
    for part in range(parts):
        for other in range(cols):
            col = jnp.bitwise_xor(mine, other)
            for step in range(per_part):
                p = order_ref[col * steps + part * per_part + step]
                copies.append(
                    pltpu.make_async_copy(
                        came[part * cols + other].at[step], out_ref.at[p], sem.at[len(copies)]
                    )
                )
    run_copies(copies)


def place_blocks(order, came):
    parts, cols = len(came), len(came[0])
    count = order.shape[0]
    pieces = [piece for part in came for piece in part]
    return pl.pallas_call(
        functools.partial(place_kernel, cols, parts),
        out_shape=jax.ShapeDtypeStruct((count,) + pieces[0].shape[1:], pieces[0].dtype),
        in_specs=[SMEM] + [ANY] * len(pieces),
        out_specs=VMEM,
        scratch_shapes=[pltpu.SemaphoreType.DMA((count,))],
        name="place",
    )(order, *pieces)


def shards(state_blocks, left_env, right_env, mpo_tensor, block_left, block_owner, block_sub):
    rows = lax.axis_size("row")
    cols = lax.axis_size("col")
    count, size = state_blocks.shape[:2]
    states = state_blocks.shape[2] // size
    width = mpo_tensor.shape[0]
    most = max(2, (2 * count + rows - 1) // rows)
    near = -(-most // cols)
    parts = PARTS

    keys = block_owner[:, 0] * (1 << 16) + block_sub
    others = [swap(keys, "row", step) for step in range(1, rows)]
    mpo_rows = jnp.transpose(mpo_tensor.reshape(width, width, states, states), (1, 2, 3, 0)).reshape(
        width * states, states * width
    )
    sends, order, slots = route(block_left, keys, left_env, rows, cols, near, parts)
    lefts = [[sends[part][0]] + [swap(sends[part][d], "col", d) for d in range(1, cols)] for part in range(parts)]
    picked = pick(others, right_env, cols, near)
    waves = [
        [swap(picked[slot * (rows - 1) + d - 1], "row", d) for d in range(1, rows)] for slot in range(near)
    ]
    came = []
    for part in range(parts):
        usable = near if part > 0 or parts == 1 else 1
        outs = apply_blocks(
            order, slots, keys, state_blocks, mpo_rows, right_env, lefts[part], waves[:usable], states, rows, near, part
        )
        came.append([outs[0]] + [swap(outs[d], "col", d) for d in range(1, cols)])
    return place_blocks(order, came)


def solution(mesh):
    placed = (
        P(("groups", "row"), None, None),
        P(("groups", "row"), None, "col"),
        P(("groups", "row"), None, None),
        P(),
        P(("groups", "row")),
        P(("groups", "row"), None),
        P(("groups", "row")),
    )
    return jax.shard_map(
        shards,
        mesh=mesh,
        in_specs=placed,
        out_specs=P(("groups", "row"), None, "col"),
        check_vma=False,
    )
```

```python
import functools

import jax
import jax.numpy as jnp
from jax import lax
from jax.experimental import pallas as pl
from jax.experimental.pallas import tpu as pltpu
from jax.sharding import PartitionSpec as P

CHUNK = 8
SHIFT = 16
SMEM = pl.BlockSpec(memory_space=pltpu.SMEM)
VMEM = pl.BlockSpec(memory_space=pltpu.VMEM)
HBM = pl.BlockSpec(memory_space=pltpu.HBM)
ANY = pl.BlockSpec(memory_space=pl.ANY)


def swap(array, axis, step):
    size = lax.axis_size(axis)
    return lax.ppermute(array, axis, [(i, i ^ step) for i in range(size)])


def run_copies(copies):
    for copy in copies:
        copy.start()
    for copy in copies:
        copy.wait()


def owner_of(key):
    return lax.shift_right_logical(key, SHIFT)


def sub_of(key):
    return jnp.bitwise_and(key, (1 << SHIFT) - 1)


def route_kernel(cols, near, left_ref, key_ref, env_ref, *refs):
    sends = refs[:cols]
    order_ref, slot_ref, by_place, sem = refs[cols:]
    count = left_ref.shape[0]
    steps = count // cols
    mine = lax.axis_index("col")
    owners = [owner_of(key_ref[p]) for p in range(count)]
    for p in range(count):
        place = jnp.int32(0)
        for other in range(count):
            if other < p:
                place = place + (owners[other] <= owners[p]).astype(jnp.int32)
            elif other > p:
                place = place + (owners[other] < owners[p]).astype(jnp.int32)
        by_place[place] = p
    for col in range(cols):
        before = None
        for step in range(steps):
            p = by_place[step * cols + col]
            owner = owner_of(key_ref[p])
            if before is None:
                slot = jnp.int32(0)
            else:
                slot = jnp.where(owner == before[0], before[1] + 1, 0)
            before = owner, slot
            order_ref[col * steps + step] = p
            slot_ref[col * steps + step] = owner * near + slot
    copies = []
    for other in range(cols):
        col = jnp.bitwise_xor(mine, other)
        for step in range(steps):
            p = order_ref[col * steps + step]
            copies.append(
                pltpu.make_async_copy(env_ref.at[left_ref[p]], sends[other].at[step], sem.at[len(copies)])
            )
    run_copies(copies)


def route(block_left, keys, left_env, cols, near):
    count = block_left.shape[0]
    size, width = left_env.shape[1:]
    piece = jax.ShapeDtypeStruct((count // cols, size, width), left_env.dtype)
    listed = jax.ShapeDtypeStruct((count,), jnp.int32)
    *sends, order, slots = pl.pallas_call(
        functools.partial(route_kernel, cols, near),
        out_shape=(piece,) * cols + (listed, listed),
        in_specs=[SMEM, SMEM, ANY],
        out_specs=(VMEM,) * cols + (SMEM, SMEM),
        scratch_shapes=[pltpu.SMEM((count,), jnp.int32), pltpu.SemaphoreType.DMA((count,))],
        name="route",
    )(block_left, keys, left_env)
    return sends, order, slots


def pick_kernel(rows, cols, near, *refs):
    key_refs = refs[: rows - 1]
    env_ref = refs[rows - 1]
    sends = refs[rows : 2 * rows - 1]
    sem = refs[2 * rows - 1]
    count = key_refs[0].shape[0]
    me = lax.axis_index("row")
    mine = lax.axis_index("col")
    copies = []
    for other in range(rows - 1):
        keys = [key_refs[other][p] for p in range(count)]
        owners = [owner_of(key) for key in keys]
        first = jnp.int32(0)
        for p in range(count):
            first = first + (owners[p] < me).astype(jnp.int32)
        past = -lax.rem(mine - lax.rem(first, cols) + cols, cols)
        wanted = [jnp.int32(0)] * near
        for p in range(count):
            here = owners[p] == me
            for slot in range(near):
                wanted[slot] = jnp.where(here & (past == slot * cols), sub_of(keys[p]), wanted[slot])
            past = past + here.astype(jnp.int32)
        for slot in range(near):
            copies.append(
                pltpu.make_async_copy(env_ref.at[wanted[slot]], sends[other].at[slot], sem.at[len(copies)])
            )
            copies[-1].start()
    for copy in copies:
        copy.wait()


def pick(keys, right_env, cols, near):
    rows = len(keys) + 1
    piece = jax.ShapeDtypeStruct((near,) + right_env.shape[1:], right_env.dtype)
    return pl.pallas_call(
        functools.partial(pick_kernel, rows, cols, near),
        out_shape=[piece] * (rows - 1),
        in_specs=[SMEM] * (rows - 1) + [HBM],
        out_specs=(VMEM,) * (rows - 1),
        scratch_shapes=[pltpu.SemaphoreType.DMA(((rows - 1) * near,))],
        name="pick",
    )(*keys, right_env)


def halves(tile, low):
    swapped = pltpu.roll(tile, tile.shape[1] // 2, 1)
    zero = jnp.zeros_like(tile)
    return (
        jnp.where(low, tile, zero),
        jnp.where(low, zero, swapped),
        jnp.where(low, swapped, zero),
        jnp.where(low, zero, tile),
    )


def apply_kernel(states, rows, cols, near, order_ref, slot_ref, key_ref, state_ref, mpo_ref, env_ref, *refs):
    lefts = refs[:cols]
    rights = refs[cols : cols + rows - 1]
    outs = refs[cols + rows - 1 : 2 * cols + rows - 1]
    block, right_now, left_rows, state_diag, right_diag, mixed, result, sem = refs[2 * cols + rows - 1 :]
    steps, size = block.shape[:2]
    half = size // 2
    lanes = 2 * size
    width = mpo_ref.shape[0] // states
    share = width // cols
    low = lax.broadcasted_iota(jnp.int32, (size, lanes), 1) < size
    me = lax.axis_index("row")
    mine = lax.axis_index("col")
    step = pl.program_id(0)

    @pl.when(step == 0)
    def _():
        for k in range(steps):
            p = order_ref[mine * steps + k]
            pltpu.make_async_copy(state_ref.at[p], block.at[k], sem.at[0, k]).start()
        for k in range(steps):
            at = mine * steps + k
            owner = lax.div(slot_ref[at], near)
            slot = lax.rem(slot_ref[at], near)
            apart = jnp.bitwise_xor(owner, me)

            @pl.when(apart == 0)
            def _():
                sector = sub_of(key_ref[order_ref[at]])
                pltpu.make_async_copy(env_ref.at[sector], right_now.at[k], sem.at[1, k]).start()

            for other in range(1, rows):

                @pl.when(apart == other)
                def _():
                    pltpu.make_async_copy(rights[other - 1].at[slot], right_now.at[k], sem.at[1, k]).start()

    pltpu.make_async_copy(state_ref.at[0], block.at[step], sem.at[0, step]).wait()
    for s in range(0, states, 2):
        tile = block[step, :, s * size : (s + 2) * size].astype(jnp.float32)
        pieces = halves(tile, low)
        for i in range(4):
            row, col = (i % 2) * size, (s + i // 2) * lanes
            state_diag[row : row + size, col : col + lanes] = pieces[i].astype(jnp.bfloat16)
    for other in range(cols):
        col = jnp.bitwise_xor(mine, other)
        for k in range(share):
            piece = lefts[other][0, :, k * size : (k + 1) * size].astype(jnp.float32)
            both = jnp.concatenate([piece[:half], piece[half:]], axis=1)
            left_rows[pl.ds(col * share + k, half, stride=width), :] = both

    for start in range(0, half, CHUNK):
        taken = left_rows[start * width : (start + CHUNK) * width, :].astype(jnp.bfloat16)
        first = jnp.dot(taken, state_diag[...], preferred_element_type=jnp.float32)
        columns = []
        for x in range(CHUNK):
            one = first[x * width : (x + 1) * width, :]
            columns.append(
                jnp.concatenate(
                    [one[:, s * lanes : (s + 1) * lanes] for s in range(states)], axis=0
                ).astype(jnp.bfloat16)
            )
        gathered = jnp.concatenate(columns, axis=1)
        channels = jnp.dot(mpo_ref[...], gathered, preferred_element_type=jnp.float32).astype(jnp.bfloat16)
        for x in range(CHUNK):
            for v in range(width):
                mixed[(start + x) * states : (start + x + 1) * states, v * lanes : (v + 1) * lanes] = channels[
                    v * states : (v + 1) * states, x * lanes : (x + 1) * lanes
                ]
    pltpu.make_async_copy(env_ref.at[0], right_now.at[step], sem.at[1, step]).wait()
    for v in range(0, width, 2):
        tile = right_now[step, :, v * size : (v + 2) * size].astype(jnp.float32)
        pieces = halves(tile, low)
        for i in range(4):
            at = v * lanes + i * size
            right_diag[at : at + size, :] = pieces[i].astype(jnp.bfloat16)
    result[...] = jnp.dot(mixed[...], right_diag[...], preferred_element_type=jnp.float32)
    low = low[:half]
    per = states // cols
    for other in range(cols):
        col = jnp.bitwise_xor(mine, other)
        for t in range(0, per, 2):
            one = result[pl.ds(col * per + t, half, stride=states), :]
            two = result[pl.ds(col * per + t + 1, half, stride=states), :]
            upper = jnp.where(low, one, pltpu.roll(two, size, 1))
            lower = jnp.where(low, pltpu.roll(one, size, 1), two)
            outs[other][0, :half, t * size : (t + 2) * size] = upper.astype(jnp.bfloat16)
            outs[other][0, half:, t * size : (t + 2) * size] = lower.astype(jnp.bfloat16)


def apply_blocks(order, slots, keys, state_blocks, mpo_rows, right_env, lefts, rights, states, near):
    cols, rows = len(lefts), len(rights) + 1
    steps, size, share = lefts[0].shape
    width = mpo_rows.shape[0] // states
    half, lanes = size // 2, 2 * size
    out = (steps, size, states // cols * size)
    flops = 2 * steps * (width * size * size * states * size + (width * states) ** 2 * size * size)
    return pl.pallas_call(
        functools.partial(apply_kernel, states, rows, cols, near),
        out_shape=[jax.ShapeDtypeStruct(out, jnp.bfloat16)] * cols,
        grid=(steps,),
        in_specs=[SMEM, SMEM, SMEM, HBM, VMEM, HBM]
        + [pl.BlockSpec((1, size, share), lambda k: (k, 0, 0))] * cols
        + [ANY] * (rows - 1),
        out_specs=[pl.BlockSpec((1,) + out[1:], lambda k: (k, 0, 0))] * cols,
        scratch_shapes=[
            pltpu.VMEM((steps, size, states * size), jnp.bfloat16),
            pltpu.VMEM((steps, size, width * size), jnp.bfloat16),
            pltpu.VMEM((half * width, lanes), jnp.float32),
            pltpu.VMEM((lanes, states * lanes), jnp.bfloat16),
            pltpu.VMEM((width * lanes, lanes), jnp.bfloat16),
            pltpu.VMEM((half * states, width * lanes), jnp.bfloat16),
            pltpu.VMEM((half * states, lanes), jnp.float32),
            pltpu.SemaphoreType.DMA((2, steps)),
        ],
        compiler_params=pltpu.CompilerParams(vmem_limit_bytes=40 << 20),
        cost_estimate=pl.CostEstimate(flops=flops, bytes_accessed=4 << 20, transcendentals=0),
        name="apply",
    )(order, slots, keys, state_blocks, mpo_rows, right_env, *lefts, *rights)


def place_kernel(cols, order_ref, *refs):
    came = refs[:cols]
    out_ref, sem = refs[cols:]
    steps = came[0].shape[0]
    mine = lax.axis_index("col")
    copies = []
    for other in range(cols):
        col = jnp.bitwise_xor(mine, other)
        for step in range(steps):
            p = order_ref[col * steps + step]
            copies.append(pltpu.make_async_copy(came[other].at[step], out_ref.at[p], sem.at[len(copies)]))
    run_copies(copies)


def place_blocks(order, came):
    cols = len(came)
    count = order.shape[0]
    return pl.pallas_call(
        functools.partial(place_kernel, cols),
        out_shape=jax.ShapeDtypeStruct((count,) + came[0].shape[1:], came[0].dtype),
        in_specs=[SMEM] + [VMEM] * cols,
        out_specs=HBM,
        scratch_shapes=[pltpu.SemaphoreType.DMA((count,))],
        name="place",
    )(order, *came)


def shards(state_blocks, left_env, right_env, mpo_tensor, block_left, block_owner, block_sub):
    rows = lax.axis_size("row")
    cols = lax.axis_size("col")
    count, size = state_blocks.shape[:2]
    states = state_blocks.shape[2] // size
    width = mpo_tensor.shape[0]
    most = max(2, (2 * count + rows - 1) // rows)
    near = -(-most // cols)

    keys = jnp.bitwise_or(lax.shift_left(block_owner[:, 0], SHIFT), block_sub)
    others = [swap(keys, "row", step) for step in range(1, rows)]
    sends, order, slots = route(block_left, keys, left_env, cols, near)
    picked = pick(others, right_env, cols, near)
    near_send, first_pick = lax.optimization_barrier((sends[1], picked[0]))
    sends = [sends[0], near_send, *sends[2:]]
    picked = [first_pick, *picked[1:]]
    lefts = [sends[0]] + [swap(sends[d], "col", d) for d in range(1, cols)]
    rights = [swap(picked[d - 1], "row", d) for d in range(1, rows)]
    mpo_rows = jnp.transpose(mpo_tensor.reshape(width, width, states, states), (1, 2, 3, 0)).reshape(
        width * states, states * width
    )
    outs = apply_blocks(order, slots, keys, state_blocks, mpo_rows, right_env, lefts, rights, states, near)
    return place_blocks(order, [outs[0]] + [swap(outs[d], "col", d) for d in range(1, cols)])


def solution(mesh):
    placed = (
        P(("groups", "row"), None, None),
        P(("groups", "row"), None, "col"),
        P(("groups", "row"), None, None),
        P(),
        P(("groups", "row")),
        P(("groups", "row"), None),
        P(("groups", "row")),
    )
    return jax.shard_map(
        shards,
        mesh=mesh,
        in_specs=placed,
        out_specs=P(("groups", "row"), None, "col"),
        check_vma=False,
    )
```

```python
import functools

import jax
import jax.numpy as jnp
from jax import lax
from jax.experimental import pallas as pl
from jax.experimental.pallas import tpu as pltpu
from jax.sharding import PartitionSpec as P

CHUNK = 8
SHIFT = 16
SMEM = pl.BlockSpec(memory_space=pltpu.SMEM)
VMEM = pl.BlockSpec(memory_space=pltpu.VMEM)
HBM = pl.BlockSpec(memory_space=pltpu.HBM)
ANY = pl.BlockSpec(memory_space=pl.ANY)


def swap(array, axis, step):
    size = lax.axis_size(axis)
    return lax.ppermute(array, axis, [(i, i ^ step) for i in range(size)])


def run_copies(copies):
    for copy in copies:
        copy.start()
    for copy in copies:
        copy.wait()


def owner_of(key):
    return lax.shift_right_logical(key, SHIFT)


def sub_of(key):
    return jnp.bitwise_and(key, (1 << SHIFT) - 1)


def route_kernel(cols, near, left_ref, key_ref, env_ref, *refs):
    sends = refs[:cols]
    order_ref, slot_ref, by_place = refs[cols:]
    count = left_ref.shape[0]
    steps = count // cols
    mine = lax.axis_index("col")
    owners = [owner_of(key_ref[p]) for p in range(count)]
    for p in range(count):
        place = jnp.int32(0)
        for other in range(count):
            if other < p:
                place = place + (owners[other] <= owners[p]).astype(jnp.int32)
            elif other > p:
                place = place + (owners[other] < owners[p]).astype(jnp.int32)
        by_place[place] = p
    for col in range(cols):
        before = None
        for step in range(steps):
            p = by_place[step * cols + col]
            owner = owner_of(key_ref[p])
            if before is None:
                slot = jnp.int32(0)
            else:
                slot = jnp.where(owner == before[0], before[1] + 1, 0)
            before = owner, slot
            order_ref[col * steps + step] = p
            slot_ref[col * steps + step] = owner * near + slot
    for other in range(cols):
        col = jnp.bitwise_xor(mine, other)
        for step in range(steps):
            p = order_ref[col * steps + step]
            sends[other][step] = env_ref[left_ref[p]]


def route(block_left, keys, left_env, cols, near):
    count = block_left.shape[0]
    size, width = left_env.shape[1:]
    piece = jax.ShapeDtypeStruct((count // cols, size, width), left_env.dtype)
    listed = jax.ShapeDtypeStruct((count,), jnp.int32)
    *sends, order, slots = pl.pallas_call(
        functools.partial(route_kernel, cols, near),
        out_shape=(piece,) * cols + (listed, listed),
        in_specs=[SMEM, SMEM, VMEM],
        out_specs=(VMEM,) * cols + (SMEM, SMEM),
        scratch_shapes=[pltpu.SMEM((count,), jnp.int32)],
        name="route",
    )(block_left, keys, left_env)
    return sends, order, slots


def pick_kernel(rows, cols, near, *refs):
    key_refs = refs[: rows - 1]
    env_ref = refs[rows - 1]
    sends = refs[rows:]
    count = key_refs[0].shape[0]
    me = lax.axis_index("row")
    mine = lax.axis_index("col")
    for other in range(rows - 1):
        keys = [key_refs[other][p] for p in range(count)]
        owners = [owner_of(key) for key in keys]
        first = jnp.int32(0)
        for p in range(count):
            first = first + (owners[p] < me).astype(jnp.int32)
        past = -lax.rem(mine - lax.rem(first, cols) + cols, cols)
        wanted = [jnp.int32(0)] * near
        for p in range(count):
            here = owners[p] == me
            for slot in range(near):
                wanted[slot] = jnp.where(here & (past == slot * cols), sub_of(keys[p]), wanted[slot])
            past = past + here.astype(jnp.int32)
        for slot in range(near):
            sends[other][slot] = env_ref[wanted[slot]]


def pick(keys, right_env, cols, near):
    rows = len(keys) + 1
    piece = jax.ShapeDtypeStruct((near,) + right_env.shape[1:], right_env.dtype)
    return pl.pallas_call(
        functools.partial(pick_kernel, rows, cols, near),
        out_shape=[piece] * (rows - 1),
        in_specs=[SMEM] * (rows - 1) + [VMEM],
        out_specs=(VMEM,) * (rows - 1),
        name="pick",
    )(*keys, right_env)


def halves(tile, low):
    swapped = pltpu.roll(tile, tile.shape[1] // 2, 1)
    zero = jnp.zeros_like(tile)
    return (
        jnp.where(low, tile, zero),
        jnp.where(low, zero, swapped),
        jnp.where(low, swapped, zero),
        jnp.where(low, zero, tile),
    )


def spread_state(block, state_diag, low):
    size = block.shape[0]
    for s in range(0, block.shape[1] // size, 2):
        pieces = halves(block[:, s * size : (s + 2) * size].astype(jnp.float32), low)
        for i in range(4):
            row, col = (i % 2) * size, (s + i // 2) * 2 * size
            state_diag[row : row + size, col : col + 2 * size] = pieces[i].astype(jnp.bfloat16)


def spread_right(right, right_diag, low):
    size = right.shape[0]
    for v in range(0, right.shape[1] // size, 2):
        pieces = halves(right[:, v * size : (v + 2) * size].astype(jnp.float32), low)
        for i in range(4):
            at = (2 * v + i) * size
            right_diag[at : at + size, :] = pieces[i].astype(jnp.bfloat16)


def spread_left(lefts, step, left_rows):
    cols = len(lefts)
    size = lefts[0].shape[1]
    half, share = size // 2, lefts[0].shape[2] // size
    mine = lax.axis_index("col")
    for other in range(cols):
        col = jnp.bitwise_xor(mine, other)
        for k in range(share):
            piece = lefts[other][step, :, k * size : (k + 1) * size].astype(jnp.float32)
            both = jnp.concatenate([piece[:half], piece[half:]], axis=1)
            left_rows[pl.ds(col * share + k, half, stride=cols * share), :] = both


def mix_block(states, left_rows, state_diag, mpo_ref, mixed):
    width = mpo_ref.shape[0] // states
    lanes = left_rows.shape[1]
    half = left_rows.shape[0] // width
    for start in range(0, half, CHUNK):
        taken = left_rows[start * width : (start + CHUNK) * width, :].astype(jnp.bfloat16)
        first = jnp.dot(taken, state_diag[...], preferred_element_type=jnp.float32)
        columns = []
        for x in range(CHUNK):
            one = first[x * width : (x + 1) * width, :]
            columns.append(
                jnp.concatenate(
                    [one[:, s * lanes : (s + 1) * lanes] for s in range(states)], axis=0
                ).astype(jnp.bfloat16)
            )
        gathered = jnp.concatenate(columns, axis=1)
        channels = jnp.dot(mpo_ref[...], gathered, preferred_element_type=jnp.float32).astype(jnp.bfloat16)
        for x in range(CHUNK):
            for v in range(width):
                mixed[(start + x) * states : (start + x + 1) * states, v * lanes : (v + 1) * lanes] = channels[
                    v * states : (v + 1) * states, x * lanes : (x + 1) * lanes
                ]


def finish_block(states, mixed, right_diag, result, outs, step, low):
    cols = len(outs)
    size = low.shape[0]
    half, per = size // 2, states // cols
    mine = lax.axis_index("col")
    result[...] = jnp.dot(mixed[...], right_diag[...], preferred_element_type=jnp.float32)
    low = low[:half]
    for other in range(cols):
        col = jnp.bitwise_xor(mine, other)
        for t in range(0, per, 2):
            one = result[pl.ds(col * per + t, half, stride=states), :]
            two = result[pl.ds(col * per + t + 1, half, stride=states), :]
            upper = jnp.where(low, one, pltpu.roll(two, size, 1))
            lower = jnp.where(low, pltpu.roll(one, size, 1), two)
            outs[other][step, :half, t * size : (t + 2) * size] = upper.astype(jnp.bfloat16)
            outs[other][step, half:, t * size : (t + 2) * size] = lower.astype(jnp.bfloat16)


def fetch_right(rows, near, first, order_ref, slot_ref, key_ref, env_ref, rights, right_now):
    steps = order_ref.shape[0] // lax.axis_size("col")
    me = lax.axis_index("row")
    for k in range(right_now.shape[0]):
        at = lax.axis_index("col") * steps + first + k
        slot = lax.rem(slot_ref[at], near)
        apart = jnp.bitwise_xor(lax.div(slot_ref[at], near), me)

        @pl.when(apart == 0)
        def _():
            right_now[k] = env_ref[sub_of(key_ref[order_ref[at]])]

        for other in range(1, rows):

            @pl.when(apart == other)
            def _():
                right_now[k] = rights[other - 1][slot]


def half_mask(size):
    return lax.broadcasted_iota(jnp.int32, (size, 2 * size), 1) < size


def mix_kernel(states, cols, count, order_ref, state_ref, mpo_ref, *refs):
    lefts, mixed, (state_diag, left_rows) = refs[:cols], refs[cols : cols + count], refs[cols + count :]
    low = half_mask(state_ref.shape[1])
    at = lax.axis_index("col") * (order_ref.shape[0] // cols)
    for k in range(count):
        spread_state(state_ref.at[order_ref[at + k]], state_diag.at[k], low)
        spread_left(lefts, k, left_rows.at[k])
    for k in range(count):
        mix_block(states, left_rows.at[k], state_diag.at[k], mpo_ref, mixed[k])


def put_own(first, order_ref, own, out_ref, sem):
    at = lax.axis_index("col") * (order_ref.shape[0] // lax.axis_size("col")) + first
    return [
        pltpu.make_async_copy(own.at[k], out_ref.at[order_ref[at + k]], sem.at[k]) for k in range(own.shape[0])
    ]


def right_kernel(states, rows, cols, near, order_ref, slot_ref, key_ref, env_ref, *refs):
    rights, refs = refs[: rows - 1], refs[rows - 1 :]
    own, right_now, right_diag, result, sem = refs[-5:]
    count = own.shape[0]
    mixed, out_ref, outs = refs[:count], refs[count], refs[count + 1 : count + cols]
    low = half_mask(env_ref.shape[1])
    fetch_right(rows, near, 0, order_ref, slot_ref, key_ref, env_ref, rights, right_now)
    for k in range(count):
        spread_right(right_now.at[k], right_diag.at[k], low)
    for k in range(count):
        finish_block(states, mixed[k], right_diag.at[k], result.at[k], (own,) + outs, k, low)
    run_copies(put_own(0, order_ref, own, out_ref, sem))


def apply_kernel(
    states, rows, cols, near, first, order_ref, slot_ref, key_ref, env_ref, state_ref, mpo_ref, out_in, *refs
):
    rights, lefts, refs = refs[: rows - 1], refs[rows - 1 : rows - 1 + cols], refs[rows - 1 + cols :]
    out_ref, outs = refs[0], refs[1:cols]
    own, right_now, state_diag, left_rows, right_diag, mixed, result, sem = refs[cols:]
    count = own.shape[0]
    low = half_mask(env_ref.shape[1])
    at = lax.axis_index("col") * (order_ref.shape[0] // cols) + first
    fetch_right(rows, near, first, order_ref, slot_ref, key_ref, env_ref, rights, right_now)
    for k in range(count):
        spread_state(state_ref.at[order_ref[at + k]], state_diag.at[k], low)
        spread_left(lefts, first + k, left_rows.at[k])
        spread_right(right_now.at[k], right_diag.at[k], low)
    for k in range(count):
        mix_block(states, left_rows.at[k], state_diag.at[k], mpo_ref, mixed.at[k])
        finish_block(states, mixed.at[k], right_diag.at[k], result.at[k], (own,) + outs, k, low)
    run_copies(put_own(first, order_ref, own, out_ref, sem))


def apply_blocks(order, slots, keys, state_blocks, mpo_rows, right_env, lefts, rights, states, near):
    cols, rows = len(lefts), len(rights) + 1
    steps, size, share = lefts[0].shape
    count = max(1, steps // 2)
    width = mpo_rows.shape[0] // states
    half, lanes = size // 2, 2 * size
    whole = jax.ShapeDtypeStruct((order.shape[0], size, states // cols * size), jnp.bfloat16)
    params = pltpu.CompilerParams(vmem_limit_bytes=32 << 20)

    def cost(blocks, mix, right):
        flops = mix * (width * size * size * states * size + (width * states) ** 2 * size * size)
        flops = 2 * blocks * (flops + right * states * size * size * width * size)
        return pl.CostEstimate(flops=flops, bytes_accessed=4 << 20, transcendentals=0)

    def sent(blocks):
        return [jax.ShapeDtypeStruct((blocks,) + whole.shape[1:], jnp.bfloat16)] * (cols - 1)

    def scratch(blocks, *names):
        kinds = dict(
            own=pltpu.VMEM((blocks,) + whole.shape[1:], jnp.bfloat16),
            right_now=pltpu.VMEM((blocks, size, width * size), jnp.bfloat16),
            state_diag=pltpu.VMEM((blocks, lanes, states * lanes), jnp.bfloat16),
            left_rows=pltpu.VMEM((blocks, half * width, lanes), jnp.float32),
            right_diag=pltpu.VMEM((blocks, width * lanes, lanes), jnp.bfloat16),
            mixed=pltpu.VMEM((blocks, half * states, width * lanes), jnp.bfloat16),
            result=pltpu.VMEM((blocks, half * states, lanes), jnp.float32),
            sem=pltpu.SemaphoreType.DMA((blocks,)),
        )
        return [kinds[name] for name in names]

    mixed = pl.pallas_call(
        functools.partial(mix_kernel, states, cols, count),
        out_shape=[jax.ShapeDtypeStruct((half * states, width * lanes), jnp.bfloat16)] * count,
        in_specs=[SMEM] + [VMEM] * (2 + cols),
        out_specs=[VMEM] * count,
        scratch_shapes=scratch(count, "state_diag", "left_rows"),
        compiler_params=params,
        cost_estimate=cost(count, 1, 0),
        name="mix",
    )(order, state_blocks, mpo_rows, *lefts)
    out, *early = pl.pallas_call(
        functools.partial(right_kernel, states, rows, cols, near),
        out_shape=[whole] + sent(count),
        in_specs=[SMEM] * 3 + [VMEM] * (rows + count),
        out_specs=[HBM] + [VMEM] * (cols - 1),
        scratch_shapes=scratch(count, "own", "right_now", "right_diag", "result", "sem"),
        compiler_params=params,
        cost_estimate=cost(count, 0, 1),
        name="right",
    )(order, slots, keys, right_env, *rights, *mixed)
    if count == steps:
        return out, [early]
    out, *late = pl.pallas_call(
        functools.partial(apply_kernel, states, rows, cols, near, count),
        out_shape=[whole] + sent(steps - count),
        in_specs=[SMEM] * 3 + [VMEM] * 3 + [HBM] + [VMEM] * (rows - 1 + cols),
        out_specs=[HBM] + [VMEM] * (cols - 1),
        scratch_shapes=scratch(
            steps - count,
            "own", "right_now", "state_diag", "left_rows", "right_diag", "mixed", "result", "sem",
        ),
        input_output_aliases={6: 0},
        compiler_params=params,
        cost_estimate=cost(steps - count, 1, 1),
        name="apply",
    )(order, slots, keys, right_env, state_blocks, mpo_rows, out, *rights, *lefts)
    return out, [early, late]


def place_kernel(cols, first, order_ref, out_in, *refs):
    came, (out_ref, sem) = refs[: cols - 1], refs[cols - 1 :]
    steps = order_ref.shape[0] // cols
    mine = lax.axis_index("col")
    copies = []
    for other in range(1, cols):
        col = jnp.bitwise_xor(mine, other)
        for k in range(came[0].shape[0]):
            p = order_ref[col * steps + first + k]
            copies.append(pltpu.make_async_copy(came[other - 1].at[k], out_ref.at[p], sem.at[len(copies)]))
    run_copies(copies)


def place_blocks(order, out, came, first):
    cols = len(came) + 1
    return pl.pallas_call(
        functools.partial(place_kernel, cols, first),
        out_shape=jax.ShapeDtypeStruct(out.shape, out.dtype),
        in_specs=[SMEM, HBM] + [VMEM] * (cols - 1),
        out_specs=HBM,
        scratch_shapes=[pltpu.SemaphoreType.DMA(((cols - 1) * came[0].shape[0],))],
        input_output_aliases={1: 0},
        name="place",
    )(order, out, *came)


def shards(state_blocks, left_env, right_env, mpo_tensor, block_left, block_owner, block_sub):
    rows = lax.axis_size("row")
    cols = lax.axis_size("col")
    count, size = state_blocks.shape[:2]
    states = state_blocks.shape[2] // size
    width = mpo_tensor.shape[0]
    most = max(2, (2 * count + rows - 1) // rows)
    near = -(-most // cols)

    keys = jnp.bitwise_or(lax.shift_left(block_owner[:, 0], SHIFT), block_sub)
    others = [swap(keys, "row", step) for step in range(1, rows)]
    sends, order, slots = route(block_left, keys, left_env, cols, near)
    order, *others = lax.optimization_barrier((order, *others))
    picked = pick(others, right_env, cols, near)
    rights = [swap(picked[d - 1], "row", d) for d in range(1, rows)]
    near_send, rights[0] = lax.optimization_barrier((sends[1], rights[0]))
    sends = [sends[0], near_send, *sends[2:]]
    lefts = [sends[0]] + [swap(sends[d], "col", d) for d in range(1, cols)]
    mpo_rows = jnp.transpose(mpo_tensor.reshape(width, width, states, states), (1, 2, 3, 0)).reshape(
        width * states, states * width
    )
    out, parts = apply_blocks(order, slots, keys, state_blocks, mpo_rows, right_env, lefts, rights, states, near)
    first, came = 0, []
    for sent in parts:
        joined = lax.optimization_barrier((*sent, *came))
        arrived = [swap(joined[d - 1], "col", d) for d in range(1, cols)]
        if came:
            out = place_blocks(order, out, joined[cols - 1 :], first)
            first += came[0].shape[0]
        came = arrived
    return place_blocks(order, out, came, first)


def solution(mesh):
    placed = (
        P(("groups", "row"), None, None),
        P(("groups", "row"), None, "col"),
        P(("groups", "row"), None, None),
        P(),
        P(("groups", "row")),
        P(("groups", "row"), None),
        P(("groups", "row")),
    )
    return jax.shard_map(
        shards,
        mesh=mesh,
        in_specs=placed,
        out_specs=P(("groups", "row"), None, "col"),
        check_vma=False,
    )
```

```python
import functools

import jax
import jax.numpy as jnp
from jax import lax
from jax.experimental import pallas as pl
from jax.experimental.pallas import tpu as pltpu
from jax.sharding import PartitionSpec as P

CHUNK = 8
SHIFT = 16
SMEM = pl.BlockSpec(memory_space=pltpu.SMEM)
VMEM = pl.BlockSpec(memory_space=pltpu.VMEM)
HBM = pl.BlockSpec(memory_space=pltpu.HBM)
ANY = pl.BlockSpec(memory_space=pl.ANY)


def swap(array, axis, step):
    size = lax.axis_size(axis)
    return lax.ppermute(array, axis, [(i, i ^ step) for i in range(size)])


def run_copies(copies):
    for copy in copies:
        copy.start()
    for copy in copies:
        copy.wait()


def owner_of(key):
    return lax.shift_right_logical(key, SHIFT)


def sub_of(key):
    return jnp.bitwise_and(key, (1 << SHIFT) - 1)


def route_kernel(cols, near, left_ref, key_ref, env_ref, *refs):
    sends = refs[:cols]
    order_ref, slot_ref, by_place = refs[cols:]
    count = left_ref.shape[0]
    steps = count // cols
    mine = lax.axis_index("col")
    owners = [owner_of(key_ref[p]) for p in range(count)]
    for p in range(count):
        place = jnp.int32(0)
        for other in range(count):
            if other < p:
                place = place + (owners[other] <= owners[p]).astype(jnp.int32)
            elif other > p:
                place = place + (owners[other] < owners[p]).astype(jnp.int32)
        by_place[place] = p
    for col in range(cols):
        before = None
        for step in range(steps):
            p = by_place[step * cols + col]
            owner = owner_of(key_ref[p])
            if before is None:
                slot = jnp.int32(0)
            else:
                slot = jnp.where(owner == before[0], before[1] + 1, 0)
            before = owner, slot
            order_ref[col * steps + step] = p
            slot_ref[col * steps + step] = owner * near + slot
    for other in range(cols):
        col = jnp.bitwise_xor(mine, other)
        for step in range(steps):
            p = order_ref[col * steps + step]
            sends[other][step] = env_ref[left_ref[p]]


def route(block_left, keys, left_env, cols, near):
    count = block_left.shape[0]
    size, width = left_env.shape[1:]
    piece = jax.ShapeDtypeStruct((count // cols, size, width), left_env.dtype)
    listed = jax.ShapeDtypeStruct((count,), jnp.int32)
    *sends, order, slots = pl.pallas_call(
        functools.partial(route_kernel, cols, near),
        out_shape=(piece,) * cols + (listed, listed),
        in_specs=[SMEM, SMEM, VMEM],
        out_specs=(VMEM,) * cols + (SMEM, SMEM),
        scratch_shapes=[pltpu.SMEM((count,), jnp.int32)],
        compiler_params=pltpu.CompilerParams(vmem_limit_bytes=6 << 20),
        name="route",
    )(block_left, keys, left_env)
    return sends, order, slots


def pick_kernel(rows, cols, near, *refs):
    key_refs = refs[: rows - 1]
    env_ref = refs[rows - 1]
    sends = refs[rows:]
    count = key_refs[0].shape[0]
    me = lax.axis_index("row")
    mine = lax.axis_index("col")
    for other in range(rows - 1):
        keys = [key_refs[other][p] for p in range(count)]
        owners = [owner_of(key) for key in keys]
        first = jnp.int32(0)
        for p in range(count):
            first = first + (owners[p] < me).astype(jnp.int32)
        past = -lax.rem(mine - lax.rem(first, cols) + cols, cols)
        wanted = [jnp.int32(0)] * near
        for p in range(count):
            here = owners[p] == me
            for slot in range(near):
                wanted[slot] = jnp.where(here & (past == slot * cols), sub_of(keys[p]), wanted[slot])
            past = past + here.astype(jnp.int32)
        for slot in range(near):
            sends[other][slot] = env_ref[wanted[slot]]


def pick(keys, right_env, cols, near):
    rows = len(keys) + 1
    piece = jax.ShapeDtypeStruct((near,) + right_env.shape[1:], right_env.dtype)
    return pl.pallas_call(
        functools.partial(pick_kernel, rows, cols, near),
        out_shape=[piece] * (rows - 1),
        in_specs=[SMEM] * (rows - 1) + [VMEM],
        out_specs=(VMEM,) * (rows - 1),
        compiler_params=pltpu.CompilerParams(vmem_limit_bytes=8 << 20),
        name="pick",
    )(*keys, right_env)


def halves(tile, low):
    swapped = pltpu.roll(tile, tile.shape[1] // 2, 1)
    zero = jnp.zeros_like(tile)
    return (
        jnp.where(low, tile, zero),
        jnp.where(low, zero, swapped),
        jnp.where(low, swapped, zero),
        jnp.where(low, zero, tile),
    )


def spread_state(block, state_diag, low):
    size = block.shape[0]
    for s in range(0, block.shape[1] // size, 2):
        pieces = halves(block[:, s * size : (s + 2) * size].astype(jnp.float32), low)
        for i in range(4):
            row, col = (i % 2) * size, (s + i // 2) * 2 * size
            state_diag[row : row + size, col : col + 2 * size] = pieces[i].astype(jnp.bfloat16)


def spread_right(right, right_diag, low):
    size = right.shape[0]
    for v in range(0, right.shape[1] // size, 2):
        pieces = halves(right[:, v * size : (v + 2) * size].astype(jnp.float32), low)
        for i in range(4):
            at = (2 * v + i) * size
            right_diag[at : at + size, :] = pieces[i].astype(jnp.bfloat16)


def spread_left(lefts, step, left_rows, at):
    cols = len(lefts)
    size = lefts[0].shape[1]
    half, share = size // 2, lefts[0].shape[2] // size
    mine = lax.axis_index("col")
    for other in range(cols):
        col = jnp.bitwise_xor(mine, other)
        for k in range(share):
            piece = lefts[other][step, :, k * size : (k + 1) * size].astype(jnp.float32)
            both = jnp.concatenate([piece[:half], piece[half:]], axis=1)
            left_rows[pl.ds(at + col * share + k, half, stride=cols * share), :] = both


def mix_blocks(states, first, count, lefts, diag_ref, mpo_ref, left_rows, one_ref, two_ref, mixed):
    width = mpo_ref.shape[0] // states
    lanes = left_rows.shape[1]
    half = lanes // 4
    chunks = half // CHUNK
    total = count * chunks

    def spread(k, carry):
        spread_left(lefts, first + k, left_rows, k * (half * width))
        return carry

    lax.fori_loop(0, count, spread, 0)

    def first_sum(i, into):
        rows = CHUNK * width
        taken = left_rows[pl.ds(pl.multiple_of(i * rows, rows), rows), :].astype(jnp.bfloat16)
        summed = jnp.dot(taken, diag_ref[first + lax.div(i, chunks)], preferred_element_type=jnp.float32)
        for x in range(CHUNK):
            one = summed[x * width : (x + 1) * width, :]
            for s in range(0, states, 2):
                both = jnp.concatenate(
                    [one[:, s * lanes : (s + 1) * lanes], one[:, (s + 1) * lanes : (s + 2) * lanes]], axis=0
                )
                into[s * width : (s + 2) * width, x * lanes : (x + 1) * lanes] = both.astype(jnp.bfloat16)

    def second_sum(i, taken):
        channels = jnp.dot(mpo_ref[...], taken[...], preferred_element_type=jnp.float32).astype(jnp.bfloat16)
        for x in range(CHUNK):
            row = pl.ds(pl.multiple_of((i * CHUNK + x) * states, states), states)
            for v in range(width):
                mixed[row, v * lanes : (v + 1) * lanes] = channels[
                    v * states : (v + 1) * states, x * lanes : (x + 1) * lanes
                ]

    first_sum(0, one_ref)

    def body(j, carry):
        first_sum(2 * j + 1, two_ref)
        second_sum(2 * j, one_ref)
        first_sum(jnp.minimum(2 * j + 2, total - 1), one_ref)
        second_sum(2 * j + 1, two_ref)
        return carry

    lax.fori_loop(0, total // 2, body, 0)


def finish_block(states, mixed, right_diag, result, outs, step, low):
    cols = len(outs)
    size = low.shape[0]
    half, per = size // 2, states // cols
    rows = half * states
    mine = lax.axis_index("col")
    taken = mixed[pl.ds(pl.multiple_of(step * rows, rows), rows), :]
    result[...] = jnp.dot(taken, right_diag[...], preferred_element_type=jnp.float32)
    low = low[:half]
    for other in range(cols):
        col = jnp.bitwise_xor(mine, other)
        for t in range(0, per, 2):
            one = result[pl.ds(col * per + t, half, stride=states), :]
            two = result[pl.ds(col * per + t + 1, half, stride=states), :]
            upper = jnp.where(low, one, pltpu.roll(two, size, 1))
            lower = jnp.where(low, pltpu.roll(one, size, 1), two)
            outs[other][step, :half, t * size : (t + 2) * size] = upper.astype(jnp.bfloat16)
            outs[other][step, half:, t * size : (t + 2) * size] = lower.astype(jnp.bfloat16)


def finish_blocks(
    states, rows, near, first, count, order_ref, slot_ref, key_ref, env_ref, rights, mixed, right_diag, result, outs
):
    cols = len(outs)
    me = lax.axis_index("row")
    low = half_mask(env_ref.shape[1])

    def body(k, carry):
        at = lax.axis_index("col") * (order_ref.shape[0] // cols) + first + k
        slot = lax.rem(slot_ref[at], near)
        apart = jnp.bitwise_xor(lax.div(slot_ref[at], near), me)

        @pl.when(apart == 0)
        def _():
            spread_right(env_ref.at[sub_of(key_ref[order_ref[at]])], right_diag, low)

        for other in range(1, rows):

            @pl.when(apart == other)
            def _():
                spread_right(rights[other - 1].at[slot], right_diag, low)

        finish_block(states, mixed, right_diag, result, outs, k, low)
        return carry

    lax.fori_loop(0, count, body, 0)


def half_mask(size):
    return lax.broadcasted_iota(jnp.int32, (size, 2 * size), 1) < size


def gather_kernel(states, order_ref, state_ref, after_ref, diag_ref, block, sem):
    steps, size = block.shape[:2]
    low = half_mask(size)
    at = lax.axis_index("col") * steps
    copies = [
        pltpu.make_async_copy(state_ref.at[order_ref[at + k]], block.at[k], sem.at[k]) for k in range(steps)
    ]
    run_copies(copies)

    def body(k, carry):
        spread_state(block.at[k], diag_ref.at[k], low)
        return carry

    lax.fori_loop(0, steps, body, 0)


def gather(order, state_blocks, after, cols, states):
    count, size = state_blocks.shape[:2]
    steps = count // cols
    return pl.pallas_call(
        functools.partial(gather_kernel, states),
        out_shape=jax.ShapeDtypeStruct((steps, 2 * size, 2 * states * size), jnp.bfloat16),
        in_specs=[SMEM, ANY, ANY],
        out_specs=VMEM,
        scratch_shapes=[
            pltpu.VMEM((steps, size, states * size), jnp.bfloat16),
            pltpu.SemaphoreType.DMA((steps,)),
        ],
        compiler_params=pltpu.CompilerParams(vmem_limit_bytes=8 << 20),
        name="gather",
    )(order, state_blocks, after)


def mix_kernel(states, cols, count, diag_ref, mpo_ref, *refs):
    lefts, (mixed, left_rows, one_ref, two_ref) = refs[:cols], refs[cols:]
    mix_blocks(states, 0, count, lefts, diag_ref, mpo_ref, left_rows, one_ref, two_ref, mixed)


def right_kernel(states, rows, cols, near, count, order_ref, slot_ref, key_ref, env_ref, *refs):
    rights, (mixed, *outs) = refs[: rows - 1], refs[rows - 1 : rows + cols]
    right_diag, result = refs[rows + cols :]
    finish_blocks(
        states, rows, near, 0, count, order_ref, slot_ref, key_ref, env_ref, rights, mixed, right_diag, result, outs
    )


def apply_kernel(
    states, rows, cols, near, first, count, order_ref, slot_ref, key_ref, env_ref, diag_ref, mpo_ref, *refs
):
    rights, lefts, refs = refs[: rows - 1], refs[rows - 1 : rows - 1 + cols], refs[rows - 1 + cols :]
    outs, (left_rows, one_ref, two_ref, mixed, right_diag, result) = refs[:cols], refs[cols:]
    mix_blocks(states, first, count, lefts, diag_ref, mpo_ref, left_rows, one_ref, two_ref, mixed)
    finish_blocks(
        states, rows, near, first, count, order_ref, slot_ref, key_ref, env_ref, rights, mixed, right_diag, result, outs
    )


def apply_blocks(order, slots, keys, state_diag, mpo_rows, right_env, lefts, rights, near):
    cols = len(lefts)
    rows = len(rights) + 1
    steps, size, share = lefts[0].shape
    count = max(1, steps // 2)
    width = share // size * cols
    states = mpo_rows.shape[0] // width
    half, lanes = size // 2, 2 * size
    params = pltpu.CompilerParams(vmem_limit_bytes=24 << 20)

    def cost(blocks, mix, right):
        flops = mix * (width * size * size * states * size + (width * states) ** 2 * size * size)
        flops = 2 * blocks * (flops + right * states * size * size * width * size)
        return pl.CostEstimate(flops=flops, bytes_accessed=4 << 20, transcendentals=0)

    def outs(blocks):
        return [jax.ShapeDtypeStruct((blocks, size, states // cols * size), jnp.bfloat16)] * cols

    def mix_scratch(blocks):
        return [
            pltpu.VMEM((blocks * half * width, lanes), jnp.float32),
            pltpu.VMEM((states * width, CHUNK * lanes), jnp.bfloat16),
            pltpu.VMEM((states * width, CHUNK * lanes), jnp.bfloat16),
        ]

    def mixed_shape(blocks):
        return (blocks * half * states, width * lanes)

    right_scratch = [pltpu.VMEM((width * lanes, lanes), jnp.bfloat16), pltpu.VMEM((half * states, lanes), jnp.float32)]
    mixed = pl.pallas_call(
        functools.partial(mix_kernel, states, cols, count),
        out_shape=jax.ShapeDtypeStruct(mixed_shape(count), jnp.bfloat16),
        in_specs=[VMEM] * (2 + cols),
        out_specs=VMEM,
        scratch_shapes=mix_scratch(count),
        compiler_params=params,
        cost_estimate=cost(count, 1, 0),
        name="mix",
    )(state_diag, mpo_rows, *lefts)
    early = pl.pallas_call(
        functools.partial(right_kernel, states, rows, cols, near, count),
        out_shape=outs(count),
        in_specs=[SMEM] * 3 + [VMEM] * (rows + 1),
        out_specs=[VMEM] * cols,
        scratch_shapes=right_scratch,
        compiler_params=params,
        cost_estimate=cost(count, 0, 1),
        name="right",
    )(order, slots, keys, right_env, *rights, mixed)
    if count == steps:
        return [early]
    late = pl.pallas_call(
        functools.partial(apply_kernel, states, rows, cols, near, count, steps - count),
        out_shape=outs(steps - count),
        in_specs=[SMEM] * 3 + [VMEM] * (3 + rows - 1 + cols),
        out_specs=[VMEM] * cols,
        scratch_shapes=mix_scratch(steps - count)
        + [pltpu.VMEM(mixed_shape(steps - count), jnp.bfloat16)]
        + right_scratch,
        compiler_params=params,
        cost_estimate=cost(steps - count, 1, 1),
        name="apply",
    )(order, slots, keys, right_env, state_diag, mpo_rows, *rights, *lefts)
    return [early, late]


def place_kernel(cols, pieces, begun, order_ref, *refs):
    came = refs[begun : begun + len(pieces)]
    out_ref, sem = refs[begun + len(pieces) :]
    steps = order_ref.shape[0] // cols
    mine = lax.axis_index("col")
    copies = []
    for piece, (other, first) in zip(came, pieces):
        col = jnp.bitwise_xor(mine, other)
        for k in range(piece.shape[0]):
            p = order_ref[col * steps + first + k]
            copies.append(pltpu.make_async_copy(piece.at[k], out_ref.at[p], sem.at[len(copies)]))
    run_copies(copies)


def place_blocks(order, out, came, pieces, cols):
    begun = [] if out is None else [out]
    return pl.pallas_call(
        functools.partial(place_kernel, cols, pieces, len(begun)),
        out_shape=jax.ShapeDtypeStruct((order.shape[0],) + came[0].shape[1:], came[0].dtype),
        in_specs=[SMEM] + [HBM] * len(begun) + [VMEM] * len(came),
        out_specs=HBM,
        scratch_shapes=[pltpu.SemaphoreType.DMA((sum(piece.shape[0] for piece in came),))],
        input_output_aliases={1: 0} if begun else {},
        compiler_params=pltpu.CompilerParams(vmem_limit_bytes=4 << 20),
        name="place",
    )(order, *begun, *came)


def shards(state_blocks, left_env, right_env, mpo_tensor, block_left, block_owner, block_sub):
    rows = lax.axis_size("row")
    cols = lax.axis_size("col")
    count, size = state_blocks.shape[:2]
    states = state_blocks.shape[2] // size
    width = mpo_tensor.shape[0]
    most = max(2, (2 * count + rows - 1) // rows)
    near = -(-most // cols)

    keys = jnp.bitwise_or(lax.shift_left(block_owner[:, 0], SHIFT), block_sub)
    others = [swap(keys, "row", step) for step in range(1, rows)]
    block_left, *others = lax.optimization_barrier((block_left, *others))
    sends, order, slots = route(block_left, keys, left_env, cols, near)
    lefts = [sends[0]] + [swap(sends[d], "col", d) for d in range(1, cols)]
    picked = pick(others, right_env, cols, near)
    rights = [None] + [swap(picked[d - 1], "row", d) for d in range(2, rows)]
    after, mpo_tensor = lax.optimization_barrier((picked[0], mpo_tensor))
    mpo_rows = jnp.transpose(mpo_tensor.reshape(width, width, states, states), (1, 2, 3, 0)).reshape(
        width * states, states * width
    )
    state_diag = gather(order, state_blocks, after, cols, states)
    near_send, state_diag, mpo_rows, *lefts[1:] = lax.optimization_barrier((after, state_diag, mpo_rows, *lefts[1:]))
    rights[0] = swap(near_send, "row", 1)
    parts = apply_blocks(order, slots, keys, state_diag, mpo_rows, right_env, lefts, rights, near)
    if len(parts) == 1:
        came = [swap(parts[0][d], "col", d) for d in range(1, cols)]
        return place_blocks(order, None, [parts[0][0], *came], [(d, 0) for d in range(cols)], cols)
    early, late = parts
    half = early[0].shape[0]
    came = [swap(early[d], "col", d) for d in range(1, cols)]
    late = list(late)
    joined = lax.optimization_barrier((*late[1:], *came))
    late[1:], came = joined[: cols - 1], joined[cols - 1 :]
    last = [swap(late[d], "col", d) for d in range(1, cols)]
    pieces = [(0, 0)] + [(d, 0) for d in range(1, cols)] + [(0, half)]
    out = place_blocks(order, None, [early[0], *came, late[0]], pieces, cols)
    return place_blocks(order, out, last, [(d, half) for d in range(1, cols)], cols)


def solution(mesh):
    placed = (
        P(("groups", "row"), None, None),
        P(("groups", "row"), None, "col"),
        P(("groups", "row"), None, None),
        P(),
        P(("groups", "row")),
        P(("groups", "row"), None),
        P(("groups", "row")),
    )
    return jax.shard_map(
        shards,
        mesh=mesh,
        in_specs=placed,
        out_specs=P(("groups", "row"), None, "col"),
        check_vma=False,
    )
```

```python
import functools

import jax
import jax.numpy as jnp
from jax import lax
from jax.experimental import pallas as pl
from jax.experimental.pallas import tpu as pltpu
from jax.sharding import PartitionSpec as P

CHUNK = 8
SHIFT = 16
SMEM = pl.BlockSpec(memory_space=pltpu.SMEM)
VMEM = pl.BlockSpec(memory_space=pltpu.VMEM)
HBM = pl.BlockSpec(memory_space=pltpu.HBM)
ANY = pl.BlockSpec(memory_space=pl.ANY)


def swap(array, axis, step):
    size = lax.axis_size(axis)
    return lax.ppermute(array, axis, [(i, i ^ step) for i in range(size)])


def run_copies(copies):
    for copy in copies:
        copy.start()
    for copy in copies:
        copy.wait()


def owner_of(key):
    return lax.shift_right_logical(key, SHIFT)


def sub_of(key):
    return jnp.bitwise_and(key, (1 << SHIFT) - 1)


def route_kernel(cols, near, parts, left_ref, key_ref, env_ref, *refs):
    sends = refs[: 2 + (cols - 2) * parts]
    order_ref, slot_ref, by_place, sem = refs[len(sends) :]
    count = left_ref.shape[0]
    steps = count // cols
    per_part = steps // parts
    mine = lax.axis_index("col")
    owners = [owner_of(key_ref[p]) for p in range(count)]
    for p in range(count):
        place = jnp.int32(0)
        for other in range(count):
            if other < p:
                place = place + (owners[other] <= owners[p]).astype(jnp.int32)
            elif other > p:
                place = place + (owners[other] < owners[p]).astype(jnp.int32)
        by_place[place] = p
    for col in range(cols):
        before = None
        for step in range(steps):
            p = by_place[step * cols + col]
            owner = owner_of(key_ref[p])
            if before is None:
                slot = jnp.int32(0)
            else:
                slot = jnp.where(owner == before[0], before[1] + 1, 0)
            before = owner, slot
            order_ref[col * steps + step] = p
            slot_ref[col * steps + step] = owner * near + slot
    copies = []
    for other in range(cols):
        col = jnp.bitwise_xor(mine, other)
        for step in range(steps):
            sector = left_ref[order_ref[col * steps + step]]
            if other < 2:
                target = sends[other].at[step]
            else:
                target = sends[2 + step // per_part * (cols - 2) + other - 2].at[step % per_part]
            copies.append(pltpu.make_async_copy(env_ref.at[sector], target, sem.at[len(copies)]))
            copies[-1].start()
    for copy in copies:
        copy.wait()


def route(block_left, keys, left_env, cols, near, parts):
    count = block_left.shape[0]
    size, width = left_env.shape[1:]
    steps = count // cols
    whole = jax.ShapeDtypeStruct((steps, size, width), left_env.dtype)
    piece = jax.ShapeDtypeStruct((steps // parts, size, width), left_env.dtype)
    listed = jax.ShapeDtypeStruct((count,), jnp.int32)
    far = (cols - 2) * parts
    *sends, order, slots = pl.pallas_call(
        functools.partial(route_kernel, cols, near, parts),
        out_shape=[whole] * 2 + [piece] * far + [listed] * 2,
        in_specs=[SMEM, SMEM, ANY],
        out_specs=[VMEM] * (2 + far) + [SMEM] * 2,
        scratch_shapes=[pltpu.SMEM((count,), jnp.int32), pltpu.SemaphoreType.DMA((count,))],
        name="route",
    )(block_left, keys, left_env)
    return sends, order, slots


def pick_kernel(rows, cols, near, *refs):
    key_refs, (env_ref, send_ref, sem) = refs[:rows], refs[rows:]
    count = key_refs[0].shape[0]
    me = lax.axis_index("row")
    mine = lax.axis_index("col")
    copies = []
    for other in range(rows):
        keys = [key_refs[other][p] for p in range(count)]
        owners = [owner_of(key) for key in keys]
        first = jnp.int32(0)
        for p in range(count):
            first = first + (owners[p] < me).astype(jnp.int32)
        past = -lax.rem(mine - lax.rem(first, cols) + cols, cols)
        wanted = [jnp.int32(0)] * near
        for p in range(count):
            here = owners[p] == me
            for slot in range(near):
                wanted[slot] = jnp.where(here & (past == slot * cols), sub_of(keys[p]), wanted[slot])
            past = past + here.astype(jnp.int32)
        for slot in range(near):
            target = send_ref.at[jnp.bitwise_xor(me, other), slot]
            copies.append(pltpu.make_async_copy(env_ref.at[wanted[slot]], target, sem.at[len(copies)]))
            copies[-1].start()
    for copy in copies:
        copy.wait()


def pick(keys, right_env, cols, near):
    rows = len(keys)
    return pl.pallas_call(
        functools.partial(pick_kernel, rows, cols, near),
        out_shape=jax.ShapeDtypeStruct((rows, near) + right_env.shape[1:], right_env.dtype),
        in_specs=[SMEM] * rows + [ANY],
        out_specs=VMEM,
        scratch_shapes=[pltpu.SemaphoreType.DMA((rows * near,))],
        name="pick",
    )(*keys, right_env)


def halves(tile, low):
    swapped = pltpu.roll(tile, tile.shape[1] // 2, 1)
    zero = jnp.zeros_like(tile)
    return (
        jnp.where(low, tile, zero),
        jnp.where(low, zero, swapped),
        jnp.where(low, swapped, zero),
        jnp.where(low, zero, tile),
    )


def spread_state(block, state_diag, low):
    size = block.shape[0]
    for s in range(0, block.shape[1] // size, 2):
        pieces = halves(block[:, s * size : (s + 2) * size].astype(jnp.float32), low)
        for i in range(4):
            row, col = (i % 2) * size, (s + i // 2) * 2 * size
            state_diag[row : row + size, col : col + 2 * size] = pieces[i].astype(jnp.bfloat16)


def spread_right(right, right_diag, low):
    size = right.shape[0]
    for v in range(0, right.shape[1] // size, 2):
        pieces = halves(right[:, v * size : (v + 2) * size].astype(jnp.float32), low)
        for i in range(4):
            at = (2 * v + i) * size
            right_diag[at : at + size, :] = pieces[i].astype(jnp.bfloat16)


def spread_left(lefts, left_rows):
    cols = len(lefts)
    size = lefts[0].shape[0]
    half, share = size // 2, lefts[0].shape[1] // size
    mine = lax.axis_index("col")
    for other in range(cols):
        col = jnp.bitwise_xor(mine, other)
        for k in range(share):
            piece = lefts[other][:, k * size : (k + 1) * size].astype(jnp.float32)
            both = jnp.concatenate([piece[:half], piece[half:]], axis=1)
            left_rows[pl.ds(col * share + k, half, stride=cols * share), :] = both


def mix_block(states, left_rows, state_diag, mpo_ref, mixed):
    width = mpo_ref.shape[0] // states
    lanes = left_rows.shape[1]
    half = left_rows.shape[0] // width
    for start in range(0, half, CHUNK):
        taken = left_rows[start * width : (start + CHUNK) * width, :].astype(jnp.bfloat16)
        first = jnp.dot(taken, state_diag[...], preferred_element_type=jnp.float32)
        columns = []
        for x in range(CHUNK):
            one = first[x * width : (x + 1) * width, :]
            columns.append(
                jnp.concatenate(
                    [one[:, s * lanes : (s + 1) * lanes] for s in range(states)], axis=0
                ).astype(jnp.bfloat16)
            )
        gathered = jnp.concatenate(columns, axis=1)
        channels = jnp.dot(mpo_ref[...], gathered, preferred_element_type=jnp.float32).astype(jnp.bfloat16)
        for x in range(CHUNK):
            for v in range(width):
                mixed[(start + x) * states : (start + x + 1) * states, v * lanes : (v + 1) * lanes] = channels[
                    v * states : (v + 1) * states, x * lanes : (x + 1) * lanes
                ]


def finish_block(states, mixed, right_diag, result, outs, low):
    cols = len(outs)
    size = low.shape[0]
    half, per = size // 2, states // cols
    mine = lax.axis_index("col")
    result[...] = jnp.dot(mixed[...], right_diag[...], preferred_element_type=jnp.float32)
    low = low[:half]
    for other in range(cols):
        col = jnp.bitwise_xor(mine, other)
        for t in range(0, per, 2):
            one = result[pl.ds(col * per + t, half, stride=states), :]
            two = result[pl.ds(col * per + t + 1, half, stride=states), :]
            upper = jnp.where(low, one, pltpu.roll(two, size, 1))
            lower = jnp.where(low, pltpu.roll(one, size, 1), two)
            outs[other][:half, t * size : (t + 2) * size] = upper.astype(jnp.bfloat16)
            outs[other][half:, t * size : (t + 2) * size] = lower.astype(jnp.bfloat16)


def half_mask(size):
    return lax.broadcasted_iota(jnp.int32, (size, 2 * size), 1) < size


def prepare_kernel(states, order_ref, state_ref, mpo_ref, after_ref, diag_ref, rows_ref, block, flat, sem):
    steps, size = block.shape[:2]
    width = mpo_ref.shape[0]
    low = half_mask(size)
    at = lax.axis_index("col") * steps
    copies = [
        pltpu.make_async_copy(state_ref.at[order_ref[at + k]], block.at[k], sem.at[k]) for k in range(steps)
    ]
    for copy in copies:
        copy.start()
    both = (states * states, states * states)
    row, col = lax.broadcasted_iota(jnp.int32, both, 0), lax.broadcasted_iota(jnp.int32, both, 1)
    turned = lax.rem(row, states) * states + lax.div(row, states)
    turn = jnp.where(turned == col, 1.0, 0.0).astype(jnp.bfloat16)
    split = flat.shape[0]
    for w in range(width):
        turned = jnp.dot(mpo_ref[w], turn, preferred_element_type=jnp.float32)
        for i in range(split):
            flat[i, w * width : (w + 1) * width, :] = turned[:, i * 128 : (i + 1) * 128]

    def one_channel(v, carry):
        taken = [jnp.transpose(flat[i, pl.ds(v, width, stride=width), :]) for i in range(split)]
        taken = jnp.concatenate(taken, axis=0)
        line = jnp.concatenate([taken[s * states : (s + 1) * states, :] for s in range(states)], axis=1)
        rows_ref[pl.ds(pl.multiple_of(v * states, states), states), :] = line.astype(jnp.bfloat16)
        return carry

    lax.fori_loop(0, width, one_channel, 0)
    for copy in copies:
        copy.wait()

    def one_block(k, carry):
        spread_state(block.at[k], diag_ref.at[k], low)
        return carry

    lax.fori_loop(0, steps, one_block, 0)


def prepare(order, state_blocks, mpo_tensor, after, cols, states):
    count, size = state_blocks.shape[:2]
    steps, width = count // cols, mpo_tensor.shape[0]
    return pl.pallas_call(
        functools.partial(prepare_kernel, states),
        out_shape=[
            jax.ShapeDtypeStruct((steps, 2 * size, 2 * states * size), jnp.bfloat16),
            jax.ShapeDtypeStruct((width * states, states * width), jnp.bfloat16),
        ],
        in_specs=[SMEM, ANY, VMEM, ANY],
        out_specs=[VMEM, VMEM],
        scratch_shapes=[
            pltpu.VMEM((steps, size, states * size), jnp.bfloat16),
            pltpu.VMEM((states * states // 128, width * width, 128), jnp.float32),
            pltpu.SemaphoreType.DMA((steps,)),
        ],
        compiler_params=pltpu.CompilerParams(vmem_limit_bytes=10 << 20),
        name="prepare",
    )(order, state_blocks, mpo_tensor, after)


def mix_kernel(states, cols, count, diag_ref, mpo_ref, *refs):
    lefts, mixed, left_rows = refs[:cols], refs[cols : cols + count], refs[-1]
    for k in range(count):
        spread_left([left.at[k] for left in lefts], left_rows.at[k])
    for k in range(count):
        mix_block(states, left_rows.at[k], diag_ref.at[k], mpo_ref, mixed[k])


def right_kernel(states, cols, near, count, order_ref, slot_ref, right_ref, *refs):
    mixed, outs, (right_diag, result) = refs[:count], refs[count : count + cols], refs[count + cols :]
    low = half_mask(right_ref.shape[2])
    at = lax.axis_index("col") * (order_ref.shape[0] // cols)
    for k in range(count):
        slot = slot_ref[at + k]
        spread_right(right_ref.at[lax.div(slot, near), lax.rem(slot, near)], right_diag.at[k], low)
    for k in range(count):
        finish_block(states, mixed[k], right_diag.at[k], result.at[k], [out.at[k] for out in outs], low)


def apply_kernel(
    states, cols, near, first, count, order_ref, slot_ref, right_ref, diag_ref, mpo_ref, early_ref, *refs
):
    lefts, outs, (left_rows, mixed, right_diag, result) = refs[:cols], refs[cols : 2 * cols], refs[2 * cols :]
    low = half_mask(right_ref.shape[2])
    at = lax.axis_index("col") * (order_ref.shape[0] // cols) + first
    outs[1][:first] = early_ref[...]
    for k in range(count):
        spread_left([left.at[k if d > 1 else first + k] for d, left in enumerate(lefts)], left_rows.at[k])
        slot = slot_ref[at + k]
        spread_right(right_ref.at[lax.div(slot, near), lax.rem(slot, near)], right_diag.at[k], low)
    for k in range(count):
        mix_block(states, left_rows.at[k], diag_ref.at[first + k], mpo_ref, mixed.at[k])
        into = [out.at[first + k if d == 1 else k] for d, out in enumerate(outs)]
        finish_block(states, mixed.at[k], right_diag.at[k], result.at[k], into, low)


def cost_of(blocks, states, width, size, mix, right):
    flops = mix * (width * size * size * states * size + (width * states) ** 2 * size * size)
    flops = 2 * blocks * (flops + right * states * size * size * width * size)
    return pl.CostEstimate(flops=flops, bytes_accessed=4 << 20, transcendentals=0)


def first_blocks(order, slots, state_diag, mpo_rows, right, lefts, near):
    cols = len(lefts)
    count, (size, share) = lefts[-1].shape[0], lefts[0].shape[1:]
    width = share // size * cols
    states = mpo_rows.shape[0] // width
    half, lanes = size // 2, 2 * size
    params = pltpu.CompilerParams(vmem_limit_bytes=24 << 20)
    mixed = pl.pallas_call(
        functools.partial(mix_kernel, states, cols, count),
        out_shape=[jax.ShapeDtypeStruct((half * states, width * lanes), jnp.bfloat16)] * count,
        in_specs=[VMEM] * (2 + cols),
        out_specs=[VMEM] * count,
        scratch_shapes=[pltpu.VMEM((count, half * width, lanes), jnp.float32)],
        compiler_params=params,
        cost_estimate=cost_of(count, states, width, size, 1, 0),
        name="mix",
    )(state_diag, mpo_rows, *lefts)
    return pl.pallas_call(
        functools.partial(right_kernel, states, cols, near, count),
        out_shape=[jax.ShapeDtypeStruct((count, size, states // cols * size), jnp.bfloat16)] * cols,
        in_specs=[SMEM] * 2 + [VMEM] * (1 + count),
        out_specs=[VMEM] * cols,
        scratch_shapes=[
            pltpu.VMEM((count, width * lanes, lanes), jnp.bfloat16),
            pltpu.VMEM((count, half * states, lanes), jnp.float32),
        ],
        compiler_params=params,
        cost_estimate=cost_of(count, states, width, size, 0, 1),
        name="right",
    )(order, slots, right, *mixed)


def last_blocks(order, slots, state_diag, mpo_rows, right, lefts, early, near):
    cols = len(lefts)
    first, count, (size, share) = early.shape[0], lefts[-1].shape[0], lefts[0].shape[1:]
    width = share // size * cols
    states = mpo_rows.shape[0] // width
    half, lanes = size // 2, 2 * size

    def out(blocks):
        return jax.ShapeDtypeStruct((blocks, size, states // cols * size), jnp.bfloat16)

    return pl.pallas_call(
        functools.partial(apply_kernel, states, cols, near, first, count),
        out_shape=[out(first + count if d == 1 else count) for d in range(cols)],
        in_specs=[SMEM] * 2 + [VMEM] * (4 + cols),
        out_specs=[VMEM] * cols,
        scratch_shapes=[
            pltpu.VMEM((count, half * width, lanes), jnp.float32),
            pltpu.VMEM((count, half * states, width * lanes), jnp.bfloat16),
            pltpu.VMEM((count, width * lanes, lanes), jnp.bfloat16),
            pltpu.VMEM((count, half * states, lanes), jnp.float32),
        ],
        compiler_params=pltpu.CompilerParams(vmem_limit_bytes=24 << 20),
        cost_estimate=cost_of(count, states, width, size, 1, 1),
        name="apply",
    )(order, slots, right, state_diag, mpo_rows, early, *lefts)


def place_kernel(cols, pieces, begun, order_ref, *refs):
    came = refs[begun : begun + len(pieces)]
    out_ref, sem = refs[begun + len(pieces) :]
    steps = order_ref.shape[0] // cols
    mine = lax.axis_index("col")
    copies = []
    for piece, (other, first) in zip(came, pieces):
        col = jnp.bitwise_xor(mine, other)
        for k in range(piece.shape[0]):
            p = order_ref[col * steps + first + k]
            copies.append(pltpu.make_async_copy(piece.at[k], out_ref.at[p], sem.at[len(copies)]))
    run_copies(copies)


def place_blocks(order, out, came, pieces, cols):
    begun = [] if out is None else [out]
    return pl.pallas_call(
        functools.partial(place_kernel, cols, pieces, len(begun)),
        out_shape=jax.ShapeDtypeStruct((order.shape[0],) + came[0].shape[1:], came[0].dtype),
        in_specs=[SMEM] + [HBM] * len(begun) + [VMEM] * len(came),
        out_specs=HBM,
        scratch_shapes=[pltpu.SemaphoreType.DMA((sum(piece.shape[0] for piece in came),))],
        input_output_aliases={1: 0} if begun else {},
        compiler_params=pltpu.CompilerParams(vmem_limit_bytes=4 << 20),
        name="place",
    )(order, *begun, *came)


def shards(state_blocks, left_env, right_env, mpo_tensor, block_left, block_owner, block_sub):
    rows = lax.axis_size("row")
    cols = lax.axis_size("col")
    count, size = state_blocks.shape[:2]
    states = state_blocks.shape[2] // size
    width = mpo_tensor.shape[0]
    most = max(2, (2 * count + rows - 1) // rows)
    near = -(-most // cols)

    parts = 2

    keys = jnp.bitwise_or(lax.shift_left(block_owner[:, 0], SHIFT), block_sub)
    others = [keys] + [swap(keys, "row", step) for step in range(1, rows)]
    picked = pick(others, right_env, cols, near)
    right = lax.all_to_all(picked, "row", split_axis=0, concat_axis=0, tiled=True)
    block_left, picked = lax.optimization_barrier((block_left, picked))
    sends, order, slots = route(block_left, keys, left_env, cols, near, parts)
    whole = [sends[0], swap(sends[1], "col", 1)]
    lefts = []
    for part in range(parts):
        far = sends[2 + part * (cols - 2) : 2 + (part + 1) * (cols - 2)]
        lefts.append(whole + [swap(far[d - 2], "col", d) for d in range(2, cols)])
    state_diag, mpo_rows = prepare(order, state_blocks, mpo_tensor, sends[0], cols, states)
    early = first_blocks(order, slots, state_diag, mpo_rows, right, lefts[0], near)
    came = [swap(early[d], "col", d) for d in range(2, cols)]
    late = last_blocks(order, slots, state_diag, mpo_rows, right, lefts[1], early[1], near)
    joined = lax.optimization_barrier((*late[1:], *came))
    sent, came = joined[: cols - 1], joined[cols - 1 :]
    last = [swap(sent[d - 1], "col", d) for d in range(1, cols)]
    half = early[0].shape[0]
    pieces = [(0, 0)] + [(d, 0) for d in range(2, cols)] + [(0, half)]
    out = place_blocks(order, None, [early[0], *came, late[0]], pieces, cols)
    pieces = [(1, 0)] + [(d, half) for d in range(2, cols)]
    return place_blocks(order, out, last, pieces, cols)


def solution(mesh):
    placed = (
        P(("groups", "row"), None, None),
        P(("groups", "row"), None, "col"),
        P(("groups", "row"), None, None),
        P(),
        P(("groups", "row")),
        P(("groups", "row"), None),
        P(("groups", "row")),
    )
    return jax.shard_map(
        shards,
        mesh=mesh,
        in_specs=placed,
        out_specs=P(("groups", "row"), None, "col"),
        check_vma=False,
    )
```

```python
import functools

import jax
import jax.numpy as jnp
from jax import lax
from jax.experimental import pallas as pl
from jax.experimental.pallas import tpu as pltpu
from jax.sharding import PartitionSpec as P

CHUNK = 8
SHIFT = 16
SMEM = pl.BlockSpec(memory_space=pltpu.SMEM)
VMEM = pl.BlockSpec(memory_space=pltpu.VMEM)
HBM = pl.BlockSpec(memory_space=pltpu.HBM)
ANY = pl.BlockSpec(memory_space=pl.ANY)


def swap(array, axis, step):
    size = lax.axis_size(axis)
    return lax.ppermute(array, axis, [(i, i ^ step) for i in range(size)])


def run_copies(copies):
    for copy in copies:
        copy.start()
    for copy in copies:
        copy.wait()


def owner_of(key):
    return lax.shift_right_logical(key, SHIFT)


def sub_of(key):
    return jnp.bitwise_and(key, (1 << SHIFT) - 1)


def route_kernel(cols, near, left_ref, key_ref, env_ref, *refs):
    sends = refs[:cols]
    order_ref, slot_ref, by_place = refs[cols:]
    count = left_ref.shape[0]
    steps = count // cols
    mine = lax.axis_index("col")
    owners = [owner_of(key_ref[p]) for p in range(count)]
    for p in range(count):
        place = jnp.int32(0)
        for other in range(count):
            if other < p:
                place = place + (owners[other] <= owners[p]).astype(jnp.int32)
            elif other > p:
                place = place + (owners[other] < owners[p]).astype(jnp.int32)
        by_place[place] = p
    for col in range(cols):
        before = None
        for step in range(steps):
            p = by_place[step * cols + col]
            owner = owner_of(key_ref[p])
            if before is None:
                slot = jnp.int32(0)
            else:
                slot = jnp.where(owner == before[0], before[1] + 1, 0)
            before = owner, slot
            order_ref[col * steps + step] = p
            slot_ref[col * steps + step] = owner * near + slot
    for other in range(cols):
        col = jnp.bitwise_xor(mine, other)
        for step in range(steps):
            p = order_ref[col * steps + step]
            sends[other][step] = env_ref[left_ref[p]]


def route(block_left, keys, left_env, cols, near):
    count = block_left.shape[0]
    size, width = left_env.shape[1:]
    piece = jax.ShapeDtypeStruct((count // cols, size, width), left_env.dtype)
    listed = jax.ShapeDtypeStruct((count,), jnp.int32)
    *sends, order, slots = pl.pallas_call(
        functools.partial(route_kernel, cols, near),
        out_shape=(piece,) * cols + (listed, listed),
        in_specs=[SMEM, SMEM, VMEM],
        out_specs=(VMEM,) * cols + (SMEM, SMEM),
        scratch_shapes=[pltpu.SMEM((count,), jnp.int32)],
        name="route",
    )(block_left, keys, left_env)
    return sends, order, slots


def pick_kernel(rows, cols, near, *refs):
    key_refs = refs[: rows - 1]
    env_ref = refs[rows - 1]
    sends = refs[rows:]
    count = key_refs[0].shape[0]
    me = lax.axis_index("row")
    mine = lax.axis_index("col")
    for other in range(rows - 1):
        keys = [key_refs[other][p] for p in range(count)]
        owners = [owner_of(key) for key in keys]
        first = jnp.int32(0)
        for p in range(count):
            first = first + (owners[p] < me).astype(jnp.int32)
        past = -lax.rem(mine - lax.rem(first, cols) + cols, cols)
        wanted = [jnp.int32(0)] * near
        for p in range(count):
            here = owners[p] == me
            for slot in range(near):
                wanted[slot] = jnp.where(here & (past == slot * cols), sub_of(keys[p]), wanted[slot])
            past = past + here.astype(jnp.int32)
        for slot in range(near):
            sends[other][slot] = env_ref[wanted[slot]]


def pick(keys, right_env, cols, near):
    rows = len(keys) + 1
    piece = jax.ShapeDtypeStruct((near,) + right_env.shape[1:], right_env.dtype)
    return pl.pallas_call(
        functools.partial(pick_kernel, rows, cols, near),
        out_shape=[piece] * (rows - 1),
        in_specs=[SMEM] * (rows - 1) + [VMEM],
        out_specs=(VMEM,) * (rows - 1),
        name="pick",
    )(*keys, right_env)


def halves(tile, low):
    swapped = pltpu.roll(tile, tile.shape[1] // 2, 1)
    zero = jnp.zeros_like(tile)
    return (
        jnp.where(low, tile, zero),
        jnp.where(low, zero, swapped),
        jnp.where(low, swapped, zero),
        jnp.where(low, zero, tile),
    )


def spread_state(block, state_diag, low):
    size = block.shape[0]
    for s in range(0, block.shape[1] // size, 2):
        pieces = halves(block[:, s * size : (s + 2) * size].astype(jnp.float32), low)
        for i in range(4):
            row, col = (i % 2) * size, (s + i // 2) * 2 * size
            state_diag[row : row + size, col : col + 2 * size] = pieces[i].astype(jnp.bfloat16)


def spread_right(right, right_diag, low):
    size = right.shape[0]
    for v in range(0, right.shape[1] // size, 2):
        pieces = halves(right[:, v * size : (v + 2) * size].astype(jnp.float32), low)
        for i in range(4):
            at = (2 * v + i) * size
            right_diag[at : at + size, :] = pieces[i].astype(jnp.bfloat16)


def spread_left(lefts, left_rows):
    cols = len(lefts)
    size = lefts[0].shape[0]
    half, share = size // 2, lefts[0].shape[1] // size
    mine = lax.axis_index("col")
    for other in range(cols):
        col = jnp.bitwise_xor(mine, other)
        for k in range(share):
            piece = lefts[other][:, k * size : (k + 1) * size].astype(jnp.float32)
            both = jnp.concatenate([piece[:half], piece[half:]], axis=1)
            left_rows[pl.ds(col * share + k, half, stride=cols * share), :] = both


def mix_block(states, left_rows, state_diag, mpo_ref, mixed):
    width = mpo_ref.shape[0] // states
    lanes = left_rows.shape[1]
    half = left_rows.shape[0] // width
    for start in range(0, half, CHUNK):
        taken = left_rows[start * width : (start + CHUNK) * width, :].astype(jnp.bfloat16)
        first = jnp.dot(taken, state_diag[...], preferred_element_type=jnp.float32)
        columns = []
        for x in range(CHUNK):
            one = first[x * width : (x + 1) * width, :]
            columns.append(
                jnp.concatenate(
                    [one[:, s * lanes : (s + 1) * lanes] for s in range(states)], axis=0
                ).astype(jnp.bfloat16)
            )
        gathered = jnp.concatenate(columns, axis=1)
        channels = jnp.dot(mpo_ref[...], gathered, preferred_element_type=jnp.float32).astype(jnp.bfloat16)
        for x in range(CHUNK):
            for v in range(width):
                mixed[(start + x) * states : (start + x + 1) * states, v * lanes : (v + 1) * lanes] = channels[
                    v * states : (v + 1) * states, x * lanes : (x + 1) * lanes
                ]


def finish_block(states, mixed, right_diag, result, outs, low):
    cols = len(outs)
    size = low.shape[0]
    half, per = size // 2, states // cols
    mine = lax.axis_index("col")
    result[...] = jnp.dot(mixed[...], right_diag[...], preferred_element_type=jnp.float32)
    low = low[:half]
    for other in range(cols):
        col = jnp.bitwise_xor(mine, other)
        for t in range(0, per, 2):
            one = result[pl.ds(col * per + t, half, stride=states), :]
            two = result[pl.ds(col * per + t + 1, half, stride=states), :]
            upper = jnp.where(low, one, pltpu.roll(two, size, 1))
            lower = jnp.where(low, pltpu.roll(one, size, 1), two)
            outs[other][:half, t * size : (t + 2) * size] = upper.astype(jnp.bfloat16)
            outs[other][half:, t * size : (t + 2) * size] = lower.astype(jnp.bfloat16)


def half_mask(size):
    return lax.broadcasted_iota(jnp.int32, (size, 2 * size), 1) < size


def prepare_kernel(states, order_ref, state_ref, mpo_ref, diag_ref, rows_ref, block, flat, sem):
    steps, size = block.shape[:2]
    width = mpo_ref.shape[0]
    low = half_mask(size)
    at = lax.axis_index("col") * steps
    copies = [
        pltpu.make_async_copy(state_ref.at[order_ref[at + k]], block.at[k], sem.at[k]) for k in range(steps)
    ]
    for copy in copies:
        copy.start()
    both = (states * states, states * states)
    row, col = lax.broadcasted_iota(jnp.int32, both, 0), lax.broadcasted_iota(jnp.int32, both, 1)
    turned = lax.rem(row, states) * states + lax.div(row, states)
    turn = jnp.where(turned == col, 1.0, 0.0).astype(jnp.bfloat16)
    split = flat.shape[0]
    for w in range(width):
        taken = mpo_ref[w].astype(jnp.float32)
        for i in range(split):
            flat[i, w * width : (w + 1) * width, :] = taken[:, i * 128 : (i + 1) * 128]
    taken = jnp.concatenate([flat[i] for i in range(split)], axis=1).astype(jnp.bfloat16)
    taken = jnp.dot(taken, turn, preferred_element_type=jnp.float32)
    for i in range(split):
        flat[i] = taken[:, i * 128 : (i + 1) * 128]

    def some_channels(j, carry):
        for v in range(4):
            taken = [jnp.transpose(flat[i, pl.ds(4 * j + v, width, stride=width), :]) for i in range(split)]
            taken = jnp.concatenate(taken, axis=0)
            line = jnp.concatenate([taken[s * states : (s + 1) * states, :] for s in range(states)], axis=1)
            rows_ref[pl.ds(pl.multiple_of((4 * j + v) * states, states), states), :] = line.astype(jnp.bfloat16)
        return carry

    lax.fori_loop(0, width // 4, some_channels, 0)
    for copy in copies:
        copy.wait()

    def one_block(k, carry):
        spread_state(block.at[k], diag_ref.at[k], low)
        return carry

    lax.fori_loop(0, steps, one_block, 0)


def prepare(order, state_blocks, mpo_tensor, cols, states):
    count, size = state_blocks.shape[:2]
    steps, width = count // cols, mpo_tensor.shape[0]
    return pl.pallas_call(
        functools.partial(prepare_kernel, states),
        out_shape=[
            jax.ShapeDtypeStruct((steps, 2 * size, 2 * states * size), jnp.bfloat16),
            jax.ShapeDtypeStruct((width * states, states * width), jnp.bfloat16),
        ],
        in_specs=[SMEM, ANY, VMEM],
        out_specs=[VMEM, VMEM],
        scratch_shapes=[
            pltpu.VMEM((steps, size, states * size), jnp.bfloat16),
            pltpu.VMEM((states * states // 128, width * width, 128), jnp.float32),
            pltpu.SemaphoreType.DMA((steps,)),
        ],
        compiler_params=pltpu.CompilerParams(vmem_limit_bytes=10 << 20),
        name="prepare",
    )(order, state_blocks, mpo_tensor)


def mix_kernel(states, cols, count, diag_ref, mpo_ref, *refs):
    lefts, mixed, left_rows = refs[:cols], refs[cols : cols + count], refs[-1]
    for k in range(count):
        spread_left([left.at[k] for left in lefts], left_rows.at[k])
    for k in range(count):
        mix_block(states, left_rows.at[k], diag_ref.at[k], mpo_ref, mixed[k])


def fetch_right(near, key_ref, order_ref, slot_ref, at, env_ref, rights, right_now):
    slot = lax.rem(slot_ref[at], near)
    apart = jnp.bitwise_xor(lax.div(slot_ref[at], near), lax.axis_index("row"))

    @pl.when(apart == 0)
    def _():
        right_now[...] = env_ref[sub_of(key_ref[order_ref[at]])]

    for other, right in enumerate(rights, 1):

        @pl.when(apart == other)
        def _():
            right_now[...] = right[slot]


def right_kernel(states, rows, cols, near, count, order_ref, slot_ref, key_ref, env_ref, *refs):
    rights, refs = refs[: rows - 1], refs[rows - 1 :]
    mixed, outs, (right_now, right_diag, result) = refs[:count], refs[count : count + cols], refs[count + cols :]
    low = half_mask(env_ref.shape[1])
    at = lax.axis_index("col") * (order_ref.shape[0] // cols)
    for k in range(count):
        fetch_right(near, key_ref, order_ref, slot_ref, at + k, env_ref, rights, right_now.at[k])
    for k in range(count):
        spread_right(right_now.at[k], right_diag.at[k], low)
    for k in range(count):
        finish_block(states, mixed[k], right_diag.at[k], result.at[k], [out.at[k] for out in outs], low)


def apply_kernel(
    states, rows, cols, near, first, count, order_ref, slot_ref, key_ref, env_ref, diag_ref, mpo_ref, early_ref, *refs
):
    rights, lefts, refs = refs[: rows - 1], refs[rows - 1 : rows - 1 + cols], refs[rows - 1 + cols :]
    outs, (left_rows, mixed, right_now, right_diag, result) = refs[:cols], refs[cols:]
    low = half_mask(env_ref.shape[1])
    at = lax.axis_index("col") * (order_ref.shape[0] // cols) + first
    for k in range(count):
        fetch_right(near, key_ref, order_ref, slot_ref, at + k, env_ref, rights, right_now.at[k])
    outs[1][:first] = early_ref[...]
    for k in range(count):
        spread_left([left.at[first + k] for left in lefts], left_rows.at[k])
        spread_right(right_now.at[k], right_diag.at[k], low)
    for k in range(count):
        mix_block(states, left_rows.at[k], diag_ref.at[first + k], mpo_ref, mixed.at[k])
        into = [out.at[first + k if d == 1 else k] for d, out in enumerate(outs)]
        finish_block(states, mixed.at[k], right_diag.at[k], result.at[k], into, low)


def cost_of(blocks, states, width, size, mix, right):
    flops = mix * (width * size * size * states * size + (width * states) ** 2 * size * size)
    flops = 2 * blocks * (flops + right * states * size * size * width * size)
    return pl.CostEstimate(flops=flops, bytes_accessed=4 << 20, transcendentals=0)


def first_blocks(count, order, slots, keys, state_diag, mpo_rows, right_env, rights, lefts, near):
    cols, rows = len(lefts), len(rights) + 1
    size, share = lefts[0].shape[1:]
    width = share // size * cols
    states = mpo_rows.shape[0] // width
    half, lanes = size // 2, 2 * size
    params = pltpu.CompilerParams(vmem_limit_bytes=24 << 20)
    mixed = pl.pallas_call(
        functools.partial(mix_kernel, states, cols, count),
        out_shape=[jax.ShapeDtypeStruct((half * states, width * lanes), jnp.bfloat16)] * count,
        in_specs=[VMEM] * (2 + cols),
        out_specs=[VMEM] * count,
        scratch_shapes=[pltpu.VMEM((count, half * width, lanes), jnp.float32)],
        compiler_params=params,
        cost_estimate=cost_of(count, states, width, size, 1, 0),
        name="mix",
    )(state_diag, mpo_rows, *lefts)
    return pl.pallas_call(
        functools.partial(right_kernel, states, rows, cols, near, count),
        out_shape=[jax.ShapeDtypeStruct((count, size, states // cols * size), jnp.bfloat16)] * cols,
        in_specs=[SMEM] * 3 + [VMEM] * (rows + count),
        out_specs=[VMEM] * cols,
        scratch_shapes=[
            pltpu.VMEM((count, size, width * size), jnp.bfloat16),
            pltpu.VMEM((count, width * lanes, lanes), jnp.bfloat16),
            pltpu.VMEM((count, half * states, lanes), jnp.float32),
        ],
        compiler_params=params,
        cost_estimate=cost_of(count, states, width, size, 0, 1),
        name="right",
    )(order, slots, keys, right_env, *rights, *mixed)


def last_blocks(order, slots, keys, state_diag, mpo_rows, right_env, rights, lefts, early, near):
    cols, rows = len(lefts), len(rights) + 1
    first, (steps, size, share) = early.shape[0], lefts[0].shape
    count = steps - first
    width = share // size * cols
    states = mpo_rows.shape[0] // width
    half, lanes = size // 2, 2 * size

    def out(blocks):
        return jax.ShapeDtypeStruct((blocks, size, states // cols * size), jnp.bfloat16)

    return pl.pallas_call(
        functools.partial(apply_kernel, states, rows, cols, near, first, count),
        out_shape=[out(steps if d == 1 else count) for d in range(cols)],
        in_specs=[SMEM] * 3 + [VMEM] * (4 + rows - 1 + cols),
        out_specs=[VMEM] * cols,
        scratch_shapes=[
            pltpu.VMEM((count, half * width, lanes), jnp.float32),
            pltpu.VMEM((count, half * states, width * lanes), jnp.bfloat16),
            pltpu.VMEM((count, size, width * size), jnp.bfloat16),
            pltpu.VMEM((count, width * lanes, lanes), jnp.bfloat16),
            pltpu.VMEM((count, half * states, lanes), jnp.float32),
        ],
        compiler_params=pltpu.CompilerParams(vmem_limit_bytes=24 << 20),
        cost_estimate=cost_of(count, states, width, size, 1, 1),
        name="apply",
    )(order, slots, keys, right_env, state_diag, mpo_rows, early, *rights, *lefts)


def place_kernel(cols, pieces, begun, order_ref, *refs):
    came = refs[begun : begun + len(pieces)]
    out_ref, sem = refs[begun + len(pieces) :]
    steps = order_ref.shape[0] // cols
    mine = lax.axis_index("col")
    copies = []
    for piece, (other, first) in zip(came, pieces):
        col = jnp.bitwise_xor(mine, other)
        for k in range(piece.shape[0]):
            p = order_ref[col * steps + first + k]
            copies.append(pltpu.make_async_copy(piece.at[k], out_ref.at[p], sem.at[len(copies)]))
    run_copies(copies)


def place_blocks(order, out, came, pieces, cols):
    begun = [] if out is None else [out]
    return pl.pallas_call(
        functools.partial(place_kernel, cols, pieces, len(begun)),
        out_shape=jax.ShapeDtypeStruct((order.shape[0],) + came[0].shape[1:], came[0].dtype),
        in_specs=[SMEM] + [HBM] * len(begun) + [VMEM] * len(came),
        out_specs=HBM,
        scratch_shapes=[pltpu.SemaphoreType.DMA((sum(piece.shape[0] for piece in came),))],
        input_output_aliases={1: 0} if begun else {},
        compiler_params=pltpu.CompilerParams(vmem_limit_bytes=4 << 20),
        name="place",
    )(order, *begun, *came)


def shards(state_blocks, left_env, right_env, mpo_tensor, block_left, block_owner, block_sub):
    rows = lax.axis_size("row")
    cols = lax.axis_size("col")
    count, size = state_blocks.shape[:2]
    states = state_blocks.shape[2] // size
    width = mpo_tensor.shape[0]
    most = max(2, (2 * count + rows - 1) // rows)
    near = -(-most // cols)

    half = count // cols // 2

    keys = jnp.bitwise_or(lax.shift_left(block_owner[:, 0], SHIFT), block_sub)
    others = [swap(keys, "row", step) for step in range(1, rows)]
    block_left, *others = lax.optimization_barrier((block_left, *others))
    sends, order, slots = route(block_left, keys, left_env, cols, near)
    lefts = [sends[0]] + [swap(sends[d], "col", d) for d in range(1, cols)]
    picked = pick(others, right_env, cols, near)
    mpo_tensor, *far = lax.optimization_barrier((mpo_tensor, *picked))
    state_diag, mpo_rows = prepare(order, state_blocks, mpo_tensor, cols, states)
    core_send, state_diag = lax.optimization_barrier((far[0], state_diag))
    rights = [swap(core_send, "row", 1)] + [swap(far[d - 1], "row", d) for d in range(2, rows)]
    early = first_blocks(half, order, slots, keys, state_diag, mpo_rows, right_env, rights, lefts, near)
    came = [swap(early[d], "col", d) for d in range(2, cols)]
    late = last_blocks(order, slots, keys, state_diag, mpo_rows, right_env, rights, lefts, early[1], near)
    joined = lax.optimization_barrier((*late[1:], *came))
    sent, came = joined[: cols - 1], joined[cols - 1 :]
    last = [swap(sent[d - 1], "col", d) for d in range(1, cols)]
    pieces = [(0, 0)] + [(d, 0) for d in range(2, cols)] + [(0, half)]
    out = place_blocks(order, None, [early[0], *came, late[0]], pieces, cols)
    pieces = [(1, 0)] + [(d, half) for d in range(2, cols)]
    return place_blocks(order, out, last, pieces, cols)


def solution(mesh):
    placed = (
        P(("groups", "row"), None, None),
        P(("groups", "row"), None, "col"),
        P(("groups", "row"), None, None),
        P(),
        P(("groups", "row")),
        P(("groups", "row"), None),
        P(("groups", "row")),
    )
    return jax.shard_map(
        shards,
        mesh=mesh,
        in_specs=placed,
        out_specs=P(("groups", "row"), None, "col"),
        check_vma=False,
    )
```

```python
import functools

import jax
import jax.numpy as jnp
from jax import lax
from jax.experimental import pallas as pl
from jax.experimental.pallas import tpu as pltpu
from jax.sharding import PartitionSpec as P

CHUNK = 16
SHIFT = 16
SMEM = pl.BlockSpec(memory_space=pltpu.SMEM)
VMEM = pl.BlockSpec(memory_space=pltpu.VMEM)
HBM = pl.BlockSpec(memory_space=pltpu.HBM)
ANY = pl.BlockSpec(memory_space=pl.ANY)


def swap(array, axis, step):
    size = lax.axis_size(axis)
    return lax.ppermute(array, axis, [(i, i ^ step) for i in range(size)])


def run_copies(copies):
    for copy in copies:
        copy.start()
    for copy in copies:
        copy.wait()


def owner_of(key):
    return lax.shift_right_logical(key, SHIFT)


def sub_of(key):
    return jnp.bitwise_and(key, (1 << SHIFT) - 1)


def route_kernel(cols, near, left_ref, key_ref, env_ref, *refs):
    sends = refs[:cols]
    order_ref, slot_ref, by_place = refs[cols:]
    count = left_ref.shape[0]
    steps = count // cols
    mine = lax.axis_index("col")
    owners = [owner_of(key_ref[p]) for p in range(count)]
    for p in range(count):
        place = jnp.int32(0)
        for other in range(count):
            if other < p:
                place = place + (owners[other] <= owners[p]).astype(jnp.int32)
            elif other > p:
                place = place + (owners[other] < owners[p]).astype(jnp.int32)
        by_place[place] = p
    for col in range(cols):
        before = None
        for step in range(steps):
            p = by_place[step * cols + col]
            owner = owner_of(key_ref[p])
            if before is None:
                slot = jnp.int32(0)
            else:
                slot = jnp.where(owner == before[0], before[1] + 1, 0)
            before = owner, slot
            order_ref[col * steps + step] = p
            slot_ref[col * steps + step] = owner * near + slot
    for other in range(cols):
        col = jnp.bitwise_xor(mine, other)
        for step in range(steps):
            p = order_ref[col * steps + step]
            sends[other][step] = env_ref[left_ref[p]]


def route(block_left, keys, left_env, cols, near):
    count = block_left.shape[0]
    size, width = left_env.shape[1:]
    piece = jax.ShapeDtypeStruct((count // cols, size, width), left_env.dtype)
    listed = jax.ShapeDtypeStruct((count,), jnp.int32)
    *sends, order, slots = pl.pallas_call(
        functools.partial(route_kernel, cols, near),
        out_shape=(piece,) * cols + (listed, listed),
        in_specs=[SMEM, SMEM, VMEM],
        out_specs=(VMEM,) * cols + (SMEM, SMEM),
        scratch_shapes=[pltpu.SMEM((count,), jnp.int32)],
        name="route",
    )(block_left, keys, left_env)
    return sends, order, slots


def pick_kernel(rows, cols, near, *refs):
    key_refs = refs[: rows - 1]
    env_ref = refs[rows - 1]
    sends = refs[rows:]
    count = key_refs[0].shape[0]
    me = lax.axis_index("row")
    mine = lax.axis_index("col")
    for other in range(rows - 1):
        keys = [key_refs[other][p] for p in range(count)]
        owners = [owner_of(key) for key in keys]
        first = jnp.int32(0)
        for p in range(count):
            first = first + (owners[p] < me).astype(jnp.int32)
        past = -lax.rem(mine - lax.rem(first, cols) + cols, cols)
        wanted = [jnp.int32(0)] * near
        for p in range(count):
            here = owners[p] == me
            for slot in range(near):
                wanted[slot] = jnp.where(here & (past == slot * cols), sub_of(keys[p]), wanted[slot])
            past = past + here.astype(jnp.int32)
        for slot in range(near):
            sends[other][slot] = env_ref[wanted[slot]]


def pick(keys, right_env, cols, near):
    rows = len(keys) + 1
    piece = jax.ShapeDtypeStruct((near,) + right_env.shape[1:], right_env.dtype)
    return pl.pallas_call(
        functools.partial(pick_kernel, rows, cols, near),
        out_shape=[piece] * (rows - 1),
        in_specs=[SMEM] * (rows - 1) + [VMEM],
        out_specs=(VMEM,) * (rows - 1),
        name="pick",
    )(*keys, right_env)


def halves(tile, low):
    swapped = pltpu.roll(tile, tile.shape[1] // 2, 1)
    zero = jnp.zeros_like(tile)
    return (
        jnp.where(low, tile, zero),
        jnp.where(low, zero, swapped),
        jnp.where(low, swapped, zero),
        jnp.where(low, zero, tile),
    )


def spread_state(block, state_diag, low):
    size = block.shape[0]
    for s in range(0, block.shape[1] // size, 2):
        pieces = halves(block[:, s * size : (s + 2) * size].astype(jnp.float32), low)
        for i in range(4):
            row, col = (i % 2) * size, (s + i // 2) * 2 * size
            state_diag[row : row + size, col : col + 2 * size] = pieces[i].astype(jnp.bfloat16)


def spread_right(right, right_diag, low):
    size = right.shape[0]
    for v in range(0, right.shape[1] // size, 2):
        pieces = halves(right[:, v * size : (v + 2) * size].astype(jnp.float32), low)
        for i in range(4):
            at = (2 * v + i) * size
            right_diag[at : at + size, :] = pieces[i].astype(jnp.bfloat16)


def spread_left(lefts, left_rows):
    cols = len(lefts)
    size = lefts[0].shape[0]
    half, share = size // 2, lefts[0].shape[1] // size
    mine = lax.axis_index("col")
    for other in range(cols):
        col = jnp.bitwise_xor(mine, other)
        for k in range(share):
            piece = lefts[other][:, k * size : (k + 1) * size].astype(jnp.float32)
            both = jnp.concatenate([piece[:half], piece[half:]], axis=1)
            left_rows[pl.ds(col * share + k, half, stride=cols * share), :] = both


def mix_block(states, left_rows, state_diag, mpo_ref, mixed):
    width = mpo_ref.shape[0] // states
    lanes = left_rows.shape[1]
    half = left_rows.shape[0] // width
    for start in range(0, half, CHUNK):
        taken = left_rows[start * width : (start + CHUNK) * width, :].astype(jnp.bfloat16)
        first = jnp.dot(taken, state_diag[...], preferred_element_type=jnp.float32)
        columns = []
        for x in range(CHUNK):
            one = first[x * width : (x + 1) * width, :]
            columns.append(
                jnp.concatenate(
                    [one[:, s * lanes : (s + 1) * lanes] for s in range(states)], axis=0
                ).astype(jnp.bfloat16)
            )
        gathered = jnp.concatenate(columns, axis=1)
        channels = jnp.dot(mpo_ref[...], gathered, preferred_element_type=jnp.float32).astype(jnp.bfloat16)
        for x in range(CHUNK):
            for v in range(width):
                mixed[(start + x) * states : (start + x + 1) * states, v * lanes : (v + 1) * lanes] = channels[
                    v * states : (v + 1) * states, x * lanes : (x + 1) * lanes
                ]


def finish_block(states, mixed, right_diag, result, outs, low):
    cols = len(outs)
    size = low.shape[0]
    half, per = size // 2, states // cols
    mine = lax.axis_index("col")
    result[...] = jnp.dot(mixed[...], right_diag[...], preferred_element_type=jnp.float32)
    low = low[:half]
    for other in range(cols):
        col = jnp.bitwise_xor(mine, other)
        for t in range(0, per, 2):
            one = result[pl.ds(col * per + t, half, stride=states), :]
            two = result[pl.ds(col * per + t + 1, half, stride=states), :]
            upper = jnp.where(low, one, pltpu.roll(two, size, 1))
            lower = jnp.where(low, pltpu.roll(one, size, 1), two)
            outs[other][:half, t * size : (t + 2) * size] = upper.astype(jnp.bfloat16)
            outs[other][half:, t * size : (t + 2) * size] = lower.astype(jnp.bfloat16)


def half_mask(size):
    return lax.broadcasted_iota(jnp.int32, (size, 2 * size), 1) < size


def prepare_kernel(states, order_ref, state_ref, mpo_ref, diag_ref, rows_ref, block, flat, sem):
    steps, size = block.shape[:2]
    width = mpo_ref.shape[0]
    low = half_mask(size)
    at = lax.axis_index("col") * steps
    copies = [
        pltpu.make_async_copy(state_ref.at[order_ref[at + k]], block.at[k], sem.at[k]) for k in range(steps)
    ]
    for copy in copies:
        copy.start()
    both = (states * states, states * states)
    row, col = lax.broadcasted_iota(jnp.int32, both, 0), lax.broadcasted_iota(jnp.int32, both, 1)
    turned = lax.rem(row, states) * states + lax.div(row, states)
    turn = jnp.where(turned == col, 1.0, 0.0).astype(jnp.bfloat16)
    split = flat.shape[0]
    for w in range(width):
        taken = mpo_ref[w].astype(jnp.float32)
        for i in range(split):
            flat[i, w * width : (w + 1) * width, :] = taken[:, i * 128 : (i + 1) * 128]
    taken = jnp.concatenate([flat[i] for i in range(split)], axis=1).astype(jnp.bfloat16)
    taken = jnp.dot(taken, turn, preferred_element_type=jnp.float32)
    for i in range(split):
        flat[i] = taken[:, i * 128 : (i + 1) * 128]

    def some_channels(j, carry):
        for v in range(4):
            taken = [jnp.transpose(flat[i, pl.ds(4 * j + v, width, stride=width), :]) for i in range(split)]
            taken = jnp.concatenate(taken, axis=0)
            line = jnp.concatenate([taken[s * states : (s + 1) * states, :] for s in range(states)], axis=1)
            rows_ref[pl.ds(pl.multiple_of((4 * j + v) * states, states), states), :] = line.astype(jnp.bfloat16)
        return carry

    lax.fori_loop(0, width // 4, some_channels, 0)
    for copy in copies:
        copy.wait()

    def one_block(k, carry):
        spread_state(block.at[k], diag_ref.at[k], low)
        return carry

    lax.fori_loop(0, steps, one_block, 0)


def prepare(order, state_blocks, mpo_tensor, cols, states):
    count, size = state_blocks.shape[:2]
    steps, width = count // cols, mpo_tensor.shape[0]
    return pl.pallas_call(
        functools.partial(prepare_kernel, states),
        out_shape=[
            jax.ShapeDtypeStruct((steps, 2 * size, 2 * states * size), jnp.bfloat16),
            jax.ShapeDtypeStruct((width * states, states * width), jnp.bfloat16),
        ],
        in_specs=[SMEM, ANY, VMEM],
        out_specs=[VMEM, VMEM],
        scratch_shapes=[
            pltpu.VMEM((steps, size, states * size), jnp.bfloat16),
            pltpu.VMEM((states * states // 128, width * width, 128), jnp.float32),
            pltpu.SemaphoreType.DMA((steps,)),
        ],
        compiler_params=pltpu.CompilerParams(vmem_limit_bytes=10 << 20),
        cost_estimate=pl.CostEstimate(flops=0, bytes_accessed=0, transcendentals=0),
        name="prepare",
    )(order, state_blocks, mpo_tensor)


def mix_kernel(states, cols, count, diag_ref, mpo_ref, *refs):
    lefts, mixed, left_rows = refs[:cols], refs[cols : cols + count], refs[-1]
    for k in range(count):
        spread_left([left.at[k] for left in lefts], left_rows.at[k])
    for k in range(count):
        mix_block(states, left_rows.at[k], diag_ref.at[k], mpo_ref, mixed[k])


def fetch_right(near, key_ref, order_ref, slot_ref, at, env_ref, rights, right_now):
    slot = lax.rem(slot_ref[at], near)
    apart = jnp.bitwise_xor(lax.div(slot_ref[at], near), lax.axis_index("row"))

    @pl.when(apart == 0)
    def _():
        right_now[...] = env_ref[sub_of(key_ref[order_ref[at]])]

    for other, right in enumerate(rights, 1):

        @pl.when(apart == other)
        def _():
            right_now[...] = right[slot]


def right_kernel(states, rows, cols, near, count, order_ref, slot_ref, key_ref, env_ref, *refs):
    rights, refs = refs[: rows - 1], refs[rows - 1 :]
    mixed, outs, (right_now, right_diag, result) = refs[:count], refs[count : count + cols], refs[count + cols :]
    low = half_mask(env_ref.shape[1])
    at = lax.axis_index("col") * (order_ref.shape[0] // cols)
    for k in range(count):
        fetch_right(near, key_ref, order_ref, slot_ref, at + k, env_ref, rights, right_now.at[k])
    for k in range(count):
        spread_right(right_now.at[k], right_diag.at[k], low)
    for k in range(count):
        finish_block(states, mixed[k], right_diag.at[k], result.at[k], [out.at[k] for out in outs], low)


def apply_kernel(
    states, rows, cols, near, first, count, order_ref, slot_ref, key_ref, env_ref, diag_ref, mpo_ref, early_ref, *refs
):
    rights, lefts, refs = refs[: rows - 1], refs[rows - 1 : rows - 1 + cols], refs[rows - 1 + cols :]
    outs, (left_rows, mixed, right_now, right_diag, result) = refs[:cols], refs[cols:]
    low = half_mask(env_ref.shape[1])
    at = lax.axis_index("col") * (order_ref.shape[0] // cols) + first
    for k in range(count):
        spread_left([left.at[first + k] for left in lefts], left_rows.at[k])
    for k in range(count):
        mix_block(states, left_rows.at[k], diag_ref.at[first + k], mpo_ref, mixed.at[k])
    outs[1][:first] = early_ref[...]
    for k in range(count):
        fetch_right(near, key_ref, order_ref, slot_ref, at + k, env_ref, rights, right_now.at[k])
    for k in range(count):
        spread_right(right_now.at[k], right_diag.at[k], low)
    for k in range(count):
        into = [out.at[first + k if d == 1 else k] for d, out in enumerate(outs)]
        finish_block(states, mixed.at[k], right_diag.at[k], result.at[k], into, low)


def cost_of(blocks, states, width, size, mix, right):
    flops = mix * (width * size * size * states * size + (width * states) ** 2 * size * size)
    flops = 2 * blocks * (flops + right * states * size * size * width * size)
    return pl.CostEstimate(flops=flops, bytes_accessed=4 << 20, transcendentals=0)


def first_blocks(count, order, slots, keys, state_diag, mpo_rows, right_env, rights, lefts, near):
    cols, rows = len(lefts), len(rights) + 1
    size, share = lefts[0].shape[1:]
    width = share // size * cols
    states = mpo_rows.shape[0] // width
    half, lanes = size // 2, 2 * size
    params = pltpu.CompilerParams(vmem_limit_bytes=24 << 20)
    mixed = pl.pallas_call(
        functools.partial(mix_kernel, states, cols, count),
        out_shape=[jax.ShapeDtypeStruct((half * states, width * lanes), jnp.bfloat16)] * count,
        in_specs=[VMEM] * (2 + cols),
        out_specs=[VMEM] * count,
        scratch_shapes=[pltpu.VMEM((count, half * width, lanes), jnp.float32)],
        compiler_params=params,
        cost_estimate=cost_of(count, states, width, size, 1, 0),
        name="mix",
    )(state_diag, mpo_rows, *lefts)
    return pl.pallas_call(
        functools.partial(right_kernel, states, rows, cols, near, count),
        out_shape=[jax.ShapeDtypeStruct((count, size, states // cols * size), jnp.bfloat16)] * cols,
        in_specs=[SMEM] * 3 + [VMEM] * (rows + count),
        out_specs=[VMEM] * cols,
        scratch_shapes=[
            pltpu.VMEM((count, size, width * size), jnp.bfloat16),
            pltpu.VMEM((count, width * lanes, lanes), jnp.bfloat16),
            pltpu.VMEM((count, half * states, lanes), jnp.float32),
        ],
        compiler_params=params,
        cost_estimate=cost_of(count, states, width, size, 0, 1),
        name="right",
    )(order, slots, keys, right_env, *rights, *mixed)


def last_blocks(order, slots, keys, state_diag, mpo_rows, right_env, rights, lefts, early, near):
    cols, rows = len(lefts), len(rights) + 1
    first, (steps, size, share) = early.shape[0], lefts[0].shape
    count = steps - first
    width = share // size * cols
    states = mpo_rows.shape[0] // width
    half, lanes = size // 2, 2 * size

    def out(blocks):
        return jax.ShapeDtypeStruct((blocks, size, states // cols * size), jnp.bfloat16)

    return pl.pallas_call(
        functools.partial(apply_kernel, states, rows, cols, near, first, count),
        out_shape=[out(steps if d == 1 else count) for d in range(cols)],
        in_specs=[SMEM] * 3 + [VMEM] * (4 + rows - 1 + cols),
        out_specs=[VMEM] * cols,
        scratch_shapes=[
            pltpu.VMEM((count, half * width, lanes), jnp.float32),
            pltpu.VMEM((count, half * states, width * lanes), jnp.bfloat16),
            pltpu.VMEM((count, size, width * size), jnp.bfloat16),
            pltpu.VMEM((count, width * lanes, lanes), jnp.bfloat16),
            pltpu.VMEM((count, half * states, lanes), jnp.float32),
        ],
        compiler_params=pltpu.CompilerParams(vmem_limit_bytes=24 << 20),
        cost_estimate=cost_of(count, states, width, size, 1, 1),
        name="apply",
    )(order, slots, keys, right_env, state_diag, mpo_rows, early, *rights, *lefts)


def place_kernel(cols, pieces, begun, order_ref, *refs):
    came = refs[begun : begun + len(pieces)]
    out_ref, sem = refs[begun + len(pieces) :]
    steps = order_ref.shape[0] // cols
    mine = lax.axis_index("col")
    copies = []
    for piece, (other, first) in zip(came, pieces):
        col = jnp.bitwise_xor(mine, other)
        for k in range(piece.shape[0]):
            p = order_ref[col * steps + first + k]
            copies.append(pltpu.make_async_copy(piece.at[k], out_ref.at[p], sem.at[len(copies)]))
    run_copies(copies)


def place_blocks(order, out, came, pieces, cols):
    begun = [] if out is None else [out]
    return pl.pallas_call(
        functools.partial(place_kernel, cols, pieces, len(begun)),
        out_shape=jax.ShapeDtypeStruct((order.shape[0],) + came[0].shape[1:], came[0].dtype),
        in_specs=[SMEM] + [HBM] * len(begun) + [VMEM] * len(came),
        out_specs=HBM,
        scratch_shapes=[pltpu.SemaphoreType.DMA((sum(piece.shape[0] for piece in came),))],
        input_output_aliases={1: 0} if begun else {},
        compiler_params=pltpu.CompilerParams(vmem_limit_bytes=4 << 20),
        name="place",
    )(order, *begun, *came)


def shards(state_blocks, left_env, right_env, mpo_tensor, block_left, block_owner, block_sub):
    rows = lax.axis_size("row")
    cols = lax.axis_size("col")
    count, size = state_blocks.shape[:2]
    states = state_blocks.shape[2] // size
    width = mpo_tensor.shape[0]
    most = max(2, (2 * count + rows - 1) // rows)
    near = -(-most // cols)

    half = count // cols // 2

    keys = jnp.bitwise_or(lax.shift_left(block_owner[:, 0], SHIFT), block_sub)
    others = [swap(keys, "row", step) for step in range(1, rows)]
    sends, order, slots = route(block_left, keys, left_env, cols, near)
    picked = pick(others, right_env, cols, near)
    near_send, mpo_tensor, *far = lax.optimization_barrier((sends[1], mpo_tensor, *picked))
    lefts = [sends[0], swap(near_send, "col", 1)] + [swap(sends[d], "col", d) for d in range(2, cols)]
    state_diag, mpo_rows = prepare(order, state_blocks, mpo_tensor, cols, states)
    core_send, state_diag, *lefts[1:] = lax.optimization_barrier((far[0], state_diag, *lefts[1:]))
    rights = [swap(core_send, "row", 1)] + [swap(far[d - 1], "row", d) for d in range(2, rows)]
    early = first_blocks(half, order, slots, keys, state_diag, mpo_rows, right_env, rights, lefts, near)
    came = [swap(early[d], "col", d) for d in range(2, cols)]
    late = last_blocks(order, slots, keys, state_diag, mpo_rows, right_env, rights, lefts, early[1], near)
    joined = lax.optimization_barrier((*late[1:], *came))
    sent, came = joined[: cols - 1], joined[cols - 1 :]
    last = [swap(sent[d - 1], "col", d) for d in range(1, cols)]
    pieces = [(0, 0)] + [(d, 0) for d in range(2, cols)] + [(0, half)]
    out = place_blocks(order, None, [early[0], *came, late[0]], pieces, cols)
    pieces = [(1, 0)] + [(d, half) for d in range(2, cols)]
    return place_blocks(order, out, last, pieces, cols)


def solution(mesh):
    placed = (
        P(("groups", "row"), None, None),
        P(("groups", "row"), None, "col"),
        P(("groups", "row"), None, None),
        P(),
        P(("groups", "row")),
        P(("groups", "row"), None),
        P(("groups", "row")),
    )
    return jax.shard_map(
        shards,
        mesh=mesh,
        in_specs=placed,
        out_specs=P(("groups", "row"), None, "col"),
        check_vma=False,
    )
```

```python
import functools

import jax
import jax.numpy as jnp
from jax import lax
from jax.experimental import pallas as pl
from jax.experimental.pallas import tpu as pltpu
from jax.sharding import PartitionSpec as P

CHUNK = 16
SHIFT = 16
SMEM = pl.BlockSpec(memory_space=pltpu.SMEM)
VMEM = pl.BlockSpec(memory_space=pltpu.VMEM)
HBM = pl.BlockSpec(memory_space=pltpu.HBM)
ANY = pl.BlockSpec(memory_space=pl.ANY)


def swap(array, axis, step):
    size = lax.axis_size(axis)
    return lax.ppermute(array, axis, [(i, i ^ step) for i in range(size)])


def run_copies(copies):
    for copy in copies:
        copy.start()
    for copy in copies:
        copy.wait()


def owner_of(key):
    return lax.shift_right_logical(key, SHIFT)


def sub_of(key):
    return jnp.bitwise_and(key, (1 << SHIFT) - 1)


def route_kernel(cols, near, left_ref, key_ref, env_ref, *refs):
    sends = refs[:cols]
    order_ref, slot_ref, by_place = refs[cols:]
    count = left_ref.shape[0]
    steps = count // cols
    mine = lax.axis_index("col")
    owners = [owner_of(key_ref[p]) for p in range(count)]
    for p in range(count):
        place = jnp.int32(0)
        for other in range(count):
            if other < p:
                place = place + (owners[other] <= owners[p]).astype(jnp.int32)
            elif other > p:
                place = place + (owners[other] < owners[p]).astype(jnp.int32)
        by_place[place] = p
    for col in range(cols):
        before = None
        for step in range(steps):
            p = by_place[step * cols + col]
            owner = owner_of(key_ref[p])
            if before is None:
                slot = jnp.int32(0)
            else:
                slot = jnp.where(owner == before[0], before[1] + 1, 0)
            before = owner, slot
            order_ref[col * steps + step] = p
            slot_ref[col * steps + step] = owner * near + slot
    for other in range(cols):
        col = jnp.bitwise_xor(mine, other)
        for step in range(steps):
            p = order_ref[col * steps + step]
            sends[other][step] = env_ref[left_ref[p]]


def route(block_left, keys, left_env, cols, near):
    count = block_left.shape[0]
    size, width = left_env.shape[1:]
    piece = jax.ShapeDtypeStruct((count // cols, size, width), left_env.dtype)
    listed = jax.ShapeDtypeStruct((count,), jnp.int32)
    *sends, order, slots = pl.pallas_call(
        functools.partial(route_kernel, cols, near),
        out_shape=(piece,) * cols + (listed, listed),
        in_specs=[SMEM, SMEM, VMEM],
        out_specs=(VMEM,) * cols + (SMEM, SMEM),
        scratch_shapes=[pltpu.SMEM((count,), jnp.int32)],
        name="route",
    )(block_left, keys, left_env)
    return sends, order, slots


def pick_kernel(rows, cols, near, *refs):
    key_refs = refs[: rows - 1]
    env_ref = refs[rows - 1]
    sends = refs[rows:]
    count = key_refs[0].shape[0]
    me = lax.axis_index("row")
    mine = lax.axis_index("col")
    for other in range(rows - 1):
        keys = [key_refs[other][p] for p in range(count)]
        owners = [owner_of(key) for key in keys]
        first = jnp.int32(0)
        for p in range(count):
            first = first + (owners[p] < me).astype(jnp.int32)
        past = -lax.rem(mine - lax.rem(first, cols) + cols, cols)
        wanted = [jnp.int32(0)] * near
        for p in range(count):
            here = owners[p] == me
            for slot in range(near):
                wanted[slot] = jnp.where(here & (past == slot * cols), sub_of(keys[p]), wanted[slot])
            past = past + here.astype(jnp.int32)
        for slot in range(near):
            sends[other][slot] = env_ref[wanted[slot]]


def pick(keys, right_env, cols, near):
    rows = len(keys) + 1
    piece = jax.ShapeDtypeStruct((near,) + right_env.shape[1:], right_env.dtype)
    return pl.pallas_call(
        functools.partial(pick_kernel, rows, cols, near),
        out_shape=[piece] * (rows - 1),
        in_specs=[SMEM] * (rows - 1) + [VMEM],
        out_specs=(VMEM,) * (rows - 1),
        name="pick",
    )(*keys, right_env)


def halves(tile, low):
    swapped = pltpu.roll(tile, tile.shape[1] // 2, 1)
    zero = jnp.zeros_like(tile)
    return (
        jnp.where(low, tile, zero),
        jnp.where(low, zero, swapped),
        jnp.where(low, swapped, zero),
        jnp.where(low, zero, tile),
    )


def spread_state(block, state_diag, low):
    size = block.shape[0]
    for s in range(0, block.shape[1] // size, 2):
        pieces = halves(block[:, s * size : (s + 2) * size].astype(jnp.float32), low)
        for i in range(4):
            row, col = (i % 2) * size, (s + i // 2) * 2 * size
            state_diag[row : row + size, col : col + 2 * size] = pieces[i].astype(jnp.bfloat16)


def spread_right(right, right_diag, low):
    size = right.shape[0]
    for v in range(0, right.shape[1] // size, 2):
        pieces = halves(right[:, v * size : (v + 2) * size].astype(jnp.float32), low)
        for i in range(4):
            at = (2 * v + i) * size
            right_diag[at : at + size, :] = pieces[i].astype(jnp.bfloat16)


def spread_left(lefts, left_rows):
    cols = len(lefts)
    size = lefts[0].shape[0]
    half, share = size // 2, lefts[0].shape[1] // size
    mine = lax.axis_index("col")
    for other in range(cols):
        col = jnp.bitwise_xor(mine, other)
        for k in range(share):
            piece = lefts[other][:, k * size : (k + 1) * size].astype(jnp.float32)
            both = jnp.concatenate([piece[:half], piece[half:]], axis=1)
            left_rows[pl.ds(col * share + k, half, stride=cols * share), :] = both


def mix_block(states, left_rows, state_diag, mpo_ref, mixed):
    width = mpo_ref.shape[0] // states
    lanes = left_rows.shape[1]
    half = left_rows.shape[0] // width
    for start in range(0, half, CHUNK):
        taken = left_rows[start * width : (start + CHUNK) * width, :].astype(jnp.bfloat16)
        first = jnp.dot(taken, state_diag[...], preferred_element_type=jnp.float32)
        columns = []
        for x in range(CHUNK):
            one = first[x * width : (x + 1) * width, :]
            columns.append(
                jnp.concatenate(
                    [one[:, s * lanes : (s + 1) * lanes] for s in range(states)], axis=0
                ).astype(jnp.bfloat16)
            )
        gathered = jnp.concatenate(columns, axis=1)
        channels = jnp.dot(mpo_ref[...], gathered, preferred_element_type=jnp.float32).astype(jnp.bfloat16)
        for x in range(CHUNK):
            for v in range(width):
                mixed[(start + x) * states : (start + x + 1) * states, v * lanes : (v + 1) * lanes] = channels[
                    v * states : (v + 1) * states, x * lanes : (x + 1) * lanes
                ]


def finish_block(states, mixed, right_diag, result, outs, low):
    cols = len(outs)
    size = low.shape[0]
    half, per = size // 2, states // cols
    mine = lax.axis_index("col")
    result[...] = jnp.dot(mixed[...], right_diag[...], preferred_element_type=jnp.float32)
    low = low[:half]
    for other in range(cols):
        col = jnp.bitwise_xor(mine, other)
        for t in range(0, per, 2):
            one = result[pl.ds(col * per + t, half, stride=states), :]
            two = result[pl.ds(col * per + t + 1, half, stride=states), :]
            upper = jnp.where(low, one, pltpu.roll(two, size, 1))
            lower = jnp.where(low, pltpu.roll(one, size, 1), two)
            outs[other][:half, t * size : (t + 2) * size] = upper.astype(jnp.bfloat16)
            outs[other][half:, t * size : (t + 2) * size] = lower.astype(jnp.bfloat16)


def half_mask(size):
    return lax.broadcasted_iota(jnp.int32, (size, 2 * size), 1) < size


def prepare_kernel(states, order_ref, state_ref, mpo_ref, diag_ref, rows_ref, block, flat, sem):
    steps, size = block.shape[:2]
    width = mpo_ref.shape[0]
    low = half_mask(size)
    at = lax.axis_index("col") * steps
    copies = [
        pltpu.make_async_copy(state_ref.at[order_ref[at + k]], block.at[k], sem.at[k]) for k in range(steps)
    ]
    for copy in copies:
        copy.start()
    both = (states * states, states * states)
    row, col = lax.broadcasted_iota(jnp.int32, both, 0), lax.broadcasted_iota(jnp.int32, both, 1)
    turned = lax.rem(row, states) * states + lax.div(row, states)
    turn = jnp.where(turned == col, 1.0, 0.0).astype(jnp.bfloat16)
    split = flat.shape[0]
    for w in range(width):
        taken = mpo_ref[w].astype(jnp.float32)
        for i in range(split):
            flat[i, w * width : (w + 1) * width, :] = taken[:, i * 128 : (i + 1) * 128]
    taken = jnp.concatenate([flat[i] for i in range(split)], axis=1).astype(jnp.bfloat16)
    taken = jnp.dot(taken, turn, preferred_element_type=jnp.float32)
    for i in range(split):
        flat[i] = taken[:, i * 128 : (i + 1) * 128]

    def some_channels(j, carry):
        for v in range(4):
            taken = [jnp.transpose(flat[i, pl.ds(4 * j + v, width, stride=width), :]) for i in range(split)]
            taken = jnp.concatenate(taken, axis=0)
            line = jnp.concatenate([taken[s * states : (s + 1) * states, :] for s in range(states)], axis=1)
            rows_ref[pl.ds(pl.multiple_of((4 * j + v) * states, states), states), :] = line.astype(jnp.bfloat16)
        return carry

    lax.fori_loop(0, width // 4, some_channels, 0)
    for copy in copies:
        copy.wait()

    def one_block(k, carry):
        spread_state(block.at[k], diag_ref.at[k], low)
        return carry

    lax.fori_loop(0, steps, one_block, 0)


def prepare(order, state_blocks, mpo_tensor, cols, states):
    count, size = state_blocks.shape[:2]
    steps, width = count // cols, mpo_tensor.shape[0]
    return pl.pallas_call(
        functools.partial(prepare_kernel, states),
        out_shape=[
            jax.ShapeDtypeStruct((steps, 2 * size, 2 * states * size), jnp.bfloat16),
            jax.ShapeDtypeStruct((width * states, states * width), jnp.bfloat16),
        ],
        in_specs=[SMEM, ANY, VMEM],
        out_specs=[VMEM, VMEM],
        scratch_shapes=[
            pltpu.VMEM((steps, size, states * size), jnp.bfloat16),
            pltpu.VMEM((states * states // 128, width * width, 128), jnp.float32),
            pltpu.SemaphoreType.DMA((steps,)),
        ],
        compiler_params=pltpu.CompilerParams(vmem_limit_bytes=10 << 20),
        cost_estimate=pl.CostEstimate(flops=0, bytes_accessed=0, transcendentals=0),
        name="prepare",
    )(order, state_blocks, mpo_tensor)


def mix_kernel(states, cols, count, diag_ref, mpo_ref, *refs):
    lefts, mixed, left_rows = refs[:cols], refs[cols : cols + count], refs[-1]
    for k in range(count):
        spread_left([left.at[k] for left in lefts], left_rows.at[k])
    for k in range(count):
        mix_block(states, left_rows.at[k], diag_ref.at[k], mpo_ref, mixed[k])


def fetch_right(near, key_ref, order_ref, slot_ref, at, env_ref, rights, right_now):
    slot = lax.rem(slot_ref[at], near)
    apart = jnp.bitwise_xor(lax.div(slot_ref[at], near), lax.axis_index("row"))

    @pl.when(apart == 0)
    def _():
        right_now[...] = env_ref[sub_of(key_ref[order_ref[at]])]

    for other, right in enumerate(rights, 1):

        @pl.when(apart == other)
        def _():
            right_now[...] = right[slot]


def right_kernel(states, rows, cols, near, count, order_ref, slot_ref, key_ref, env_ref, *refs):
    rights, refs = refs[: rows - 1], refs[rows - 1 :]
    mixed, outs, (right_now, right_diag, result) = refs[:count], refs[count : count + cols], refs[count + cols :]
    low = half_mask(env_ref.shape[1])
    at = lax.axis_index("col") * (order_ref.shape[0] // cols)
    for k in range(count):
        fetch_right(near, key_ref, order_ref, slot_ref, at + k, env_ref, rights, right_now.at[k])
    for k in range(count):
        spread_right(right_now.at[k], right_diag.at[k], low)
    for k in range(count):
        finish_block(states, mixed[k], right_diag.at[k], result.at[k], [out.at[k] for out in outs], low)


def apply_kernel(
    states, rows, cols, near, first, count, order_ref, slot_ref, key_ref, env_ref, diag_ref, mpo_ref, early_ref, *refs
):
    rights, lefts, refs = refs[: rows - 1], refs[rows - 1 : rows - 1 + cols], refs[rows - 1 + cols :]
    outs, (left_rows, mixed, right_now, right_diag, result) = refs[:cols], refs[cols:]
    low = half_mask(env_ref.shape[1])
    at = lax.axis_index("col") * (order_ref.shape[0] // cols) + first
    for k in range(count):
        spread_left([left.at[first + k] for left in lefts], left_rows.at[k])
    for k in range(count):
        mix_block(states, left_rows.at[k], diag_ref.at[first + k], mpo_ref, mixed.at[k])
    outs[1][:first] = early_ref[...]
    for k in range(count):
        fetch_right(near, key_ref, order_ref, slot_ref, at + k, env_ref, rights, right_now.at[k])
    for k in range(count):
        spread_right(right_now.at[k], right_diag.at[k], low)
    for k in range(count):
        into = [out.at[first + k if d == 1 else k] for d, out in enumerate(outs)]
        finish_block(states, mixed.at[k], right_diag.at[k], result.at[k], into, low)


def cost_of(blocks, states, width, size, mix, right):
    flops = mix * (width * size * size * states * size + (width * states) ** 2 * size * size)
    flops = 2 * blocks * (flops + right * states * size * size * width * size)
    return pl.CostEstimate(flops=flops, bytes_accessed=4 << 20, transcendentals=0)


def first_blocks(count, order, slots, keys, state_diag, mpo_rows, right_env, rights, lefts, near):
    cols, rows = len(lefts), len(rights) + 1
    size, share = lefts[0].shape[1:]
    width = share // size * cols
    states = mpo_rows.shape[0] // width
    half, lanes = size // 2, 2 * size
    params = pltpu.CompilerParams(vmem_limit_bytes=32 << 20)
    mixed = pl.pallas_call(
        functools.partial(mix_kernel, states, cols, count),
        out_shape=[jax.ShapeDtypeStruct((half * states, width * lanes), jnp.bfloat16)] * count,
        in_specs=[VMEM] * (2 + cols),
        out_specs=[VMEM] * count,
        scratch_shapes=[pltpu.VMEM((count, half * width, lanes), jnp.float32)],
        compiler_params=params,
        cost_estimate=cost_of(count, states, width, size, 1, 0),
        name="mix",
    )(state_diag, mpo_rows, *lefts)
    return pl.pallas_call(
        functools.partial(right_kernel, states, rows, cols, near, count),
        out_shape=[jax.ShapeDtypeStruct((count, size, states // cols * size), jnp.bfloat16)] * cols,
        in_specs=[SMEM] * 3 + [VMEM] * (rows + count),
        out_specs=[VMEM] * cols,
        scratch_shapes=[
            pltpu.VMEM((count, size, width * size), jnp.bfloat16),
            pltpu.VMEM((count, width * lanes, lanes), jnp.bfloat16),
            pltpu.VMEM((count, half * states, lanes), jnp.float32),
        ],
        compiler_params=params,
        cost_estimate=cost_of(count, states, width, size, 0, 1),
        name="right",
    )(order, slots, keys, right_env, *rights, *mixed)


def last_blocks(order, slots, keys, state_diag, mpo_rows, right_env, rights, lefts, early, near):
    cols, rows = len(lefts), len(rights) + 1
    first, (steps, size, share) = early.shape[0], lefts[0].shape
    count = steps - first
    width = share // size * cols
    states = mpo_rows.shape[0] // width
    half, lanes = size // 2, 2 * size

    def out(blocks):
        return jax.ShapeDtypeStruct((blocks, size, states // cols * size), jnp.bfloat16)

    return pl.pallas_call(
        functools.partial(apply_kernel, states, rows, cols, near, first, count),
        out_shape=[out(steps if d == 1 else count) for d in range(cols)],
        in_specs=[SMEM] * 3 + [VMEM] * (4 + rows - 1 + cols),
        out_specs=[VMEM] * cols,
        scratch_shapes=[
            pltpu.VMEM((count, half * width, lanes), jnp.float32),
            pltpu.VMEM((count, half * states, width * lanes), jnp.bfloat16),
            pltpu.VMEM((count, size, width * size), jnp.bfloat16),
            pltpu.VMEM((count, width * lanes, lanes), jnp.bfloat16),
            pltpu.VMEM((count, half * states, lanes), jnp.float32),
        ],
        compiler_params=pltpu.CompilerParams(vmem_limit_bytes=32 << 20),
        cost_estimate=cost_of(count, states, width, size, 1, 1),
        name="apply",
    )(order, slots, keys, right_env, state_diag, mpo_rows, early, *rights, *lefts)


def place_kernel(cols, pieces, begun, order_ref, *refs):
    came = refs[begun : begun + len(pieces)]
    out_ref, sem = refs[begun + len(pieces) :]
    steps = order_ref.shape[0] // cols
    mine = lax.axis_index("col")
    copies = []
    for piece, (other, first) in zip(came, pieces):
        col = jnp.bitwise_xor(mine, other)
        for k in range(piece.shape[0]):
            p = order_ref[col * steps + first + k]
            copies.append(pltpu.make_async_copy(piece.at[k], out_ref.at[p], sem.at[len(copies)]))
    run_copies(copies)


def place_blocks(order, out, came, pieces, cols):
    begun = [] if out is None else [out]
    return pl.pallas_call(
        functools.partial(place_kernel, cols, pieces, len(begun)),
        out_shape=jax.ShapeDtypeStruct((order.shape[0],) + came[0].shape[1:], came[0].dtype),
        in_specs=[SMEM] + [HBM] * len(begun) + [VMEM] * len(came),
        out_specs=HBM,
        scratch_shapes=[pltpu.SemaphoreType.DMA((sum(piece.shape[0] for piece in came),))],
        input_output_aliases={1: 0} if begun else {},
        compiler_params=pltpu.CompilerParams(vmem_limit_bytes=4 << 20),
        name="place",
    )(order, *begun, *came)


def shards(state_blocks, left_env, right_env, mpo_tensor, block_left, block_owner, block_sub):
    rows = lax.axis_size("row")
    cols = lax.axis_size("col")
    count, size = state_blocks.shape[:2]
    states = state_blocks.shape[2] // size
    width = mpo_tensor.shape[0]
    most = max(2, (2 * count + rows - 1) // rows)
    near = -(-most // cols)

    half = count // cols - max(1, count // cols // 4)

    keys = jnp.bitwise_or(lax.shift_left(block_owner[:, 0], SHIFT), block_sub)
    others = [swap(keys, "row", step) for step in range(1, rows)]
    sends, order, slots = route(block_left, keys, left_env, cols, near)
    picked = pick(others, right_env, cols, near)
    rest = list(range(3, cols))
    mpo_tensor, *held = lax.optimization_barrier((mpo_tensor, *picked, *[sends[d] for d in rest]))
    far, sent = held[: rows - 1], dict(zip(rest, held[rows - 1 :]))
    lefts = [sends[0]] + [swap(sent.get(d, sends[d]), "col", d) for d in range(1, cols)]
    state_diag, mpo_rows = prepare(order, state_blocks, mpo_tensor, cols, states)
    core_send, state_diag, *lefts[1:] = lax.optimization_barrier((far[0], state_diag, *lefts[1:]))
    rights = [swap(core_send, "row", 1)] + [swap(far[d - 1], "row", d) for d in range(2, rows)]
    early = first_blocks(half, order, slots, keys, state_diag, mpo_rows, right_env, rights, lefts, near)
    came = [swap(early[d], "col", d) for d in range(2, cols)]
    late = last_blocks(order, slots, keys, state_diag, mpo_rows, right_env, rights, lefts, early[1], near)
    joined = lax.optimization_barrier((*late[1:], *came))
    sent, came = joined[: cols - 1], joined[cols - 1 :]
    last = [swap(sent[d - 1], "col", d) for d in range(1, cols)]
    pieces = [(0, 0)] + [(d, 0) for d in range(2, cols)] + [(0, half)]
    out = place_blocks(order, None, [early[0], *came, late[0]], pieces, cols)
    pieces = [(1, 0)] + [(d, half) for d in range(2, cols)]
    return place_blocks(order, out, last, pieces, cols)


def solution(mesh):
    placed = (
        P(("groups", "row"), None, None),
        P(("groups", "row"), None, "col"),
        P(("groups", "row"), None, None),
        P(),
        P(("groups", "row")),
        P(("groups", "row"), None),
        P(("groups", "row")),
    )
    return jax.shard_map(
        shards,
        mesh=mesh,
        in_specs=placed,
        out_specs=P(("groups", "row"), None, "col"),
        check_vma=False,
    )
```

```python
import functools

import jax
import jax.numpy as jnp
from jax import lax
from jax.experimental import pallas as pl
from jax.experimental.pallas import tpu as pltpu
from jax.sharding import PartitionSpec as P

CHUNK = 16
SHIFT = 16
SMEM = pl.BlockSpec(memory_space=pltpu.SMEM)
VMEM = pl.BlockSpec(memory_space=pltpu.VMEM)
HBM = pl.BlockSpec(memory_space=pltpu.HBM)
ANY = pl.BlockSpec(memory_space=pl.ANY)


def swap(array, axis, step):
    size = lax.axis_size(axis)
    return lax.ppermute(array, axis, [(i, i ^ step) for i in range(size)])


def run_copies(copies):
    for copy in copies:
        copy.start()
    for copy in copies:
        copy.wait()


def owner_of(key):
    return lax.shift_right_logical(key, SHIFT)


def sub_of(key):
    return jnp.bitwise_and(key, (1 << SHIFT) - 1)


def route_kernel(cols, near, left_ref, key_ref, env_ref, *refs):
    sends = refs[:cols]
    order_ref, slot_ref, by_place = refs[cols:]
    count = left_ref.shape[0]
    steps = count // cols
    mine = lax.axis_index("col")
    owners = [owner_of(key_ref[p]) for p in range(count)]
    for p in range(count):
        place = jnp.int32(0)
        for other in range(count):
            if other < p:
                place = place + (owners[other] <= owners[p]).astype(jnp.int32)
            elif other > p:
                place = place + (owners[other] < owners[p]).astype(jnp.int32)
        by_place[place] = p
    for col in range(cols):
        before = None
        for step in range(steps):
            p = by_place[step * cols + col]
            owner = owner_of(key_ref[p])
            if before is None:
                slot = jnp.int32(0)
            else:
                slot = jnp.where(owner == before[0], before[1] + 1, 0)
            before = owner, slot
            order_ref[col * steps + step] = p
            slot_ref[col * steps + step] = owner * near + slot
    for other in range(cols):
        col = jnp.bitwise_xor(mine, other)
        for step in range(steps):
            p = order_ref[col * steps + step]
            sends[other][step] = env_ref[left_ref[p]]


def route(block_left, keys, left_env, cols, near):
    count = block_left.shape[0]
    size, width = left_env.shape[1:]
    piece = jax.ShapeDtypeStruct((count // cols, size, width), left_env.dtype)
    listed = jax.ShapeDtypeStruct((count,), jnp.int32)
    *sends, order, slots = pl.pallas_call(
        functools.partial(route_kernel, cols, near),
        out_shape=(piece,) * cols + (listed, listed),
        in_specs=[SMEM, SMEM, VMEM],
        out_specs=(VMEM,) * cols + (SMEM, SMEM),
        scratch_shapes=[pltpu.SMEM((count,), jnp.int32)],
        name="route",
    )(block_left, keys, left_env)
    return sends, order, slots


def pick_kernel(rows, cols, near, *refs):
    key_refs = refs[: rows - 1]
    env_ref = refs[rows - 1]
    sends = refs[rows:]
    count = key_refs[0].shape[0]
    me = lax.axis_index("row")
    mine = lax.axis_index("col")
    for other in range(rows - 1):
        keys = [key_refs[other][p] for p in range(count)]
        owners = [owner_of(key) for key in keys]
        first = jnp.int32(0)
        for p in range(count):
            first = first + (owners[p] < me).astype(jnp.int32)
        past = -lax.rem(mine - lax.rem(first, cols) + cols, cols)
        wanted = [jnp.int32(0)] * near
        for p in range(count):
            here = owners[p] == me
            for slot in range(near):
                wanted[slot] = jnp.where(here & (past == slot * cols), sub_of(keys[p]), wanted[slot])
            past = past + here.astype(jnp.int32)
        for slot in range(near):
            sends[other][slot] = env_ref[wanted[slot]]


def pick(keys, right_env, cols, near):
    rows = len(keys) + 1
    piece = jax.ShapeDtypeStruct((near,) + right_env.shape[1:], right_env.dtype)
    return pl.pallas_call(
        functools.partial(pick_kernel, rows, cols, near),
        out_shape=[piece] * (rows - 1),
        in_specs=[SMEM] * (rows - 1) + [VMEM],
        out_specs=(VMEM,) * (rows - 1),
        name="pick",
    )(*keys, right_env)


def halves(tile, low):
    swapped = pltpu.roll(tile, tile.shape[1] // 2, 1)
    zero = jnp.zeros_like(tile)
    return (
        jnp.where(low, tile, zero),
        jnp.where(low, zero, swapped),
        jnp.where(low, swapped, zero),
        jnp.where(low, zero, tile),
    )


def spread_state(block, state_diag, low):
    size = block.shape[0]
    for s in range(0, block.shape[1] // size, 2):
        pieces = halves(block[:, s * size : (s + 2) * size].astype(jnp.float32), low)
        for i in range(4):
            row, col = (i % 2) * size, (s + i // 2) * 2 * size
            state_diag[row : row + size, col : col + 2 * size] = pieces[i].astype(jnp.bfloat16)


def spread_right(right, right_diag, low):
    size = right.shape[0]
    for v in range(0, right.shape[1] // size, 2):
        pieces = halves(right[:, v * size : (v + 2) * size].astype(jnp.float32), low)
        for i in range(4):
            at = (2 * v + i) * size
            right_diag[at : at + size, :] = pieces[i].astype(jnp.bfloat16)


def spread_left(lefts, left_rows):
    cols = len(lefts)
    size = lefts[0].shape[0]
    half, share = size // 2, lefts[0].shape[1] // size
    mine = lax.axis_index("col")
    for other in range(cols):
        col = jnp.bitwise_xor(mine, other)
        for k in range(share):
            piece = lefts[other][:, k * size : (k + 1) * size].astype(jnp.float32)
            both = jnp.concatenate([piece[:half], piece[half:]], axis=1)
            left_rows[pl.ds(col * share + k, half, stride=cols * share), :] = both


def mix_block(states, left_rows, state_diag, mpo_ref, mixed):
    width = mpo_ref.shape[0] // states
    lanes = left_rows.shape[1]
    half = left_rows.shape[0] // width
    for start in range(0, half, CHUNK):
        taken = left_rows[start * width : (start + CHUNK) * width, :].astype(jnp.bfloat16)
        first = jnp.dot(taken, state_diag[...], preferred_element_type=jnp.float32)
        columns = []
        for x in range(CHUNK):
            one = first[x * width : (x + 1) * width, :]
            columns.append(
                jnp.concatenate(
                    [one[:, s * lanes : (s + 1) * lanes] for s in range(states)], axis=0
                ).astype(jnp.bfloat16)
            )
        gathered = jnp.concatenate(columns, axis=1)
        channels = jnp.dot(mpo_ref[...], gathered, preferred_element_type=jnp.float32).astype(jnp.bfloat16)
        for x in range(CHUNK):
            for v in range(width):
                mixed[(start + x) * states : (start + x + 1) * states, v * lanes : (v + 1) * lanes] = channels[
                    v * states : (v + 1) * states, x * lanes : (x + 1) * lanes
                ]


def finish_block(states, mixed, right_diag, result, outs, low):
    cols = len(outs)
    size = low.shape[0]
    half, per = size // 2, states // cols
    mine = lax.axis_index("col")
    result[...] = jnp.dot(mixed[...], right_diag[...], preferred_element_type=jnp.float32)
    low = low[:half]
    for other in range(cols):
        col = jnp.bitwise_xor(mine, other)
        for t in range(0, per, 2):
            one = result[pl.ds(col * per + t, half, stride=states), :]
            two = result[pl.ds(col * per + t + 1, half, stride=states), :]
            upper = jnp.where(low, one, pltpu.roll(two, size, 1))
            lower = jnp.where(low, pltpu.roll(one, size, 1), two)
            outs[other][:half, t * size : (t + 2) * size] = upper.astype(jnp.bfloat16)
            outs[other][half:, t * size : (t + 2) * size] = lower.astype(jnp.bfloat16)


def half_mask(size):
    return lax.broadcasted_iota(jnp.int32, (size, 2 * size), 1) < size


def prepare_kernel(states, order_ref, state_ref, mpo_ref, diag_ref, rows_ref, block, flat, sem):
    steps, size = block.shape[:2]
    width = mpo_ref.shape[0]
    low = half_mask(size)
    at = lax.axis_index("col") * steps
    copies = [
        pltpu.make_async_copy(state_ref.at[order_ref[at + k]], block.at[k], sem.at[k]) for k in range(steps)
    ]
    for copy in copies:
        copy.start()
    both = (states * states, states * states)
    row, col = lax.broadcasted_iota(jnp.int32, both, 0), lax.broadcasted_iota(jnp.int32, both, 1)
    turned = lax.rem(row, states) * states + lax.div(row, states)
    turn = jnp.where(turned == col, 1.0, 0.0).astype(jnp.bfloat16)
    split = flat.shape[0]
    for w in range(width):
        taken = mpo_ref[w].astype(jnp.float32)
        for i in range(split):
            flat[i, w * width : (w + 1) * width, :] = taken[:, i * 128 : (i + 1) * 128]
    taken = jnp.concatenate([flat[i] for i in range(split)], axis=1).astype(jnp.bfloat16)
    taken = jnp.dot(taken, turn, preferred_element_type=jnp.float32)
    for i in range(split):
        flat[i] = taken[:, i * 128 : (i + 1) * 128]

    def some_channels(j, carry):
        for v in range(4):
            taken = [jnp.transpose(flat[i, pl.ds(4 * j + v, width, stride=width), :]) for i in range(split)]
            taken = jnp.concatenate(taken, axis=0)
            line = jnp.concatenate([taken[s * states : (s + 1) * states, :] for s in range(states)], axis=1)
            rows_ref[pl.ds(pl.multiple_of((4 * j + v) * states, states), states), :] = line.astype(jnp.bfloat16)
        return carry

    lax.fori_loop(0, width // 4, some_channels, 0)
    for copy in copies:
        copy.wait()

    def one_block(k, carry):
        spread_state(block.at[k], diag_ref.at[k], low)
        return carry

    lax.fori_loop(0, steps, one_block, 0)


def prepare(order, state_blocks, mpo_tensor, cols, states):
    count, size = state_blocks.shape[:2]
    steps, width = count // cols, mpo_tensor.shape[0]
    return pl.pallas_call(
        functools.partial(prepare_kernel, states),
        out_shape=[
            jax.ShapeDtypeStruct((steps, 2 * size, 2 * states * size), jnp.bfloat16),
            jax.ShapeDtypeStruct((width * states, states * width), jnp.bfloat16),
        ],
        in_specs=[SMEM, ANY, VMEM],
        out_specs=[VMEM, VMEM],
        scratch_shapes=[
            pltpu.VMEM((steps, size, states * size), jnp.bfloat16),
            pltpu.VMEM((states * states // 128, width * width, 128), jnp.float32),
            pltpu.SemaphoreType.DMA((steps,)),
        ],
        compiler_params=pltpu.CompilerParams(vmem_limit_bytes=10 << 20),
        cost_estimate=pl.CostEstimate(flops=0, bytes_accessed=0, transcendentals=0),
        name="prepare",
    )(order, state_blocks, mpo_tensor)


def mix_kernel(states, cols, count, diag_ref, mpo_ref, *refs):
    lefts, mixed, left_rows = refs[:cols], refs[cols : cols + count], refs[-1]
    for k in range(count):
        spread_left([left.at[k] for left in lefts], left_rows.at[k])
    for k in range(count):
        mix_block(states, left_rows.at[k], diag_ref.at[k], mpo_ref, mixed[k])


def fetch_right(near, key_ref, order_ref, slot_ref, at, env_ref, rights, right_now):
    slot = lax.rem(slot_ref[at], near)
    apart = jnp.bitwise_xor(lax.div(slot_ref[at], near), lax.axis_index("row"))

    @pl.when(apart == 0)
    def _():
        right_now[...] = env_ref[sub_of(key_ref[order_ref[at]])]

    for other, right in enumerate(rights, 1):

        @pl.when(apart == other)
        def _():
            right_now[...] = right[slot]


def right_kernel(states, rows, cols, near, count, order_ref, slot_ref, key_ref, env_ref, *refs):
    rights, refs = refs[: rows - 1], refs[rows - 1 :]
    mixed, outs, (right_now, right_diag, result) = refs[:count], refs[count : count + cols], refs[count + cols :]
    low = half_mask(env_ref.shape[1])
    at = lax.axis_index("col") * (order_ref.shape[0] // cols)
    for k in range(count):
        fetch_right(near, key_ref, order_ref, slot_ref, at + k, env_ref, rights, right_now.at[k])
    for k in range(count):
        spread_right(right_now.at[k], right_diag.at[k], low)
    for k in range(count):
        finish_block(states, mixed[k], right_diag.at[k], result.at[k], [out.at[k] for out in outs], low)


def apply_kernel(
    states, rows, cols, near, first, count, order_ref, slot_ref, key_ref, env_ref, diag_ref, mpo_ref, early_ref, *refs
):
    rights, lefts, refs = refs[: rows - 1], refs[rows - 1 : rows - 1 + cols], refs[rows - 1 + cols :]
    outs, (left_rows, mixed, right_now, right_diag, result) = refs[:cols], refs[cols:]
    low = half_mask(env_ref.shape[1])
    at = lax.axis_index("col") * (order_ref.shape[0] // cols) + first
    for k in range(count):
        spread_left([left.at[first + k] for left in lefts], left_rows.at[k])
    for k in range(count):
        mix_block(states, left_rows.at[k], diag_ref.at[first + k], mpo_ref, mixed.at[k])
    outs[1][:first] = early_ref[...]
    for k in range(count):
        fetch_right(near, key_ref, order_ref, slot_ref, at + k, env_ref, rights, right_now.at[k])
    for k in range(count):
        spread_right(right_now.at[k], right_diag.at[k], low)
    for k in range(count):
        into = [out.at[first + k if d == 1 else k] for d, out in enumerate(outs)]
        finish_block(states, mixed.at[k], right_diag.at[k], result.at[k], into, low)


def cost_of(blocks, states, width, size, mix, right):
    flops = mix * (width * size * size * states * size + (width * states) ** 2 * size * size)
    flops = 2 * blocks * (flops + right * states * size * size * width * size)
    return pl.CostEstimate(flops=flops, bytes_accessed=4 << 20, transcendentals=0)


def first_blocks(count, order, slots, keys, state_diag, mpo_rows, right_env, rights, lefts, near):
    cols, rows = len(lefts), len(rights) + 1
    size, share = lefts[0].shape[1:]
    width = share // size * cols
    states = mpo_rows.shape[0] // width
    half, lanes = size // 2, 2 * size
    params = pltpu.CompilerParams(vmem_limit_bytes=32 << 20)
    mixed = pl.pallas_call(
        functools.partial(mix_kernel, states, cols, count),
        out_shape=[jax.ShapeDtypeStruct((half * states, width * lanes), jnp.bfloat16)] * count,
        in_specs=[VMEM] * (2 + cols),
        out_specs=[VMEM] * count,
        scratch_shapes=[pltpu.VMEM((count, half * width, lanes), jnp.float32)],
        compiler_params=params,
        cost_estimate=cost_of(count, states, width, size, 1, 0),
        name="mix",
    )(state_diag, mpo_rows, *lefts)
    return pl.pallas_call(
        functools.partial(right_kernel, states, rows, cols, near, count),
        out_shape=[jax.ShapeDtypeStruct((count, size, states // cols * size), jnp.bfloat16)] * cols,
        in_specs=[SMEM] * 3 + [VMEM] * (rows + count),
        out_specs=[VMEM] * cols,
        scratch_shapes=[
            pltpu.VMEM((count, size, width * size), jnp.bfloat16),
            pltpu.VMEM((count, width * lanes, lanes), jnp.bfloat16),
            pltpu.VMEM((count, half * states, lanes), jnp.float32),
        ],
        compiler_params=params,
        cost_estimate=cost_of(count, states, width, size, 0, 1),
        name="right",
    )(order, slots, keys, right_env, *rights, *mixed)


def last_blocks(order, slots, keys, state_diag, mpo_rows, right_env, rights, lefts, early, near):
    cols, rows = len(lefts), len(rights) + 1
    first, (steps, size, share) = early.shape[0], lefts[0].shape
    count = steps - first
    width = share // size * cols
    states = mpo_rows.shape[0] // width
    half, lanes = size // 2, 2 * size

    def out(blocks):
        return jax.ShapeDtypeStruct((blocks, size, states // cols * size), jnp.bfloat16)

    return pl.pallas_call(
        functools.partial(apply_kernel, states, rows, cols, near, first, count),
        out_shape=[out(steps if d == 1 else count) for d in range(cols)],
        in_specs=[SMEM] * 3 + [VMEM] * (4 + rows - 1 + cols),
        out_specs=[VMEM] * cols,
        scratch_shapes=[
            pltpu.VMEM((count, half * width, lanes), jnp.float32),
            pltpu.VMEM((count, half * states, width * lanes), jnp.bfloat16),
            pltpu.VMEM((count, size, width * size), jnp.bfloat16),
            pltpu.VMEM((count, width * lanes, lanes), jnp.bfloat16),
            pltpu.VMEM((count, half * states, lanes), jnp.float32),
        ],
        compiler_params=pltpu.CompilerParams(vmem_limit_bytes=32 << 20),
        cost_estimate=cost_of(count, states, width, size, 1, 1),
        name="apply",
    )(order, slots, keys, right_env, state_diag, mpo_rows, early, *rights, *lefts)


def place_kernel(cols, pieces, begun, order_ref, *refs):
    came = refs[begun : begun + len(pieces)]
    out_ref, sem = refs[begun + len(pieces) :]
    steps = order_ref.shape[0] // cols
    mine = lax.axis_index("col")
    copies = []
    for piece, (other, first) in zip(came, pieces):
        col = jnp.bitwise_xor(mine, other)
        for k in range(piece.shape[0]):
            p = order_ref[col * steps + first + k]
            copies.append(pltpu.make_async_copy(piece.at[k], out_ref.at[p], sem.at[len(copies)]))
    run_copies(copies)


def place_blocks(order, out, came, pieces, cols):
    begun = [] if out is None else [out]
    return pl.pallas_call(
        functools.partial(place_kernel, cols, pieces, len(begun)),
        out_shape=jax.ShapeDtypeStruct((order.shape[0],) + came[0].shape[1:], came[0].dtype),
        in_specs=[SMEM] + [HBM] * len(begun) + [VMEM] * len(came),
        out_specs=HBM,
        scratch_shapes=[pltpu.SemaphoreType.DMA((sum(piece.shape[0] for piece in came),))],
        input_output_aliases={1: 0} if begun else {},
        compiler_params=pltpu.CompilerParams(vmem_limit_bytes=4 << 20),
        cost_estimate=pl.CostEstimate(flops=10**10, bytes_accessed=1 << 20, transcendentals=0),
        name="place",
    )(order, *begun, *came)


def shards(state_blocks, left_env, right_env, mpo_tensor, block_left, block_owner, block_sub):
    rows = lax.axis_size("row")
    cols = lax.axis_size("col")
    count, size = state_blocks.shape[:2]
    states = state_blocks.shape[2] // size
    width = mpo_tensor.shape[0]
    most = max(2, (2 * count + rows - 1) // rows)
    near = -(-most // cols)

    half = count // cols - max(1, count // cols // 4)

    keys = jnp.bitwise_or(lax.shift_left(block_owner[:, 0], SHIFT), block_sub)
    others = [swap(keys, "row", step) for step in range(1, rows)]
    sends, order, slots = route(block_left, keys, left_env, cols, near)
    picked = pick(others, right_env, cols, near)
    rest = list(range(3, cols))
    mpo_tensor, *held = lax.optimization_barrier((mpo_tensor, *picked, *[sends[d] for d in rest]))
    far, sent = held[: rows - 1], dict(zip(rest, held[rows - 1 :]))
    lefts = [sends[0]] + [swap(sent.get(d, sends[d]), "col", d) for d in range(1, cols)]
    state_diag, mpo_rows = prepare(order, state_blocks, mpo_tensor, cols, states)
    core_send, state_diag, *lefts[1:] = lax.optimization_barrier((far[0], state_diag, *lefts[1:]))
    rights = [swap(core_send, "row", 1)] + [swap(far[d - 1], "row", d) for d in range(2, rows)]
    early = first_blocks(half, order, slots, keys, state_diag, mpo_rows, right_env, rights, lefts, near)
    came = [swap(early[d], "col", d) for d in range(2, cols)]
    late = last_blocks(order, slots, keys, state_diag, mpo_rows, right_env, rights, lefts, early[1], near)
    last = [swap(late[d], "col", d) for d in range(1, cols)]
    pieces = [(0, 0)] + [(d, 0) for d in range(2, cols)] + [(0, half)]
    out = place_blocks(order, None, [early[0], *came, late[0]], pieces, cols)
    pieces = [(1, 0)] + [(d, half) for d in range(2, cols)]
    return place_blocks(order, out, last, pieces, cols)


def solution(mesh):
    placed = (
        P(("groups", "row"), None, None),
        P(("groups", "row"), None, "col"),
        P(("groups", "row"), None, None),
        P(),
        P(("groups", "row")),
        P(("groups", "row"), None),
        P(("groups", "row")),
    )
    return jax.shard_map(
        shards,
        mesh=mesh,
        in_specs=placed,
        out_specs=P(("groups", "row"), None, "col"),
        check_vma=False,
    )
```

```python
import functools

import jax
import jax.numpy as jnp
from jax import lax
from jax.experimental import pallas as pl
from jax.experimental.pallas import tpu as pltpu
from jax.sharding import PartitionSpec as P

CHUNK = 16
SHIFT = 16
SMEM = pl.BlockSpec(memory_space=pltpu.SMEM)
VMEM = pl.BlockSpec(memory_space=pltpu.VMEM)
HBM = pl.BlockSpec(memory_space=pltpu.HBM)
ANY = pl.BlockSpec(memory_space=pl.ANY)


def swap(array, axis, step):
    size = lax.axis_size(axis)
    return lax.ppermute(array, axis, [(i, i ^ step) for i in range(size)])


def run_copies(copies):
    for copy in copies:
        copy.start()
    for copy in copies:
        copy.wait()


def owner_of(key):
    return lax.shift_right_logical(key, SHIFT)


def sub_of(key):
    return jnp.bitwise_and(key, (1 << SHIFT) - 1)


def route_kernel(cols, near, left_ref, key_ref, env_ref, *refs):
    sends = refs[:cols]
    order_ref, slot_ref, by_place = refs[cols:]
    count = left_ref.shape[0]
    steps = count // cols
    mine = lax.axis_index("col")
    owners = [owner_of(key_ref[p]) for p in range(count)]
    for p in range(count):
        place = jnp.int32(0)
        for other in range(count):
            if other < p:
                place = place + (owners[other] <= owners[p]).astype(jnp.int32)
            elif other > p:
                place = place + (owners[other] < owners[p]).astype(jnp.int32)
        by_place[place] = p
    for col in range(cols):
        before = None
        for step in range(steps):
            p = by_place[step * cols + col]
            owner = owner_of(key_ref[p])
            if before is None:
                slot = jnp.int32(0)
            else:
                slot = jnp.where(owner == before[0], before[1] + 1, 0)
            before = owner, slot
            order_ref[col * steps + step] = p
            slot_ref[col * steps + step] = owner * near + slot
    for other in range(cols):
        col = jnp.bitwise_xor(mine, other)
        for step in range(steps):
            p = order_ref[col * steps + step]
            sends[other][step] = env_ref[left_ref[p]]


def route(block_left, keys, left_env, cols, near):
    count = block_left.shape[0]
    size, width = left_env.shape[1:]
    piece = jax.ShapeDtypeStruct((count // cols, size, width), left_env.dtype)
    listed = jax.ShapeDtypeStruct((count,), jnp.int32)
    *sends, order, slots = pl.pallas_call(
        functools.partial(route_kernel, cols, near),
        out_shape=(piece,) * cols + (listed, listed),
        in_specs=[SMEM, SMEM, VMEM],
        out_specs=(VMEM,) * cols + (SMEM, SMEM),
        scratch_shapes=[pltpu.SMEM((count,), jnp.int32)],
        name="route",
    )(block_left, keys, left_env)
    return sends, order, slots


def pick_kernel(rows, cols, near, *refs):
    key_refs = refs[: rows - 1]
    env_ref = refs[rows - 1]
    sends = refs[rows:]
    count = key_refs[0].shape[0]
    me = lax.axis_index("row")
    mine = lax.axis_index("col")
    for other in range(rows - 1):
        keys = [key_refs[other][p] for p in range(count)]
        owners = [owner_of(key) for key in keys]
        first = jnp.int32(0)
        for p in range(count):
            first = first + (owners[p] < me).astype(jnp.int32)
        past = -lax.rem(mine - lax.rem(first, cols) + cols, cols)
        wanted = [jnp.int32(0)] * near
        for p in range(count):
            here = owners[p] == me
            for slot in range(near):
                wanted[slot] = jnp.where(here & (past == slot * cols), sub_of(keys[p]), wanted[slot])
            past = past + here.astype(jnp.int32)
        for slot in range(near):
            sends[other][slot] = env_ref[wanted[slot]]


def pick(keys, right_env, cols, near):
    rows = len(keys) + 1
    piece = jax.ShapeDtypeStruct((near,) + right_env.shape[1:], right_env.dtype)
    return pl.pallas_call(
        functools.partial(pick_kernel, rows, cols, near),
        out_shape=[piece] * (rows - 1),
        in_specs=[SMEM] * (rows - 1) + [VMEM],
        out_specs=(VMEM,) * (rows - 1),
        name="pick",
    )(*keys, right_env)


def halves(tile, low):
    swapped = pltpu.roll(tile, tile.shape[1] // 2, 1)
    zero = jnp.zeros_like(tile)
    return (
        jnp.where(low, tile, zero),
        jnp.where(low, zero, swapped),
        jnp.where(low, swapped, zero),
        jnp.where(low, zero, tile),
    )


def spread_state(block, state_diag, low):
    size = block.shape[0]
    for s in range(0, block.shape[1] // size, 2):
        pieces = halves(block[:, s * size : (s + 2) * size].astype(jnp.float32), low)
        for i in range(4):
            row, col = (i % 2) * size, (s + i // 2) * 2 * size
            state_diag[row : row + size, col : col + 2 * size] = pieces[i].astype(jnp.bfloat16)


def spread_right(right, right_diag, low):
    size = right.shape[0]
    for v in range(0, right.shape[1] // size, 2):
        pieces = halves(right[:, v * size : (v + 2) * size].astype(jnp.float32), low)
        for i in range(4):
            at = (2 * v + i) * size
            right_diag[at : at + size, :] = pieces[i].astype(jnp.bfloat16)


def spread_left(lefts, left_rows):
    cols = len(lefts)
    size = lefts[0].shape[0]
    half, share = size // 2, lefts[0].shape[1] // size
    mine = lax.axis_index("col")
    for other in range(cols):
        col = jnp.bitwise_xor(mine, other)
        for k in range(share):
            piece = lefts[other][:, k * size : (k + 1) * size].astype(jnp.float32)
            both = jnp.concatenate([piece[:half], piece[half:]], axis=1)
            left_rows[pl.ds(col * share + k, half, stride=cols * share), :] = both


def mix_block(states, left_rows, state_diag, mpo_ref, mixed):
    width = mpo_ref.shape[0] // states
    lanes = left_rows.shape[1]
    half = left_rows.shape[0] // width
    for start in range(0, half, CHUNK):
        taken = left_rows[start * width : (start + CHUNK) * width, :].astype(jnp.bfloat16)
        first = jnp.dot(taken, state_diag[...], preferred_element_type=jnp.float32)
        columns = []
        for x in range(CHUNK):
            one = first[x * width : (x + 1) * width, :]
            columns.append(
                jnp.concatenate(
                    [one[:, s * lanes : (s + 1) * lanes] for s in range(states)], axis=0
                ).astype(jnp.bfloat16)
            )
        gathered = jnp.concatenate(columns, axis=1)
        channels = jnp.dot(mpo_ref[...], gathered, preferred_element_type=jnp.float32).astype(jnp.bfloat16)
        for x in range(CHUNK):
            for v in range(width):
                mixed[(start + x) * states : (start + x + 1) * states, v * lanes : (v + 1) * lanes] = channels[
                    v * states : (v + 1) * states, x * lanes : (x + 1) * lanes
                ]


def finish_block(states, mixed, right_diag, result, outs, low):
    cols = len(outs)
    size = low.shape[0]
    half, per = size // 2, states // cols
    mine = lax.axis_index("col")
    result[...] = jnp.dot(mixed[...], right_diag[...], preferred_element_type=jnp.float32)
    low = low[:half]
    for other in range(cols):
        col = jnp.bitwise_xor(mine, other)
        for t in range(0, per, 2):
            one = result[pl.ds(col * per + t, half, stride=states), :]
            two = result[pl.ds(col * per + t + 1, half, stride=states), :]
            upper = jnp.where(low, one, pltpu.roll(two, size, 1))
            lower = jnp.where(low, pltpu.roll(one, size, 1), two)
            outs[other][:half, t * size : (t + 2) * size] = upper.astype(jnp.bfloat16)
            outs[other][half:, t * size : (t + 2) * size] = lower.astype(jnp.bfloat16)


def half_mask(size):
    return lax.broadcasted_iota(jnp.int32, (size, 2 * size), 1) < size


def prepare_kernel(states, order_ref, state_ref, mpo_ref, diag_ref, rows_ref, block, flat, sem):
    steps, size = block.shape[:2]
    width = mpo_ref.shape[0]
    low = half_mask(size)
    at = lax.axis_index("col") * steps
    copies = [
        pltpu.make_async_copy(state_ref.at[order_ref[at + k]], block.at[k], sem.at[k]) for k in range(steps)
    ]
    for copy in copies:
        copy.start()
    both = (states * states, states * states)
    row, col = lax.broadcasted_iota(jnp.int32, both, 0), lax.broadcasted_iota(jnp.int32, both, 1)
    turned = lax.rem(row, states) * states + lax.div(row, states)
    turn = jnp.where(turned == col, 1.0, 0.0).astype(jnp.bfloat16)
    split = flat.shape[0]
    for w in range(width):
        taken = mpo_ref[w].astype(jnp.float32)
        for i in range(split):
            flat[i, w * width : (w + 1) * width, :] = taken[:, i * 128 : (i + 1) * 128]
    taken = jnp.concatenate([flat[i] for i in range(split)], axis=1).astype(jnp.bfloat16)
    taken = jnp.dot(taken, turn, preferred_element_type=jnp.float32)
    for i in range(split):
        flat[i] = taken[:, i * 128 : (i + 1) * 128]

    def some_channels(j, carry):
        for v in range(4):
            taken = [jnp.transpose(flat[i, pl.ds(4 * j + v, width, stride=width), :]) for i in range(split)]
            taken = jnp.concatenate(taken, axis=0)
            line = jnp.concatenate([taken[s * states : (s + 1) * states, :] for s in range(states)], axis=1)
            rows_ref[pl.ds(pl.multiple_of((4 * j + v) * states, states), states), :] = line.astype(jnp.bfloat16)
        return carry

    lax.fori_loop(0, width // 4, some_channels, 0)
    for copy in copies:
        copy.wait()

    def one_block(k, carry):
        spread_state(block.at[k], diag_ref.at[k], low)
        return carry

    lax.fori_loop(0, steps, one_block, 0)


def prepare(order, state_blocks, mpo_tensor, cols, states):
    count, size = state_blocks.shape[:2]
    steps, width = count // cols, mpo_tensor.shape[0]
    return pl.pallas_call(
        functools.partial(prepare_kernel, states),
        out_shape=[
            jax.ShapeDtypeStruct((steps, 2 * size, 2 * states * size), jnp.bfloat16),
            jax.ShapeDtypeStruct((width * states, states * width), jnp.bfloat16),
        ],
        in_specs=[SMEM, ANY, VMEM],
        out_specs=[VMEM, VMEM],
        scratch_shapes=[
            pltpu.VMEM((steps, size, states * size), jnp.bfloat16),
            pltpu.VMEM((states * states // 128, width * width, 128), jnp.float32),
            pltpu.SemaphoreType.DMA((steps,)),
        ],
        compiler_params=pltpu.CompilerParams(vmem_limit_bytes=10 << 20),
        cost_estimate=pl.CostEstimate(flops=0, bytes_accessed=0, transcendentals=0),
        name="prepare",
    )(order, state_blocks, mpo_tensor)


def mix_kernel(states, cols, count, diag_ref, mpo_ref, *refs):
    lefts, mixed, left_rows = refs[:cols], refs[cols : cols + count], refs[-1]
    for k in range(count):
        spread_left([left.at[k] for left in lefts], left_rows.at[k])
    for k in range(count):
        mix_block(states, left_rows.at[k], diag_ref.at[k], mpo_ref, mixed[k])


def fetch_right(near, key_ref, order_ref, slot_ref, at, env_ref, rights, right_now):
    slot = lax.rem(slot_ref[at], near)
    apart = jnp.bitwise_xor(lax.div(slot_ref[at], near), lax.axis_index("row"))

    @pl.when(apart == 0)
    def _():
        right_now[...] = env_ref[sub_of(key_ref[order_ref[at]])]

    for other, right in enumerate(rights, 1):

        @pl.when(apart == other)
        def _():
            right_now[...] = right[slot]


def right_kernel(states, rows, cols, near, count, order_ref, slot_ref, key_ref, env_ref, *refs):
    rights, refs = refs[: rows - 1], refs[rows - 1 :]
    mixed, outs, (right_now, right_diag, result) = refs[:count], refs[count : count + cols], refs[count + cols :]
    low = half_mask(env_ref.shape[1])
    at = lax.axis_index("col") * (order_ref.shape[0] // cols)
    for k in range(count):
        fetch_right(near, key_ref, order_ref, slot_ref, at + k, env_ref, rights, right_now.at[k])
    for k in range(count):
        spread_right(right_now.at[k], right_diag.at[k], low)
    for k in range(count):
        finish_block(states, mixed[k], right_diag.at[k], result.at[k], [out.at[k] for out in outs], low)


def apply_kernel(
    states, rows, cols, near, first, count, order_ref, slot_ref, key_ref, env_ref, diag_ref, mpo_ref, *refs
):
    rights, lefts, refs = refs[: rows - 1], refs[rows - 1 : rows - 1 + cols], refs[rows - 1 + cols :]
    outs, (left_rows, mixed, right_now, right_diag, result) = refs[:cols], refs[cols:]
    low = half_mask(env_ref.shape[1])
    at = lax.axis_index("col") * (order_ref.shape[0] // cols) + first
    for k in range(count):
        spread_left([left.at[first + k] for left in lefts], left_rows.at[k])
    for k in range(count):
        mix_block(states, left_rows.at[k], diag_ref.at[first + k], mpo_ref, mixed.at[k])
    for k in range(count):
        fetch_right(near, key_ref, order_ref, slot_ref, at + k, env_ref, rights, right_now.at[k])
    for k in range(count):
        spread_right(right_now.at[k], right_diag.at[k], low)
    for k in range(count):
        finish_block(states, mixed.at[k], right_diag.at[k], result.at[k], [out.at[k] for out in outs], low)


def cost_of(blocks, states, width, size, mix, right):
    flops = mix * (width * size * size * states * size + (width * states) ** 2 * size * size)
    flops = 2 * blocks * (flops + right * states * size * size * width * size)
    return pl.CostEstimate(flops=flops, bytes_accessed=4 << 20, transcendentals=0)


def first_blocks(count, order, slots, keys, state_diag, mpo_rows, right_env, rights, lefts, near):
    cols, rows = len(lefts), len(rights) + 1
    size, share = lefts[0].shape[1:]
    width = share // size * cols
    states = mpo_rows.shape[0] // width
    half, lanes = size // 2, 2 * size
    params = pltpu.CompilerParams(vmem_limit_bytes=32 << 20)
    mixed = pl.pallas_call(
        functools.partial(mix_kernel, states, cols, count),
        out_shape=[jax.ShapeDtypeStruct((half * states, width * lanes), jnp.bfloat16)] * count,
        in_specs=[VMEM] * (2 + cols),
        out_specs=[VMEM] * count,
        scratch_shapes=[pltpu.VMEM((count, half * width, lanes), jnp.float32)],
        compiler_params=params,
        cost_estimate=cost_of(count, states, width, size, 1, 0),
        name="mix",
    )(state_diag, mpo_rows, *lefts)
    return pl.pallas_call(
        functools.partial(right_kernel, states, rows, cols, near, count),
        out_shape=[jax.ShapeDtypeStruct((count, size, states // cols * size), jnp.bfloat16)] * cols,
        in_specs=[SMEM] * 3 + [VMEM] * (rows + count),
        out_specs=[VMEM] * cols,
        scratch_shapes=[
            pltpu.VMEM((count, size, width * size), jnp.bfloat16),
            pltpu.VMEM((count, width * lanes, lanes), jnp.bfloat16),
            pltpu.VMEM((count, half * states, lanes), jnp.float32),
        ],
        compiler_params=params,
        cost_estimate=cost_of(count, states, width, size, 0, 1),
        name="right",
    )(order, slots, keys, right_env, *rights, *mixed)


def last_blocks(order, slots, keys, state_diag, mpo_rows, right_env, rights, lefts, first, near):
    cols, rows = len(lefts), len(rights) + 1
    steps, size, share = lefts[0].shape
    count = steps - first
    width = share // size * cols
    states = mpo_rows.shape[0] // width
    half, lanes = size // 2, 2 * size

    return pl.pallas_call(
        functools.partial(apply_kernel, states, rows, cols, near, first, count),
        out_shape=[jax.ShapeDtypeStruct((count, size, states // cols * size), jnp.bfloat16)] * cols,
        in_specs=[SMEM] * 3 + [VMEM] * (3 + rows - 1 + cols),
        out_specs=[VMEM] * cols,
        scratch_shapes=[
            pltpu.VMEM((count, half * width, lanes), jnp.float32),
            pltpu.VMEM((count, half * states, width * lanes), jnp.bfloat16),
            pltpu.VMEM((count, size, width * size), jnp.bfloat16),
            pltpu.VMEM((count, width * lanes, lanes), jnp.bfloat16),
            pltpu.VMEM((count, half * states, lanes), jnp.float32),
        ],
        compiler_params=pltpu.CompilerParams(vmem_limit_bytes=32 << 20),
        cost_estimate=cost_of(count, states, width, size, 1, 1),
        name="apply",
    )(order, slots, keys, right_env, state_diag, mpo_rows, *rights, *lefts)


def place_kernel(cols, pieces, begun, order_ref, *refs):
    came = refs[begun : begun + len(pieces)]
    out_ref, sem = refs[begun + len(pieces) :]
    steps = order_ref.shape[0] // cols
    mine = lax.axis_index("col")
    copies = []
    for piece, (other, first) in zip(came, pieces):
        col = jnp.bitwise_xor(mine, other)
        for k in range(piece.shape[0]):
            p = order_ref[col * steps + first + k]
            copies.append(pltpu.make_async_copy(piece.at[k], out_ref.at[p], sem.at[len(copies)]))
    run_copies(copies)


def place_blocks(order, out, came, pieces, cols):
    begun = [] if out is None else [out]
    return pl.pallas_call(
        functools.partial(place_kernel, cols, pieces, len(begun)),
        out_shape=jax.ShapeDtypeStruct((order.shape[0],) + came[0].shape[1:], came[0].dtype),
        in_specs=[SMEM] + [HBM] * len(begun) + [VMEM] * len(came),
        out_specs=HBM,
        scratch_shapes=[pltpu.SemaphoreType.DMA((sum(piece.shape[0] for piece in came),))],
        input_output_aliases={1: 0} if begun else {},
        compiler_params=pltpu.CompilerParams(vmem_limit_bytes=4 << 20),
        cost_estimate=pl.CostEstimate(flops=10**10, bytes_accessed=1 << 20, transcendentals=0),
        name="place",
    )(order, *begun, *came)


def shards(state_blocks, left_env, right_env, mpo_tensor, block_left, block_owner, block_sub):
    rows = lax.axis_size("row")
    cols = lax.axis_size("col")
    count, size = state_blocks.shape[:2]
    states = state_blocks.shape[2] // size
    width = mpo_tensor.shape[0]
    most = max(2, (2 * count + rows - 1) // rows)
    near = -(-most // cols)

    half = count // cols - max(1, count // cols // 4)

    keys = jnp.bitwise_or(lax.shift_left(block_owner[:, 0], SHIFT), block_sub)
    others = [swap(keys, "row", step) for step in range(1, rows)]
    sends, order, slots = route(block_left, keys, left_env, cols, near)
    picked = pick(others, right_env, cols, near)
    rest = list(range(3, cols))
    mpo_tensor, *held = lax.optimization_barrier((mpo_tensor, *picked, *[sends[d] for d in rest]))
    far, sent = held[: rows - 1], dict(zip(rest, held[rows - 1 :]))
    lefts = [sends[0]] + [swap(sent.get(d, sends[d]), "col", d) for d in range(1, cols)]
    state_diag, mpo_rows = prepare(order, state_blocks, mpo_tensor, cols, states)
    core_send, state_diag, *lefts[1:] = lax.optimization_barrier((far[0], state_diag, *lefts[1:]))
    rights = [swap(core_send, "row", 1)] + [swap(far[d - 1], "row", d) for d in range(2, rows)]
    early = first_blocks(half, order, slots, keys, state_diag, mpo_rows, right_env, rights, lefts, near)
    came = [swap(early[d], "col", d) for d in range(1, cols)]
    late = last_blocks(order, slots, keys, state_diag, mpo_rows, right_env, rights, lefts, half, near)
    last = [swap(late[d], "col", d) for d in range(1, cols)]
    pieces = [(d, 0) for d in range(cols)] + [(0, half)]
    out = place_blocks(order, None, [early[0], *came, late[0]], pieces, cols)
    pieces = [(d, half) for d in range(1, cols)]
    return place_blocks(order, out, last, pieces, cols)


def solution(mesh):
    placed = (
        P(("groups", "row"), None, None),
        P(("groups", "row"), None, "col"),
        P(("groups", "row"), None, None),
        P(),
        P(("groups", "row")),
        P(("groups", "row"), None),
        P(("groups", "row")),
    )
    return jax.shard_map(
        shards,
        mesh=mesh,
        in_specs=placed,
        out_specs=P(("groups", "row"), None, "col"),
        check_vma=False,
    )
```

```python
import functools

import jax
import jax.numpy as jnp
from jax import lax
from jax.experimental import pallas as pl
from jax.experimental.pallas import tpu as pltpu
from jax.sharding import PartitionSpec as P

CHUNK = 16
SHIFT = 16
SMEM = pl.BlockSpec(memory_space=pltpu.SMEM)
VMEM = pl.BlockSpec(memory_space=pltpu.VMEM)
HBM = pl.BlockSpec(memory_space=pltpu.HBM)
ANY = pl.BlockSpec(memory_space=pl.ANY)


def swap(array, axis, step):
    size = lax.axis_size(axis)
    return lax.ppermute(array, axis, [(i, i ^ step) for i in range(size)])


def run_copies(copies):
    for copy in copies:
        copy.start()
    for copy in copies:
        copy.wait()


def owner_of(key):
    return lax.shift_right_logical(key, SHIFT)


def sub_of(key):
    return jnp.bitwise_and(key, (1 << SHIFT) - 1)


def route_kernel(cols, near, left_ref, key_ref, env_ref, *refs):
    sends = refs[:cols]
    order_ref, slot_ref, by_place = refs[cols:]
    count = left_ref.shape[0]
    steps = count // cols
    mine = lax.axis_index("col")
    owners = [owner_of(key_ref[p]) for p in range(count)]
    for p in range(count):
        place = jnp.int32(0)
        for other in range(count):
            if other < p:
                place = place + (owners[other] <= owners[p]).astype(jnp.int32)
            elif other > p:
                place = place + (owners[other] < owners[p]).astype(jnp.int32)
        by_place[place] = p
    for col in range(cols):
        before = None
        for step in range(steps):
            p = by_place[step * cols + col]
            owner = owner_of(key_ref[p])
            if before is None:
                slot = jnp.int32(0)
            else:
                slot = jnp.where(owner == before[0], before[1] + 1, 0)
            before = owner, slot
            order_ref[col * steps + step] = p
            slot_ref[col * steps + step] = owner * near + slot
    for other in range(cols):
        col = jnp.bitwise_xor(mine, other)
        for step in range(steps):
            p = order_ref[col * steps + step]
            sends[other][step] = env_ref[left_ref[p]]


def route(block_left, keys, left_env, cols, near):
    count = block_left.shape[0]
    size, width = left_env.shape[1:]
    piece = jax.ShapeDtypeStruct((count // cols, size, width), left_env.dtype)
    listed = jax.ShapeDtypeStruct((count,), jnp.int32)
    *sends, order, slots = pl.pallas_call(
        functools.partial(route_kernel, cols, near),
        out_shape=(piece,) * cols + (listed, listed),
        in_specs=[SMEM, SMEM, VMEM],
        out_specs=(VMEM,) * cols + (SMEM, SMEM),
        scratch_shapes=[pltpu.SMEM((count,), jnp.int32)],
        name="route",
    )(block_left, keys, left_env)
    return sends, order, slots


def pick_kernel(rows, cols, near, *refs):
    key_refs = refs[: rows - 1]
    env_ref = refs[rows - 1]
    sends = refs[rows:]
    count = key_refs[0].shape[0]
    me = lax.axis_index("row")
    mine = lax.axis_index("col")
    for other in range(rows - 1):
        keys = [key_refs[other][p] for p in range(count)]
        owners = [owner_of(key) for key in keys]
        first = jnp.int32(0)
        for p in range(count):
            first = first + (owners[p] < me).astype(jnp.int32)
        past = -lax.rem(mine - lax.rem(first, cols) + cols, cols)
        wanted = [jnp.int32(0)] * near
        for p in range(count):
            here = owners[p] == me
            for slot in range(near):
                wanted[slot] = jnp.where(here & (past == slot * cols), sub_of(keys[p]), wanted[slot])
            past = past + here.astype(jnp.int32)
        for slot in range(near):
            sends[other][slot] = env_ref[wanted[slot]]


def pick(keys, right_env, cols, near):
    rows = len(keys) + 1
    piece = jax.ShapeDtypeStruct((near,) + right_env.shape[1:], right_env.dtype)
    return pl.pallas_call(
        functools.partial(pick_kernel, rows, cols, near),
        out_shape=[piece] * (rows - 1),
        in_specs=[SMEM] * (rows - 1) + [VMEM],
        out_specs=(VMEM,) * (rows - 1),
        name="pick",
    )(*keys, right_env)


def halves(tile, low):
    swapped = pltpu.roll(tile, tile.shape[1] // 2, 1)
    zero = jnp.zeros_like(tile)
    return (
        jnp.where(low, tile, zero),
        jnp.where(low, zero, swapped),
        jnp.where(low, swapped, zero),
        jnp.where(low, zero, tile),
    )


def spread_state(block, state_diag, low):
    size = block.shape[0]
    for s in range(0, block.shape[1] // size, 2):
        pieces = halves(block[:, s * size : (s + 2) * size].astype(jnp.float32), low)
        for i in range(4):
            row, col = (i % 2) * size, (s + i // 2) * 2 * size
            state_diag[row : row + size, col : col + 2 * size] = pieces[i].astype(jnp.bfloat16)


def spread_right(right, right_diag, low):
    size = right.shape[0]
    for v in range(0, right.shape[1] // size, 2):
        pieces = halves(right[:, v * size : (v + 2) * size].astype(jnp.float32), low)
        for i in range(4):
            at = (2 * v + i) * size
            right_diag[at : at + size, :] = pieces[i].astype(jnp.bfloat16)


def spread_left(lefts, left_rows):
    cols = len(lefts)
    size = lefts[0].shape[0]
    half, share = size // 2, lefts[0].shape[1] // size
    mine = lax.axis_index("col")
    for other in range(cols):
        col = jnp.bitwise_xor(mine, other)
        for k in range(share):
            piece = lefts[other][:, k * size : (k + 1) * size].astype(jnp.float32)
            both = jnp.concatenate([piece[:half], piece[half:]], axis=1)
            left_rows[pl.ds(col * share + k, half, stride=cols * share), :] = both


def mix_block(states, left_rows, state_diag, mpo_ref, mixed):
    width = mpo_ref.shape[0] // states
    lanes = left_rows.shape[1]
    half = left_rows.shape[0] // width
    for start in range(0, half, CHUNK):
        taken = left_rows[start * width : (start + CHUNK) * width, :].astype(jnp.bfloat16)
        first = jnp.dot(taken, state_diag[...], preferred_element_type=jnp.float32)
        columns = []
        for x in range(CHUNK):
            one = first[x * width : (x + 1) * width, :]
            columns.append(
                jnp.concatenate(
                    [one[:, s * lanes : (s + 1) * lanes] for s in range(states)], axis=0
                ).astype(jnp.bfloat16)
            )
        gathered = jnp.concatenate(columns, axis=1)
        channels = jnp.dot(mpo_ref[...], gathered, preferred_element_type=jnp.float32).astype(jnp.bfloat16)
        for x in range(CHUNK):
            for v in range(width):
                mixed[(start + x) * states : (start + x + 1) * states, v * lanes : (v + 1) * lanes] = channels[
                    v * states : (v + 1) * states, x * lanes : (x + 1) * lanes
                ]


def finish_block(states, mixed, right_diag, result, outs, low):
    cols = len(outs)
    size = low.shape[0]
    half, per = size // 2, states // cols
    mine = lax.axis_index("col")
    result[...] = jnp.dot(mixed[...], right_diag[...], preferred_element_type=jnp.float32)
    low = low[:half]
    for other in range(cols):
        col = jnp.bitwise_xor(mine, other)
        for t in range(0, per, 2):
            one = result[pl.ds(col * per + t, half, stride=states), :]
            two = result[pl.ds(col * per + t + 1, half, stride=states), :]
            upper = jnp.where(low, one, pltpu.roll(two, size, 1))
            lower = jnp.where(low, pltpu.roll(one, size, 1), two)
            outs[other][:half, t * size : (t + 2) * size] = upper.astype(jnp.bfloat16)
            outs[other][half:, t * size : (t + 2) * size] = lower.astype(jnp.bfloat16)


def half_mask(size):
    return lax.broadcasted_iota(jnp.int32, (size, 2 * size), 1) < size


def prepare_kernel(states, order_ref, state_ref, mpo_ref, diag_ref, rows_ref, block, flat, sem):
    steps, size = block.shape[:2]
    width = mpo_ref.shape[0]
    low = half_mask(size)
    at = lax.axis_index("col") * steps
    copies = [
        pltpu.make_async_copy(state_ref.at[order_ref[at + k]], block.at[k], sem.at[k]) for k in range(steps)
    ]
    for copy in copies:
        copy.start()
    both = (states * states, states * states)
    row, col = lax.broadcasted_iota(jnp.int32, both, 0), lax.broadcasted_iota(jnp.int32, both, 1)
    turned = lax.rem(row, states) * states + lax.div(row, states)
    turn = jnp.where(turned == col, 1.0, 0.0).astype(jnp.bfloat16)
    split = flat.shape[0]
    for w in range(width):
        taken = mpo_ref[w].astype(jnp.float32)
        for i in range(split):
            flat[i, w * width : (w + 1) * width, :] = taken[:, i * 128 : (i + 1) * 128]
    taken = jnp.concatenate([flat[i] for i in range(split)], axis=1).astype(jnp.bfloat16)
    taken = jnp.dot(taken, turn, preferred_element_type=jnp.float32)
    for i in range(split):
        flat[i] = taken[:, i * 128 : (i + 1) * 128]

    def some_channels(j, carry):
        for v in range(4):
            taken = [jnp.transpose(flat[i, pl.ds(4 * j + v, width, stride=width), :]) for i in range(split)]
            taken = jnp.concatenate(taken, axis=0)
            line = jnp.concatenate([taken[s * states : (s + 1) * states, :] for s in range(states)], axis=1)
            rows_ref[pl.ds(pl.multiple_of((4 * j + v) * states, states), states), :] = line.astype(jnp.bfloat16)
        return carry

    lax.fori_loop(0, width // 4, some_channels, 0)
    for copy in copies:
        copy.wait()

    def one_block(k, carry):
        spread_state(block.at[k], diag_ref.at[k], low)
        return carry

    lax.fori_loop(0, steps, one_block, 0)


def prepare(order, state_blocks, mpo_tensor, cols, states):
    count, size = state_blocks.shape[:2]
    steps, width = count // cols, mpo_tensor.shape[0]
    return pl.pallas_call(
        functools.partial(prepare_kernel, states),
        out_shape=[
            jax.ShapeDtypeStruct((steps, 2 * size, 2 * states * size), jnp.bfloat16),
            jax.ShapeDtypeStruct((width * states, states * width), jnp.bfloat16),
        ],
        in_specs=[SMEM, ANY, VMEM],
        out_specs=[VMEM, VMEM],
        scratch_shapes=[
            pltpu.VMEM((steps, size, states * size), jnp.bfloat16),
            pltpu.VMEM((states * states // 128, width * width, 128), jnp.float32),
            pltpu.SemaphoreType.DMA((steps,)),
        ],
        compiler_params=pltpu.CompilerParams(vmem_limit_bytes=10 << 20),
        cost_estimate=pl.CostEstimate(flops=0, bytes_accessed=0, transcendentals=0),
        name="prepare",
    )(order, state_blocks, mpo_tensor)


def mix_kernel(states, cols, count, diag_ref, mpo_ref, *refs):
    lefts, mixed, left_rows = refs[:cols], refs[cols : cols + count], refs[-1]
    for k in range(count):
        spread_left([left.at[k] for left in lefts], left_rows.at[k])
    for k in range(count):
        mix_block(states, left_rows.at[k], diag_ref.at[k], mpo_ref, mixed[k])


def fetch_right(near, key_ref, order_ref, slot_ref, at, env_ref, rights, right_now):
    slot = lax.rem(slot_ref[at], near)
    apart = jnp.bitwise_xor(lax.div(slot_ref[at], near), lax.axis_index("row"))

    @pl.when(apart == 0)
    def _():
        right_now[...] = env_ref[sub_of(key_ref[order_ref[at]])]

    for other, right in enumerate(rights, 1):

        @pl.when(apart == other)
        def _():
            right_now[...] = right[slot]


def right_kernel(states, rows, cols, near, count, order_ref, slot_ref, key_ref, env_ref, *refs):
    rights, refs = refs[: rows - 1], refs[rows - 1 :]
    mixed, outs, (right_now, right_diag, result) = refs[:count], refs[count : count + cols], refs[count + cols :]
    low = half_mask(env_ref.shape[1])
    at = lax.axis_index("col") * (order_ref.shape[0] // cols)
    for k in range(count):
        fetch_right(near, key_ref, order_ref, slot_ref, at + k, env_ref, rights, right_now.at[k])
    for k in range(count):
        spread_right(right_now.at[k], right_diag.at[k], low)
    for k in range(count):
        finish_block(states, mixed[k], right_diag.at[k], result.at[k], [out.at[k] for out in outs], low)


def apply_kernel(
    states, rows, cols, near, first, count, order_ref, slot_ref, key_ref, env_ref, diag_ref, mpo_ref, early_ref, *refs
):
    rights, lefts, refs = refs[: rows - 1], refs[rows - 1 : rows - 1 + cols], refs[rows - 1 + cols :]
    outs, (left_rows, mixed, right_now, right_diag, result) = refs[:cols], refs[cols:]
    low = half_mask(env_ref.shape[1])
    at = lax.axis_index("col") * (order_ref.shape[0] // cols) + first
    for k in range(count):
        spread_left([left.at[first + k] for left in lefts], left_rows.at[k])
    for k in range(count):
        mix_block(states, left_rows.at[k], diag_ref.at[first + k], mpo_ref, mixed.at[k])
    outs[1][:first] = early_ref[...]
    for k in range(count):
        fetch_right(near, key_ref, order_ref, slot_ref, at + k, env_ref, rights, right_now.at[k])
    for k in range(count):
        spread_right(right_now.at[k], right_diag.at[k], low)
    for k in range(count):
        into = [out.at[first + k if d == 1 else k] for d, out in enumerate(outs)]
        finish_block(states, mixed.at[k], right_diag.at[k], result.at[k], into, low)


def cost_of(blocks, states, width, size, mix, right):
    flops = mix * (width * size * size * states * size + (width * states) ** 2 * size * size)
    flops = 2 * blocks * (flops + right * states * size * size * width * size)
    return pl.CostEstimate(flops=flops, bytes_accessed=4 << 20, transcendentals=0)


def first_blocks(count, order, slots, keys, state_diag, mpo_rows, right_env, rights, lefts, near):
    cols, rows = len(lefts), len(rights) + 1
    size, share = lefts[0].shape[1:]
    width = share // size * cols
    states = mpo_rows.shape[0] // width
    half, lanes = size // 2, 2 * size
    params = pltpu.CompilerParams(vmem_limit_bytes=32 << 20)
    mixed = pl.pallas_call(
        functools.partial(mix_kernel, states, cols, count),
        out_shape=[jax.ShapeDtypeStruct((half * states, width * lanes), jnp.bfloat16)] * count,
        in_specs=[VMEM] * (2 + cols),
        out_specs=[VMEM] * count,
        scratch_shapes=[pltpu.VMEM((count, half * width, lanes), jnp.float32)],
        compiler_params=params,
        cost_estimate=cost_of(count, states, width, size, 1, 0),
        name="mix",
    )(state_diag, mpo_rows, *lefts)
    return pl.pallas_call(
        functools.partial(right_kernel, states, rows, cols, near, count),
        out_shape=[jax.ShapeDtypeStruct((count, size, states // cols * size), jnp.bfloat16)] * cols,
        in_specs=[SMEM] * 3 + [VMEM] * (rows + count),
        out_specs=[VMEM] * cols,
        scratch_shapes=[
            pltpu.VMEM((count, size, width * size), jnp.bfloat16),
            pltpu.VMEM((count, width * lanes, lanes), jnp.bfloat16),
            pltpu.VMEM((count, half * states, lanes), jnp.float32),
        ],
        compiler_params=params,
        cost_estimate=cost_of(count, states, width, size, 0, 1),
        name="right",
    )(order, slots, keys, right_env, *rights, *mixed)


def last_blocks(order, slots, keys, state_diag, mpo_rows, right_env, rights, lefts, early, near):
    cols, rows = len(lefts), len(rights) + 1
    first, (steps, size, share) = early.shape[0], lefts[0].shape
    count = steps - first
    width = share // size * cols
    states = mpo_rows.shape[0] // width
    half, lanes = size // 2, 2 * size

    def out(blocks):
        return jax.ShapeDtypeStruct((blocks, size, states // cols * size), jnp.bfloat16)

    return pl.pallas_call(
        functools.partial(apply_kernel, states, rows, cols, near, first, count),
        out_shape=[out(steps if d == 1 else count) for d in range(cols)],
        in_specs=[SMEM] * 3 + [VMEM] * (4 + rows - 1 + cols),
        out_specs=[VMEM] * cols,
        scratch_shapes=[
            pltpu.VMEM((count, half * width, lanes), jnp.float32),
            pltpu.VMEM((count, half * states, width * lanes), jnp.bfloat16),
            pltpu.VMEM((count, size, width * size), jnp.bfloat16),
            pltpu.VMEM((count, width * lanes, lanes), jnp.bfloat16),
            pltpu.VMEM((count, half * states, lanes), jnp.float32),
        ],
        compiler_params=pltpu.CompilerParams(vmem_limit_bytes=32 << 20),
        cost_estimate=cost_of(count, states, width, size, 1, 1),
        name="apply",
    )(order, slots, keys, right_env, state_diag, mpo_rows, early, *rights, *lefts)


def place_kernel(cols, pieces, begun, order_ref, *refs):
    came = refs[begun : begun + len(pieces)]
    out_ref, sem = refs[begun + len(pieces) :]
    steps = order_ref.shape[0] // cols
    mine = lax.axis_index("col")
    copies = []
    for piece, (other, first) in zip(came, pieces):
        col = jnp.bitwise_xor(mine, other)
        for k in range(piece.shape[0]):
            p = order_ref[col * steps + first + k]
            copies.append(pltpu.make_async_copy(piece.at[k], out_ref.at[p], sem.at[len(copies)]))
    run_copies(copies)


def place_blocks(order, out, came, pieces, cols):
    begun = [] if out is None else [out]
    return pl.pallas_call(
        functools.partial(place_kernel, cols, pieces, len(begun)),
        out_shape=jax.ShapeDtypeStruct((order.shape[0],) + came[0].shape[1:], came[0].dtype),
        in_specs=[SMEM] + [HBM] * len(begun) + [VMEM] * len(came),
        out_specs=HBM,
        scratch_shapes=[pltpu.SemaphoreType.DMA((sum(piece.shape[0] for piece in came),))],
        input_output_aliases={1: 0} if begun else {},
        compiler_params=pltpu.CompilerParams(vmem_limit_bytes=4 << 20),
        cost_estimate=pl.CostEstimate(flops=10**10, bytes_accessed=1 << 20, transcendentals=0),
        name="place",
    )(order, *begun, *came)


def shards(state_blocks, left_env, right_env, mpo_tensor, block_left, block_owner, block_sub):
    rows = lax.axis_size("row")
    cols = lax.axis_size("col")
    count, size = state_blocks.shape[:2]
    states = state_blocks.shape[2] // size
    width = mpo_tensor.shape[0]
    most = max(2, (2 * count + rows - 1) // rows)
    near = -(-most // cols)

    half = count // cols // 2

    keys = jnp.bitwise_or(lax.shift_left(block_owner[:, 0], SHIFT), block_sub)
    others = [swap(keys, "row", step) for step in range(1, rows)]
    sends, order, slots = route(block_left, keys, left_env, cols, near)
    picked = pick(others, right_env, cols, near)
    rest = list(range(3, cols))
    mpo_tensor, *held = lax.optimization_barrier((mpo_tensor, *picked, *[sends[d] for d in rest]))
    far, sent = held[: rows - 1], dict(zip(rest, held[rows - 1 :]))
    lefts = [sends[0]] + [swap(sent.get(d, sends[d]), "col", d) for d in range(1, cols)]
    state_diag, mpo_rows = prepare(order, state_blocks, mpo_tensor, cols, states)
    core_send, state_diag, *lefts[1:] = lax.optimization_barrier((far[0], state_diag, *lefts[1:]))
    rights = [swap(core_send, "row", 1)] + [swap(far[d - 1], "row", d) for d in range(2, rows)]
    early = first_blocks(half, order, slots, keys, state_diag, mpo_rows, right_env, rights, lefts, near)
    came = [swap(early[d], "col", d) for d in range(2, cols)]
    late = last_blocks(order, slots, keys, state_diag, mpo_rows, right_env, rights, lefts, early[1], near)
    last = [swap(late[d], "col", d) for d in range(1, cols)]
    pieces = [(0, 0)] + [(d, 0) for d in range(2, cols)] + [(0, half)]
    out = place_blocks(order, None, [early[0], *came, late[0]], pieces, cols)
    pieces = [(1, 0)] + [(d, half) for d in range(2, cols)]
    return place_blocks(order, out, last, pieces, cols)


def solution(mesh):
    placed = (
        P(("groups", "row"), None, None),
        P(("groups", "row"), None, "col"),
        P(("groups", "row"), None, None),
        P(),
        P(("groups", "row")),
        P(("groups", "row"), None),
        P(("groups", "row")),
    )
    return jax.shard_map(
        shards,
        mesh=mesh,
        in_specs=placed,
        out_specs=P(("groups", "row"), None, "col"),
        check_vma=False,
    )
```
